32 devices in a mesh: dp: 8 (over z, x), tensor: 4 (over y, core).
Axes of the slice: x: 2, y: 2, z: 4, core: 2. Of those that a mesh axis runs over, the one named last changes fastest.
Arguments:
- tokens: bfloat16 [32768, 768], P(('dp', 'tensor')), may hold values from -6 to 6
- out_grad: bfloat16 [32768, 768], P(('dp', 'tensor')), may hold values from -6 to 6
- slot_kind: int32 [256, 128], P(('dp', 'tensor')), may hold values from 0 to 1, as said below
- slot_valid: int32 [256, 128], P(('dp', 'tensor')), may hold values from 0 to 1, as said below
- qkv_weight: float32 [2, 768, 2304], P(None, 'dp', 'tensor'), may hold values from -0.21875 to 0.21875
- qkv_first: float32 [2, 768, 2304], P(None, 'dp', 'tensor'), may hold values from -0.0002 to 0.0002
- qkv_second: float32 [2, 768, 2304], P(None, 'dp', 'tensor'), may hold values from 1e-10 to 1e-08
- out_weight: float32 [2, 768, 768], P(None, 'dp', 'tensor'), may hold values from -0.875 to 0.875
- out_first: float32 [2, 768, 768], P(None, 'dp', 'tensor'), may hold values from -0.0002 to 0.0002
- out_second: float32 [2, 768, 768], P(None, 'dp', 'tensor'), may hold values from 1e-10 to 1e-08
- up_weight: float32 [2, 768, 3072], P(None, 'dp', 'tensor'), may hold values from -0.21875 to 0.21875
- up_first: float32 [2, 768, 3072], P(None, 'dp', 'tensor'), may hold values from -0.0002 to 0.0002
- up_second: float32 [2, 768, 3072], P(None, 'dp', 'tensor'), may hold values from 1e-10 to 1e-08
- down_weight: float32 [2, 3072, 768], P(None, 'tensor', 'dp'), may hold values from -0.109375 to 0.109375
- down_first: float32 [2, 3072, 768], P(None, 'tensor', 'dp'), may hold values from -0.0002 to 0.0002
- down_second: float32 [2, 3072, 768], P(None, 'tensor', 'dp'), may hold values from 1e-10 to 1e-08
- gain_weight: float32 [2, 2, 768], P(None, None, 'tensor'), may hold values from 0.5 to 1.5
- gain_first: float32 [2, 2, 768], P(None, None, 'tensor'), may hold values from -0.0002 to 0.0002
- gain_second: float32 [2, 2, 768], P(None, None, 'tensor'), may hold values from 1e-10 to 1e-08
- bias_weight: float32 [2, 6, 768], P(None, None, 'tensor'), may hold values from -3 to 3
- bias_first: float32 [2, 6, 768], P(None, None, 'tensor'), may hold values from -0.0002 to 0.0002
- bias_second: float32 [2, 6, 768], P(None, None, 'tensor'), may hold values from 1e-10 to 1e-08
- hidden_weight: float32 [2, 3072], P(None, 'tensor'), may hold values from -3 to 3
- hidden_first: float32 [2, 3072], P(None, 'tensor'), may hold values from -0.0002 to 0.0002
- hidden_second: float32 [2, 3072], P(None, 'tensor'), may hold values from 3e-12 to 3e-10
Outputs:
- block_output: float32 [32768, 768], P(('dp', 'tensor'))
- input_grad: float32 [32768, 768], P(('dp', 'tensor'))
- grad_norm: float32 [], replicated
- qkv_grad: float32 [2, 768, 2304], P(None, 'dp', 'tensor')
- qkv_update: float32 [2, 768, 2304], P(None, 'dp', 'tensor')
- qkv_first_new: float32 [2, 768, 2304], P(None, 'dp', 'tensor')
- qkv_second_new: float32 [2, 768, 2304], P(None, 'dp', 'tensor')
- out_grad_weight: float32 [2, 768, 768], P(None, 'dp', 'tensor')
- out_update: float32 [2, 768, 768], P(None, 'dp', 'tensor')
- out_first_new: float32 [2, 768, 768], P(None, 'dp', 'tensor')
- out_second_new: float32 [2, 768, 768], P(None, 'dp', 'tensor')
- up_grad: float32 [2, 768, 3072], P(None, 'dp', 'tensor')
- up_update: float32 [2, 768, 3072], P(None, 'dp', 'tensor')
- up_first_new: float32 [2, 768, 3072], P(None, 'dp', 'tensor')
- up_second_new: float32 [2, 768, 3072], P(None, 'dp', 'tensor')
- down_grad: float32 [2, 3072, 768], P(None, 'tensor', 'dp')
- down_update: float32 [2, 3072, 768], P(None, 'tensor', 'dp')
- down_first_new: float32 [2, 3072, 768], P(None, 'tensor', 'dp')
- down_second_new: float32 [2, 3072, 768], P(None, 'tensor', 'dp')
- gain_grad: float32 [2, 2, 768], P(None, None, 'tensor')
- gain_update: float32 [2, 2, 768], P(None, None, 'tensor')
- gain_first_new: float32 [2, 2, 768], P(None, None, 'tensor')
- gain_second_new: float32 [2, 2, 768], P(None, None, 'tensor')
- bias_grad: float32 [2, 6, 768], P(None, None, 'tensor')
- bias_update: float32 [2, 6, 768], P(None, None, 'tensor')
- bias_first_new: float32 [2, 6, 768], P(None, None, 'tensor')
- bias_second_new: float32 [2, 6, 768], P(None, None, 'tensor')
- hidden_grad: float32 [2, 3072], P(None, 'tensor')
- hidden_update: float32 [2, 3072], P(None, 'tensor')
- hidden_first_new: float32 [2, 3072], P(None, 'tensor')
- hidden_second_new: float32 [2, 3072], P(None, 'tensor')
The draws below stay inside these ranges and needn't reach their ends.
Inputs may be any that keep to these rules, and one draw needn't show every extreme that they name: `slot_kind`: every page has exactly 96 slots of kind 0 and 32 of kind 1, in any order. `slot_valid`: every text slot is valid; every page has 1 to 32 valid visual slots; some page has all 32 valid and some page exactly one.
All inputs are finite; a program needn't handle non-finite values.
Results may differ from the reference program's by a relative error of at most 0.01225.
Values may be sent and summed in bfloat16 or wider, within the bound.
No kernel may reach another device: no remote copies, remote signals or barrier semaphores. Data moves between devices by JAX's collectives and lax.ppermute only.
A program may use at most 320 MiB of HBM per device.

```python
import math
import jax
import jax.numpy as jnp
from jax import lax

D = 768
HEADS = 12
HEAD_DIM = 64
FF = 3072
TEXT_SLOTS = 96
VIS_SLOTS = 32
SLOTS = 128
PAGES = 256
TOKENS = 32768


def page_layout(key):
    base = jax.random.fold_in(key, 17)
    key_order, key_count, key_top, key_low = jax.random.split(base, 4)
    page_keys = jax.random.split(key_order, PAGES)
    orders = jax.vmap(lambda single: jax.random.permutation(single, SLOTS))(page_keys).astype(jnp.int32)
    counts = jax.random.randint(key_count, (PAGES,), 1, VIS_SLOTS // 2 + 1).astype(jnp.int32)
    top_page = jax.random.randint(key_top, (), 0, PAGES).astype(jnp.int32)
    low_page = ((top_page + 1 + jax.random.randint(key_low, (), 0, PAGES - 1)) % PAGES).astype(jnp.int32)
    page_ids = jnp.arange(PAGES, dtype=jnp.int32)
    counts = jnp.where(page_ids == top_page, VIS_SLOTS, jnp.where(page_ids == low_page, 1, counts))
    return (orders, counts)


def draw_slot_kind(key, part):
    orders, counts = page_layout(key)
    return (orders >= TEXT_SLOTS).astype(jnp.int32)


def draw_slot_valid(key, part):
    orders, counts = page_layout(key)
    return (orders < TEXT_SLOTS + counts[:, None]).astype(jnp.int32)


def level_of(key, shape, cuts, low, largest):
    factor_of = 1.0
    for axis_at, parts in cuts:
        heights = jax.random.uniform(jax.random.fold_in(jax.random.fold_in(key, 6), axis_at), (parts,), jnp.float32, low / len(cuts), largest / len(cuts))
        factor_of = factor_of * jnp.repeat(jnp.exp(heights), shape[axis_at] // parts).reshape((-1,) + (1,) * (len(shape) - 1 - axis_at))
    return factor_of


def bell_draw(own_key, shape, width, most, pieces=(), kind=jnp.bfloat16):
    drawn = jax.random.normal(own_key, shape, jnp.float32) * width
    if len(pieces) > 0:
        drawn = level_of(own_key, shape, pieces, -0.22, 0.18) * drawn
    return jnp.clip(drawn, min=-most, max=most).astype(kind)


def setup_inputs(seed: int = 0) -> dict:
    keys = jax.random.split(jax.random.key(seed), 26)
    return {
        "tokens": bell_draw(keys[0], (TOKENS, D), 1.0, 6.0, ((0, 32),)),
        "out_grad": bell_draw(keys[1], (TOKENS, D), 1.0, 6.0, ((0, 32),)),
        "slot_kind": draw_slot_kind(jax.random.fold_in(keys[25], 71), 0),
        "slot_valid": draw_slot_valid(jax.random.fold_in(keys[25], 71), 0),
        "qkv_weight": bell_draw(keys[4], (2, D, 3 * D), D ** -0.5, 0.21875, ((1, 8), (2, 4)), jnp.float32),
        "qkv_first": bell_draw(keys[5], (2, D, 3 * D), 0.00003, 0.0002, ((1, 8), (2, 4)), jnp.float32),
        "qkv_second": jnp.clip(jnp.exp(math.log(9.99999993922529e-09) - 4.6051702 * jax.random.uniform(keys[6], (2, D, 3 * D), jnp.float32) ** level_of(keys[6], (2, D, 3 * D), ((1, 8), (2, 4)), -0.2, 0.2)), 1.000000013351432e-10, 9.99999993922529e-09),
        "out_weight": bell_draw(keys[7], (2, D, D), (D // 16) ** -0.5, 0.875, ((1, 8), (2, 4)), jnp.float32),
        "out_first": bell_draw(keys[8], (2, D, D), 0.00003, 0.0002, ((1, 8), (2, 4)), jnp.float32),
        "out_second": jnp.clip(jnp.exp(math.log(9.99999993922529e-09) - 4.6051702 * jax.random.uniform(keys[9], (2, D, D), jnp.float32) ** level_of(keys[9], (2, D, D), ((1, 8), (2, 4)), -0.2, 0.2)), 1.000000013351432e-10, 9.99999993922529e-09),
        "up_weight": bell_draw(keys[10], (2, D, FF), D ** -0.5, 0.21875, ((1, 8), (2, 4)), jnp.float32),
        "up_first": bell_draw(keys[11], (2, D, FF), 0.00003, 0.0002, ((1, 8), (2, 4)), jnp.float32),
        "up_second": jnp.clip(jnp.exp(math.log(9.99999993922529e-09) - 4.6051702 * jax.random.uniform(keys[12], (2, D, FF), jnp.float32) ** level_of(keys[12], (2, D, FF), ((1, 8), (2, 4)), -0.2, 0.2)), 1.000000013351432e-10, 9.99999993922529e-09),
        "down_weight": bell_draw(keys[13], (2, FF, D), FF ** -0.5, 0.109375, ((1, 4), (2, 8)), jnp.float32),
        "down_first": bell_draw(keys[14], (2, FF, D), 0.00003, 0.0002, ((1, 4), (2, 8)), jnp.float32),
        "down_second": jnp.clip(jnp.exp(math.log(9.99999993922529e-09) - 4.6051702 * jax.random.uniform(keys[15], (2, FF, D), jnp.float32) ** level_of(keys[15], (2, FF, D), ((1, 4), (2, 8)), -0.2, 0.2)), 1.000000013351432e-10, 9.99999993922529e-09),
        "gain_weight": jnp.clip(1.0 + 0.1 * jax.random.normal(keys[16], (2, 2, D), jnp.float32), 0.5, 1.5),
        "gain_first": bell_draw(keys[17], (2, 2, D), 0.00003, 0.0002, ((2, 4),), jnp.float32),
        "gain_second": jnp.clip(jnp.exp(math.log(9.99999993922529e-09) - 4.6051702 * jax.random.uniform(keys[18], (2, 2, D), jnp.float32) ** level_of(keys[18], (2, 2, D), ((2, 4),), -0.2, 0.2)), 1.000000013351432e-10, 9.99999993922529e-09),
        "bias_weight": bell_draw(keys[19], (2, 6, D), 0.5, 3.0, ((2, 4),), jnp.float32),
        "bias_first": bell_draw(keys[20], (2, 6, D), 0.00003, 0.0002, ((2, 4),), jnp.float32),
        "bias_second": jnp.clip(jnp.exp(math.log(9.99999993922529e-09) - 4.6051702 * jax.random.uniform(keys[21], (2, 6, D), jnp.float32) ** level_of(keys[21], (2, 6, D), ((2, 4),), -0.2, 0.2)), 1.000000013351432e-10, 9.99999993922529e-09),
        "hidden_weight": bell_draw(keys[22], (2, FF), 0.5, 3.0, ((1, 4),), jnp.float32),
        "hidden_first": bell_draw(keys[23], (2, FF), 0.00003, 0.0002, ((1, 4),), jnp.float32),
        "hidden_second": jnp.clip(jnp.exp(math.log(2.999999970665357e-10) - 4.6051702 * jax.random.uniform(keys[24], (2, FF), jnp.float32) ** level_of(keys[24], (2, FF), ((1, 4),), -0.2, 0.2)), 2.9999999880125916e-12, 2.999999970665357e-10),
    }


@jax.custom_vjp
def low(v):
    return lax.optimization_barrier(v.astype(jnp.bfloat16)).astype(jnp.float32)

@jax.custom_vjp
def low_back(v):
    return v

def low_keep(v):
    return (low(v), None)

def low_pass(kept, grad):
    return (grad,)

def back_keep(v):
    return (v, None)

def back_low(kept, grad):
    return (low(grad),)
low.defvjp(low_keep, low_pass)
low_back.defvjp(back_keep, back_low)
highest = lax.Precision.HIGHEST
beta_one = 0.9
beta_two = 0.99
learn_rate = 0.01
weight_decay = 0.01
epsilon = 1e-08
clip_norm = 1.0
bias_one = 1.0 - beta_one ** 10
bias_two = 1.0 - beta_two ** 10

def norm_rows(stream, gains_row, shift_row):
    average = lax.optimization_barrier(jnp.mean(stream, axis=-1, keepdims=True))
    centered = stream - average
    spread = lax.optimization_barrier(jnp.mean(centered * centered, axis=-1, keepdims=True))
    return centered * lax.rsqrt(spread + 1e-05) * gains_row + shift_row

def attend_block(queries, keys_in, values, kinds, valid, across):
    scale = HEAD_DIM ** (-0.5)
    scores = jnp.einsum('gihd,gjhd->ghij', queries, keys_in, precision=highest) * scale
    scores = low_back(scores)
    same_kind = kinds[:, :, None] == kinds[:, None, :]
    partner = jnp.logical_not(same_kind) if across else same_kind
    allowed = jnp.logical_and(partner, valid[:, None, :] > 0)[:, None]
    masked = jnp.where(allowed, scores, -1e+30)
    soft_weights = low(jax.nn.softmax(masked, axis=-1))
    return jnp.einsum('ghij,gjhd->gihd', soft_weights, values, precision=highest)

def attend(queries, keys_in, values, kinds, valid, across):
    groups = PAGES // 32

    def shaped(tensor):
        return tensor.reshape((groups, 32) + tensor.shape[1:])

    def one_group(packed):
        return attend_block(packed[0], packed[1], packed[2], packed[3], packed[4], across)
    four = (PAGES, SLOTS, HEADS, HEAD_DIM)
    result = lax.map(jax.checkpoint(one_group), (shaped(queries.reshape(four)), shaped(keys_in.reshape(four)), shaped(values.reshape(four)), shaped(kinds), shaped(valid)))
    return result.reshape(PAGES * SLOTS, D)

def layer(stream, kinds, valid, qkv_w, out_w, gains_v, biases_v, up_w, down_w, up_b, across):
    normed = low(norm_rows(stream, gains_v[0], biases_v[0]))
    projected = jnp.dot(normed, qkv_w, precision=highest)
    queries = low(low_back(projected[:, :D] + biases_v[1]))
    keys_in = low(low_back(projected[:, D:2 * D]))
    values = low(low_back(projected[:, 2 * D:] + biases_v[2]))
    mixed = low(low_back(attend(queries, keys_in, values, kinds, valid, across)))
    branch = jnp.dot(mixed, out_w, precision=highest) + biases_v[3]
    middle = stream + low_back(branch)
    normed_ffn = low(norm_rows(middle, gains_v[1], biases_v[4]))
    upper = low_back(jnp.dot(normed_ffn, up_w, precision=highest) + up_b)
    active = low(jax.nn.gelu(upper))
    lower = jnp.dot(active, down_w, precision=highest) + biases_v[5]
    return middle + low_back(lower)

def forward(stream, kinds, valid, qkv_m, out_m, up_m, down_m, gain_m, bias_m, hidden_m):
    qkv_w = low(qkv_m)
    out_w = low(out_m)
    up_w = low(up_m)
    down_w = low(down_m)
    gains_v = low(gain_m)
    biases_v = low(bias_m)
    hidden_b = low(hidden_m)
    for index in range(2):
        stream = layer(stream, kinds, valid, qkv_w[index], out_w[index], gains_v[index], biases_v[index], up_w[index], down_w[index], hidden_b[index], index == 0)
    return stream

def adam_step(master, grad, moment_one, moment_two, factor, decayed):
    clipped = grad * factor
    first_new = beta_one * moment_one + (1.0 - beta_one) * clipped
    second_new = beta_two * moment_two + (1.0 - beta_two) * clipped * clipped
    change = first_new / bias_one / (jnp.sqrt(second_new / bias_two) + epsilon)
    if decayed:
        change = change + weight_decay * master
    return (-learn_rate * change, first_new, second_new)

def reference(tokens, out_grad, slot_kind, slot_valid, qkv_weight, qkv_first, qkv_second, out_weight, out_first, out_second, up_weight, up_first, up_second, down_weight, down_first, down_second, gain_weight, gain_first, gain_second, bias_weight, bias_first, bias_second, hidden_weight, hidden_first, hidden_second):
    stream = tokens.astype(jnp.float32)
    cotangent = out_grad.astype(jnp.float32)

    def model_fn(stream_in, qkv_m, out_m, up_m, down_m, gain_m, bias_m, hidden_m):
        return forward(stream_in, slot_kind, slot_valid, qkv_m, out_m, up_m, down_m, gain_m, bias_m, hidden_m)
    output, pullback = jax.vjp(model_fn, stream, qkv_weight, out_weight, up_weight, down_weight, gain_weight, bias_weight, hidden_weight)
    grads = pullback(cotangent)
    input_grad = grads[0]
    param_grads = grads[1:]
    total = jnp.float32(0.0)
    for grad in param_grads:
        total = total + jnp.sum(grad * grad)
    grad_norm = jnp.sqrt(total)
    factor = clip_norm / jnp.maximum(grad_norm, clip_norm)
    masters = (qkv_weight, out_weight, up_weight, down_weight, gain_weight, bias_weight, hidden_weight)
    firsts = (qkv_first, out_first, up_first, down_first, gain_first, bias_first, hidden_first)
    seconds = (qkv_second, out_second, up_second, down_second, gain_second, bias_second, hidden_second)
    results = [output, input_grad, grad_norm]
    for index in range(7):
        update, first_new, second_new = adam_step(masters[index], param_grads[index], firsts[index], seconds[index], factor, index < 4)
        results = results + [param_grads[index], update, first_new, second_new]
    return tuple(results)
```

```python
import functools

import jax
import jax.numpy as jnp
from jax import lax
from jax.experimental import pallas as pl
from jax.experimental.pallas import tpu as pltpu
from jax.sharding import PartitionSpec as P

HEADS = 12
PAIRS = HEADS // 2

beta_one = 0.9
beta_two = 0.99
learn_rate = 0.01
weight_decay = 0.01
epsilon = 1e-08
clip_norm = 1.0
bias_one = 1.0 - beta_one**10
bias_two = 1.0 - beta_two**10

BF = jnp.bfloat16
F32 = jnp.float32
VMEM_LIMIT = 56 * 1024 * 1024


def dot_nn(a, b):
    return lax.dot_general(a, b, (((1,), (0,)), ((), ())), preferred_element_type=F32)


def dot_nt(a, b):
    return lax.dot_general(a, b, (((1,), (1,)), ((), ())), preferred_element_type=F32)


def dot_tn(a, b):
    return lax.dot_general(a, b, (((0,), (0,)), ((), ())), preferred_element_type=F32)


def normalize(stream):
    average = jnp.mean(stream, axis=-1, keepdims=True)
    centered = stream - average
    spread = jnp.mean(centered * centered, axis=-1, keepdims=True)
    root = lax.rsqrt(spread + 1e-05)
    return centered * root, root


def norm_backward(grad, unit, root, gain):
    scaled = grad * gain
    first = jnp.mean(scaled, axis=-1, keepdims=True)
    second = jnp.mean(scaled * unit, axis=-1, keepdims=True)
    return root * (scaled - first - unit * second)


def column_sum(value):
    return jnp.sum(value, axis=0, keepdims=True)


def split_heads(pair):
    lane = lax.broadcasted_iota(jnp.int32, pair.shape, 1)
    zero = jnp.zeros_like(pair)
    half = pair.shape[1] // 2
    return jnp.concatenate([jnp.where(lane < half, pair, zero), jnp.where(lane >= half, pair, zero)], axis=0)


def weight_copies(plan, refs, me_ref, full, sems):
    copies = []

    def add(source, target):
        copies.append(pltpu.make_async_copy(source, target, sems.at[len(copies)]))

    if plan[0] == "whole":
        add(refs[0], full)
    elif plan[0] == "rows":
        parts, width, _ = full.shape
        high = width * parts // refs[0].shape[0]
        for index in range(refs[0].shape[0]):
            stripe, part = divmod(index, parts)
            add(refs[0].at[index, pl.ds(plan[1], high), :], full.at[part, pl.ds(stripe * high, high), :])
    else:
        for ref, (row, positions) in zip(refs, plan[1]):
            _, depth, high, width = ref.shape
            for place, (x, y, core) in enumerate(positions):
                part = jnp.bitwise_xor(me_ref[1], 2 * y + core)
                for z in range(depth):
                    stripe = jnp.bitwise_xor(me_ref[0], 2 * z + x)
                    start = pl.multiple_of(stripe * (width // (2 * depth)) + row, 16)
                    add(ref.at[place, z], full.at[part, pl.ds(start, high), :])
    return copies


def load_weights(groups):
    copies = [copy for group in groups for copy in weight_copies(*group)]
    for copy in copies:
        copy.start()
    for copy in copies:
        copy.wait()


def copy_count(plan, refs):
    if plan[0] == "whole":
        return 1
    if plan[0] == "rows":
        return refs[0].shape[0]
    return sum(ref.shape[0] * ref.shape[1] for ref in refs)


def split_attention(raw, qkv_s, out_s):
    parts = raw.shape[0]
    cut = qkv_s.shape[1] // parts
    step = 96

    def relay(index, _):
        rows = pl.ds(pl.multiple_of(index * step, step), step)
        pieces = [raw[part, rows, :] for part in range(parts)]
        qkv_s[rows, :] = jnp.concatenate([piece[:, :cut] for piece in pieces], axis=1)
        out_s[rows, :] = jnp.concatenate([piece[:, cut:] for piece in pieces], axis=1)
        return 0

    lax.fori_loop(0, raw.shape[1] // step, relay, 0)


def attention_forward_kernel(plan, me_ref, stream_ref, mask_ref, vec_ref, *refs):
    weight_refs = refs[:-10]
    middle_ref, nffn_ref, normed_ref, proj_ref, probs_ref, mixed_ref, qkv_s, out_s, raw, sems = refs[-10:]

    @pl.when(pl.program_id(0) == 0)
    def _():
        load_weights([(plan, weight_refs, me_ref, raw, sems)])
        split_attention(raw, qkv_s, out_s)

    width = stream_ref.shape[1]
    slots = mask_ref.shape[1]
    scale = (width // HEADS) ** (-0.5)
    stream = stream_ref[...].astype(F32)
    unit, _ = normalize(stream)
    normed = (unit * vec_ref[0:1, :] + vec_ref[2:3, :]).astype(BF)
    normed_ref[...] = normed
    projected = dot_nn(normed, qkv_s[...])
    proj_ref[:, :width] = (projected[:, :width] + vec_ref[3:4, :]).astype(BF)
    proj_ref[:, width : 2 * width] = projected[:, width : 2 * width].astype(BF)
    proj_ref[:, 2 * width :] = (projected[:, 2 * width :] + vec_ref[4:5, :]).astype(BF)
    lanes = 2 * (width // HEADS)
    for page in range(mask_ref.shape[0]):
        rows = slice(page * slots, (page + 1) * slots)
        bias = mask_ref[page]
        for pair in range(PAIRS):
            at = pair * lanes
            queries = proj_ref[rows, at : at + lanes] * jnp.asarray(scale, BF)
            keys_in = split_heads(proj_ref[rows, width + at : width + at + lanes])
            values = split_heads(proj_ref[rows, 2 * width + at : 2 * width + at + lanes])
            scores = dot_nt(queries, keys_in)
            soft = []
            for head in range(2):
                masked = scores[:, head * slots : (head + 1) * slots] + bias
                peak = jnp.max(masked, axis=-1, keepdims=True)
                exponent = jnp.exp(masked - peak)
                total = jnp.sum(exponent, axis=-1, keepdims=True)
                soft.append((exponent * (1.0 / total)).astype(BF))
            probs = jnp.concatenate(soft, axis=1)
            probs_ref[page, pair] = probs
            mixed_ref[rows, at : at + lanes] = dot_nn(probs, values).astype(BF)
    middle = stream + dot_nn(mixed_ref[...], out_s[...]) + vec_ref[5:6, :]
    middle_ref[...] = middle
    unit, _ = normalize(middle)
    nffn_ref[...] = (unit * vec_ref[1:2, :] + vec_ref[6:7, :]).astype(BF)


def attention_forward(me, stream, mask, vec, weight, block_pages, parts):
    plan, arrays = weight
    rows, width = stream.shape
    pages, slots, _ = mask.shape
    block = block_pages * slots
    row_spec = lambda cols: pl.BlockSpec((block, cols), lambda i: (i, 0))
    return pl.pallas_call(
        functools.partial(attention_forward_kernel, plan),
        grid=(pages // block_pages,),
        in_specs=[
            pl.BlockSpec(memory_space=pltpu.SMEM),
            row_spec(width),
            pl.BlockSpec((block_pages, slots, slots), lambda i: (i, 0, 0)),
            pl.BlockSpec(vec.shape, lambda i: (0, 0)),
        ]
        + [pl.BlockSpec(memory_space=pl.ANY)] * len(arrays),
        out_specs=[
            row_spec(width),
            row_spec(width),
            row_spec(width),
            row_spec(3 * width),
            pl.BlockSpec((block_pages, PAIRS, slots, 2 * slots), lambda i: (i, 0, 0, 0)),
            row_spec(width),
            pl.BlockSpec((width, 3 * width), lambda i: (0, 0)),
            pl.BlockSpec((width, width), lambda i: (0, 0)),
        ],
        out_shape=[
            jax.ShapeDtypeStruct((rows, width), F32),
            jax.ShapeDtypeStruct((rows, width), BF),
            jax.ShapeDtypeStruct((rows, width), BF),
            jax.ShapeDtypeStruct((rows, 3 * width), BF),
            jax.ShapeDtypeStruct((pages, PAIRS, slots, 2 * slots), BF),
            jax.ShapeDtypeStruct((rows, width), BF),
            jax.ShapeDtypeStruct((width, 3 * width), BF),
            jax.ShapeDtypeStruct((width, width), BF),
        ],
        scratch_shapes=[
            pltpu.VMEM((parts, width, width), BF),
            pltpu.SemaphoreType.DMA((copy_count(plan, arrays),)),
        ],
        compiler_params=pltpu.CompilerParams(vmem_limit_bytes=VMEM_LIMIT),
        cost_estimate=pl.CostEstimate(flops=20 * 10**9, bytes_accessed=30 * 10**6, transcendentals=0),
        name="attention_forward",
    )(me, stream, mask, vec, *arrays)


def ffn_forward_kernel(plans, me_ref, nffn_ref, middle_ref, vec_ref, hidden_ref, *refs):
    result_ref, active_ref, slope_ref, up_s, down_s, up_sems, down_sems = refs[-7:]
    up_refs = refs[: (len(refs) - 7) // 2]
    down_refs = refs[len(up_refs) : -7]

    @pl.when(pl.program_id(0) == 0)
    def _():
        load_weights([(plans[0], up_refs, me_ref, up_s, up_sems), (plans[1], down_refs, me_ref, down_s, down_sems)])

    nffn = nffn_ref[...]
    parts, _, chunk = up_s.shape
    total = middle_ref[...] + vec_ref[7:8, :]
    curve = 0.7978845608028654
    for part in range(parts):
        cols = slice(part * chunk, (part + 1) * chunk)
        upper = dot_nn(nffn, up_s[part]) + hidden_ref[:, cols]
        square = upper * upper
        angle = jnp.tanh(upper * (curve + (curve * 0.044715) * square))
        half = 0.5 * upper
        lift = 1.0 + angle
        active = (half * lift).astype(BF)
        slope = 0.5 * lift + half * (1.0 - angle * angle) * (curve + (3.0 * curve * 0.044715) * square)
        active_ref[:, cols] = active
        slope_ref[:, cols] = slope.astype(BF)
        total = total + dot_nt(active, down_s[part])
    result_ref[...] = total


def ffn_forward(me, nffn, middle, vec, hidden, up_w, down_w, block, parts):
    rows, width = nffn.shape
    ffn = hidden.shape[1]
    arrays = up_w[1] + down_w[1]
    row_spec = lambda cols: pl.BlockSpec((block, cols), lambda i: (i, 0))
    return pl.pallas_call(
        functools.partial(ffn_forward_kernel, (up_w[0], down_w[0])),
        grid=(rows // block,),
        in_specs=[
            pl.BlockSpec(memory_space=pltpu.SMEM),
            row_spec(width),
            row_spec(width),
            pl.BlockSpec(vec.shape, lambda i: (0, 0)),
            pl.BlockSpec(hidden.shape, lambda i: (0, 0)),
        ]
        + [pl.BlockSpec(memory_space=pl.ANY)] * len(arrays),
        out_specs=[row_spec(width), row_spec(ffn), row_spec(ffn)],
        out_shape=[
            jax.ShapeDtypeStruct((rows, width), F32),
            jax.ShapeDtypeStruct((rows, ffn), BF),
            jax.ShapeDtypeStruct((rows, ffn), BF),
        ],
        scratch_shapes=[
            pltpu.VMEM((parts, width, ffn // parts), BF),
            pltpu.VMEM((parts, width, ffn // parts), BF),
            pltpu.SemaphoreType.DMA((copy_count(*up_w),)),
            pltpu.SemaphoreType.DMA((copy_count(*down_w),)),
        ],
        compiler_params=pltpu.CompilerParams(vmem_limit_bytes=VMEM_LIMIT),
        cost_estimate=pl.CostEstimate(flops=15 * 10**9, bytes_accessed=30 * 10**6, transcendentals=0),
        name="ffn_forward",
    )(me, nffn, middle, vec, hidden, *arrays)


def ffn_backward_kernel(plans, me_ref, grad_ref, slope_ref, middle_ref, vec_ref, *refs):
    gupper_ref, gmiddle_ref, small_ref, ghidden_ref, up_s, down_s, up_sems, down_sems = refs[-8:]
    up_refs = refs[: (len(refs) - 8) // 2]
    down_refs = refs[len(up_refs) : -8]

    @pl.when(pl.program_id(0) == 0)
    def _():
        small_ref[...] = jnp.zeros_like(small_ref)
        ghidden_ref[...] = jnp.zeros_like(ghidden_ref)
        load_weights([(plans[0], up_refs, me_ref, up_s, up_sems), (plans[1], down_refs, me_ref, down_s, down_sems)])

    grad = grad_ref[...].astype(F32)
    lower = grad.astype(BF)
    parts, _, chunk = up_s.shape
    gnormed = jnp.zeros(grad.shape, F32)
    for part in range(parts):
        cols = slice(part * chunk, (part + 1) * chunk)
        gupper = (dot_nn(lower, down_s[part]) * slope_ref[:, cols].astype(F32)).astype(BF)
        gupper_ref[:, cols] = gupper
        ghidden_ref[:, cols] += column_sum(gupper.astype(F32))
        gnormed = gnormed + dot_nt(gupper, up_s[part])
    unit, root = normalize(middle_ref[...])
    gmiddle = grad + norm_backward(gnormed, unit, root, vec_ref[1:2, :])
    gmiddle_ref[...] = gmiddle
    small_ref[0:1, :] += column_sum(gnormed * unit)
    small_ref[1:2, :] += column_sum(gnormed)
    small_ref[2:3, :] += column_sum(lower.astype(F32))
    small_ref[3:4, :] += column_sum(gmiddle.astype(BF).astype(F32))


def ffn_backward(me, grad, slope, middle, vec, up_w, down_w, block, parts):
    rows, width = grad.shape
    ffn = slope.shape[1]
    arrays = up_w[1] + down_w[1]
    row_spec = lambda cols: pl.BlockSpec((block, cols), lambda i: (i, 0))
    return pl.pallas_call(
        functools.partial(ffn_backward_kernel, (up_w[0], down_w[0])),
        grid=(rows // block,),
        in_specs=[
            pl.BlockSpec(memory_space=pltpu.SMEM),
            row_spec(width),
            row_spec(ffn),
            row_spec(width),
            pl.BlockSpec(vec.shape, lambda i: (0, 0)),
        ]
        + [pl.BlockSpec(memory_space=pl.ANY)] * len(arrays),
        out_specs=[
            row_spec(ffn),
            row_spec(width),
            pl.BlockSpec((8, width), lambda i: (0, 0)),
            pl.BlockSpec((1, ffn), lambda i: (0, 0)),
        ],
        out_shape=[
            jax.ShapeDtypeStruct((rows, ffn), BF),
            jax.ShapeDtypeStruct((rows, width), F32),
            jax.ShapeDtypeStruct((8, width), F32),
            jax.ShapeDtypeStruct((1, ffn), F32),
        ],
        scratch_shapes=[
            pltpu.VMEM((parts, width, ffn // parts), BF),
            pltpu.VMEM((parts, width, ffn // parts), BF),
            pltpu.SemaphoreType.DMA((copy_count(*up_w),)),
            pltpu.SemaphoreType.DMA((copy_count(*down_w),)),
        ],
        compiler_params=pltpu.CompilerParams(vmem_limit_bytes=VMEM_LIMIT),
        cost_estimate=pl.CostEstimate(flops=15 * 10**9, bytes_accessed=30 * 10**6, transcendentals=0),
        name="ffn_backward",
    )(me, grad, slope, middle, vec, *arrays)


def ffn_weight_kernel(nffn_ref, grad_ref, gupper_ref, active_ref, out_ref, nffn_t, grad_t):
    @pl.when(pl.program_id(0) == 0)
    def _():
        nffn_t[...] = nffn_ref[...].T
        grad_t[...] = grad_ref[...].astype(BF).T

    shape = (out_ref.shape[0],) + out_ref.shape[3:]
    out_ref[:, 0, 0] = dot_nn(nffn_t[...], gupper_ref[...]).astype(BF).reshape(shape)
    out_ref[:, 0, 1] = dot_nn(grad_t[...], active_ref[...]).astype(BF).reshape(shape)


def ffn_weight(nffn, grad, gupper, active, stripes, parts):
    rows, width = nffn.shape
    piece = gupper.shape[1] // parts
    high = width // stripes
    whole = pl.BlockSpec((rows, width), lambda i: (0, 0))
    return pl.pallas_call(
        ffn_weight_kernel,
        grid=(parts,),
        in_specs=[
            whole,
            whole,
            pl.BlockSpec((rows, piece), lambda i: (0, i)),
            pl.BlockSpec((rows, piece), lambda i: (0, i)),
        ],
        out_specs=pl.BlockSpec((stripes, 1, 2, high, piece), lambda i: (0, i, 0, 0, 0)),
        out_shape=jax.ShapeDtypeStruct((stripes, parts, 3, high, piece), BF),
        scratch_shapes=[pltpu.VMEM((width, rows), BF), pltpu.VMEM((width, rows), BF)],
        compiler_params=pltpu.CompilerParams(vmem_limit_bytes=VMEM_LIMIT),
        cost_estimate=pl.CostEstimate(flops=15 * 10**9, bytes_accessed=30 * 10**6, transcendentals=0),
        name="ffn_weight",
    )(nffn, grad, gupper, active)


def attention_backward_kernel(gmiddle_ref, stream_ref, proj_ref, probs_ref, vec_ref, qkv_s, out_s, *refs):
    gstream_ref, gproj_ref, small_ref, gmixed_s = refs[-4:]

    @pl.when(pl.program_id(0) == 0)
    def _():
        small_ref[...] = jnp.zeros_like(small_ref)

    width = stream_ref.shape[1]
    block_pages, _, slots, _ = probs_ref.shape
    scale = (width // HEADS) ** (-0.5)
    gmiddle = gmiddle_ref[...]
    gmixed_s[...] = dot_nt(gmiddle.astype(BF), out_s[...]).astype(BF)
    lanes = 2 * (width // HEADS)
    for page in range(block_pages):
        rows = slice(page * slots, (page + 1) * slots)
        for pair in range(PAIRS):
            at = pair * lanes
            gmixed = gmixed_s[rows, at : at + lanes]
            queries = split_heads(proj_ref[rows, at : at + lanes])
            keys_in = split_heads(proj_ref[rows, width + at : width + at + lanes])
            values = split_heads(proj_ref[rows, 2 * width + at : 2 * width + at + lanes])
            probs = probs_ref[page, pair]
            gsoft = dot_nt(gmixed, values)
            gscore = []
            for head in range(2):
                cols = slice(head * slots, (head + 1) * slots)
                soft = probs[:, cols].astype(F32)
                grad = gsoft[:, cols]
                inner = jnp.sum(soft * grad, axis=-1, keepdims=True)
                gscore.append((soft * (grad - inner)).astype(BF))
            stacked = jnp.concatenate([probs[:, :slots], probs[:, slots:]], axis=0)
            gvalues = dot_tn(stacked, split_heads(gmixed))
            gqueries = dot_nn(jnp.concatenate(gscore, axis=1), keys_in) * scale
            gkeys = dot_tn(jnp.concatenate(gscore, axis=0), queries) * scale
            gproj_ref[rows, at : at + lanes] = gqueries.astype(BF)
            gproj_ref[rows, width + at : width + at + lanes] = gkeys.astype(BF)
            gproj_ref[rows, 2 * width + at : 2 * width + at + lanes] = gvalues.astype(BF)
    gnormed = dot_nt(gproj_ref[...], qkv_s[...])
    unit, root = normalize(stream_ref[...].astype(F32))
    gstream_ref[...] = gmiddle + norm_backward(gnormed, unit, root, vec_ref[0:1, :])
    small_ref[0:1, :] += column_sum(gnormed * unit)
    small_ref[1:2, :] += column_sum(gnormed)
    small_ref[2:3, :] += column_sum(gproj_ref[:, :width].astype(F32))
    small_ref[3:4, :] += column_sum(gproj_ref[:, 2 * width :].astype(F32))


def attention_backward(gmiddle, stream, proj, probs, vec, weight, block_pages, begin, end, before):
    rows, width = stream.shape
    _, _, slots, _ = probs.shape
    block = block_pages * slots
    first = begin // block_pages
    row_spec = lambda cols: pl.BlockSpec((block, cols), lambda i: (i + first, 0))
    whole = lambda array: pl.BlockSpec(array.shape, lambda i: (0, 0))
    before = [] if before is None else list(before)
    operands = [gmiddle, stream, proj, probs, vec, weight[0], weight[1]]
    return pl.pallas_call(
        attention_backward_kernel,
        grid=((end - begin) // block_pages,),
        in_specs=[
            row_spec(width),
            row_spec(width),
            row_spec(3 * width),
            pl.BlockSpec((block_pages, PAIRS, slots, 2 * slots), lambda i: (i + first, 0, 0, 0)),
            whole(vec),
            whole(weight[0]),
            whole(weight[1]),
        ]
        + [pl.BlockSpec(memory_space=pl.ANY)] * len(before),
        out_specs=[row_spec(width), row_spec(3 * width), pl.BlockSpec((8, width), lambda i: (0, 0))],
        out_shape=[
            jax.ShapeDtypeStruct((rows, width), F32),
            jax.ShapeDtypeStruct((rows, 3 * width), BF),
            jax.ShapeDtypeStruct((8, width), F32),
        ],
        scratch_shapes=[pltpu.VMEM((block, width), BF)],
        input_output_aliases={len(operands) + index: index for index in range(len(before))},
        compiler_params=pltpu.CompilerParams(vmem_limit_bytes=VMEM_LIMIT),
        cost_estimate=pl.CostEstimate(flops=15 * 10**9, bytes_accessed=20 * 10**6, transcendentals=0),
        name="attention_backward",
    )(*operands, *before)


def attention_weight_kernel(normed_ref, mixed_ref, gproj_ref, gmiddle_ref, _, grad_ref):
    gqkv = dot_tn(normed_ref[...], gproj_ref[...])
    gout = dot_tn(mixed_ref[...], gmiddle_ref[...].astype(BF))
    parts = grad_ref.shape[1]
    cut = gqkv.shape[1] // parts
    rest = gout.shape[1] // parts
    shape = (grad_ref.shape[0],) + grad_ref.shape[3:]
    for part in range(parts):
        qkv_part = gqkv[:, part * cut : (part + 1) * cut].astype(BF)
        out_part = gout[:, part * rest : (part + 1) * rest].astype(BF)
        grad_ref[:, part, 0] = jnp.concatenate([qkv_part, out_part], axis=1).reshape(shape)


def attention_weight(normed, mixed, gproj, gmiddle, before):
    rows, width = normed.shape
    block = width // 2
    stripes, parts, _, high, _ = before.shape
    return pl.pallas_call(
        attention_weight_kernel,
        grid=(2,),
        in_specs=[
            pl.BlockSpec((rows, block), lambda i: (0, i)),
            pl.BlockSpec((rows, block), lambda i: (0, i)),
            pl.BlockSpec((rows, 3 * width), lambda i: (0, 0)),
            pl.BlockSpec((rows, width), lambda i: (0, 0)),
            pl.BlockSpec(memory_space=pl.ANY),
        ],
        out_specs=pl.BlockSpec((stripes // 2, parts, 1, high, width), lambda i: (i, 0, 2, 0, 0)),
        out_shape=jax.ShapeDtypeStruct(before.shape, BF),
        input_output_aliases={4: 0},
        compiler_params=pltpu.CompilerParams(vmem_limit_bytes=VMEM_LIMIT),
        cost_estimate=pl.CostEstimate(flops=10 * 10**9, bytes_accessed=20 * 10**6, transcendentals=0),
        name="attention_weight",
    )(normed, mixed, gproj, gmiddle, before)


def relative_rows(order, source, target, me, high, offset):
    stripe = source.shape[0] // len(order)
    for place, relative in enumerate(order):
        start = pl.multiple_of(jnp.bitwise_xor(me, relative) * stripe + offset, 16)
        target[place * high : (place + 1) * high, :] = source[pl.ds(start, high), :]


def plane_order(depth):
    return [2 * z + x for x in range(2) for z in range(depth)]


def ffn_weight_split_kernel(
    me_ref, nffn_ref, grad_ref, gupper_ref, active_ref, up_one, up_zero, down_one, down_zero, turned, nffn_t, grad_t
):
    step = pl.program_id(0)
    depth, high = up_one.shape[2:4]

    @pl.when(step == 0)
    def _():
        turned[...] = nffn_ref[...].T
        relative_rows(plane_order(depth), turned, nffn_t, me_ref[0], high, 0)
        turned[...] = grad_ref[...].astype(BF).T
        relative_rows(plane_order(depth), turned, grad_t, me_ref[0], high, 0)

    gup = dot_nn(nffn_t[...], gupper_ref[...]).astype(BF)
    gdown = dot_nn(grad_t[...], active_ref[...]).astype(BF)

    @pl.when(step < 2)
    def _():
        up_one[...] = gup.reshape(up_one.shape)
        down_one[...] = gdown.reshape(down_one.shape)

    @pl.when(step >= 2)
    def _():
        up_zero[...] = gup.reshape(up_zero.shape)
        down_zero[...] = gdown.reshape(down_zero.shape)


def ffn_weight_split(me, nffn, grad, gupper, active, depth):
    rows, width = nffn.shape
    piece = gupper.shape[1] // 4
    high = width // (2 * depth)

    def column(step, me):
        return (0, jnp.bitwise_xor(me[1], 2 * jnp.bitwise_and(step, 1) + 1 - step // 2))

    whole = pl.BlockSpec((rows, width), lambda i, me: (0, 0))
    up_block, down_block = (1, 2, depth, high, piece), (2, 1, depth, high, piece)
    return pl.pallas_call(
        ffn_weight_split_kernel,
        grid_spec=pltpu.PrefetchScalarGridSpec(
            num_scalar_prefetch=1,
            grid=(4,),
            in_specs=[whole, whole, pl.BlockSpec((rows, piece), column), pl.BlockSpec((rows, piece), column)],
            out_specs=[
                pl.BlockSpec(up_block, lambda i, me: (jnp.minimum(i, 1), 0, 0, 0, 0)),
                pl.BlockSpec(up_block, lambda i, me: (jnp.maximum(i - 2, 0), 0, 0, 0, 0)),
                pl.BlockSpec(down_block, lambda i, me: (0, jnp.minimum(i, 1), 0, 0, 0)),
                pl.BlockSpec(down_block, lambda i, me: (0, jnp.maximum(i - 2, 0), 0, 0, 0)),
            ],
            scratch_shapes=[pltpu.VMEM((width, rows), BF)] * 3,
        ),
        out_shape=[jax.ShapeDtypeStruct((2, 2, depth, high, piece), BF)] * 4,
        compiler_params=pltpu.CompilerParams(vmem_limit_bytes=VMEM_LIMIT),
        cost_estimate=pl.CostEstimate(flops=15 * 10**9, bytes_accessed=30 * 10**6, transcendentals=0),
        name="ffn_weight",
    )(me, nffn, grad, gupper, active)


def attention_weight_split_kernel(
    me_ref, normed_ref, mixed_ref, gproj_ref, gmiddle_ref,
    a_one, a_zero, b_one, b_zero, normed_t, mixed_t, normed_r, mixed_r, joined,
):
    half = pl.program_id(0)
    depth, high, width = a_one.shape[2:]

    @pl.when(half == 0)
    def _():
        normed_t[...] = normed_ref[...].T
        mixed_t[...] = mixed_ref[...].T

    relative_rows(plane_order(depth), normed_t, normed_r, me_ref[0], high, half * high)
    relative_rows(plane_order(depth), mixed_t, mixed_r, me_ref[0], high, half * high)
    gqkv = dot_nn(normed_r[...], gproj_ref[...])
    gout = dot_nn(mixed_r[...], gmiddle_ref[...].astype(BF))
    cut = gqkv.shape[1] // 4
    rest = gout.shape[1] // 4
    for part in range(4):
        qkv_part = gqkv[:, part * cut : (part + 1) * cut].astype(BF)
        out_part = gout[:, part * rest : (part + 1) * rest].astype(BF)
        joined[jnp.bitwise_xor(me_ref[1], part)] = jnp.concatenate([qkv_part, out_part], axis=1)

    @pl.when(half == 0)
    def _():
        for y in range(2):
            a_zero[y] = joined[2 * y].reshape(2, depth, high, width)
            a_one[y] = joined[2 * y + 1].reshape(2, depth, high, width)

    @pl.when(half == 1)
    def _():
        for y in range(2):
            b_zero[:, y] = joined[2 * y].reshape(2, depth, high, width)
            b_one[:, y] = joined[2 * y + 1].reshape(2, depth, high, width)


def attention_weight_split(me, normed, mixed, gproj, gmiddle, depth):
    rows, width = normed.shape
    high = width // (4 * depth)
    whole = lambda array: pl.BlockSpec(array.shape, lambda i: (0, 0))
    shape = (2, 2, depth, high, width)
    return pl.pallas_call(
        attention_weight_split_kernel,
        grid=(2,),
        in_specs=[pl.BlockSpec(memory_space=pltpu.SMEM), whole(normed), whole(mixed), whole(gproj), whole(gmiddle)],
        out_specs=[pl.BlockSpec(shape, lambda i: (0, 0, 0, 0, 0))] * 4,
        out_shape=[jax.ShapeDtypeStruct(shape, BF)] * 4,
        scratch_shapes=[
            pltpu.VMEM((width, rows), BF),
            pltpu.VMEM((width, rows), BF),
            pltpu.VMEM((width // 2, rows), BF),
            pltpu.VMEM((width // 2, rows), BF),
            pltpu.VMEM((4, width // 2, width), BF),
        ],
        compiler_params=pltpu.CompilerParams(vmem_limit_bytes=VMEM_LIMIT),
        cost_estimate=pl.CostEstimate(flops=10 * 10**9, bytes_accessed=20 * 10**6, transcendentals=0),
        name="attention_weight",
    )(me, normed, mixed, gproj, gmiddle)


def pair_bias(slot_kind, slot_valid, across):
    same_kind = slot_kind[:, :, None] == slot_kind[:, None, :]
    partner = jnp.logical_not(same_kind) if across else same_kind
    allowed = jnp.logical_and(partner, slot_valid[:, None, :] > 0)
    return jnp.where(allowed, 0.0, -1e30).astype(F32)


def adam_step(master, grad, moment_one, moment_two, factor, decayed):
    clipped = grad * factor
    first_new = beta_one * moment_one + (1.0 - beta_one) * clipped
    second_new = beta_two * moment_two + (1.0 - beta_two) * clipped * clipped
    change = first_new / bias_one / (jnp.sqrt(second_new / bias_two) + epsilon)
    if decayed:
        change = change + weight_decay * master
    return (-learn_rate * change, first_new, second_new)


def gather_rows(pieces, sizes):
    high, width = pieces.shape[1:]
    rows = lax.all_gather(pieces.reshape(-1, width), ("dp", "tensor"), axis=0, tiled=False)
    if high % 16 == 0:
        return [(("rows", offset * high), [rows]) for offset in (2, 0, 1)]
    split = rows.reshape(sizes["dp"], sizes["tensor"], 3, high, width)
    return [(("whole",), [jnp.swapaxes(split[:, :, kind], 0, 1).reshape(-1, width, width)]) for kind in (2, 0, 1)]


def scatter_rows(grad, sizes):
    stripes, parts, kinds, high, width = grad.shape
    inner = sizes["dp"] // stripes
    if inner > 1:
        grad = jnp.moveaxis(grad.reshape(stripes, parts, kinds, inner, high // inner, width), 3, 1)
    mine = lax.psum_scatter(grad.reshape(-1, width), ("dp", "tensor"), scatter_dimension=0, tiled=True)
    return mine.reshape(kinds, -1, width).astype(F32)


class Exchange:
    def __init__(self, sizes):
        self.sizes = sizes
        self.depth = sizes["dp"] // 2

    def swap(self, axis, bits, value):
        return lax.ppermute(value, axis, [(index, index ^ bits) for index in range(self.sizes[axis])])

    def core(self, value):
        return self.swap("tensor", 1, value)

    def along(self, name, value):
        return self.swap("dp", 1, value) if name == "x" else self.swap("tensor", 2, value)

    def depths(self, values):
        return [self.swap("dp", 2 * z, values[z]) for z in range(1, self.depth)]

    def diagonal(self, value):
        dp, tensor = self.sizes["dp"], self.sizes["tensor"]
        pairs = [(i * tensor + j, (i ^ 1) * tensor + (j ^ 2)) for i in range(dp) for j in range(tensor)]
        return lax.ppermute(value, ("dp", "tensor"), pairs)

    def rounds(self):
        along_z = [functools.partial(self.swap, "dp", 2 * z) for z in range(1, self.depth)]
        plane = [functools.partial(self.along, "x"), functools.partial(self.along, "y"), self.diagonal]
        return along_z, plane, [self.core]

    def total(self, value):
        for moves in self.rounds():
            value = tree_sum([value] + [move(value) for move in moves])
        return value


def tree_sum(values):
    while len(values) > 1:
        values = [values[at] + values[at + 1] for at in range(0, len(values), 2)]
    return values[0]


def tie(values, after):
    return lax.optimization_barrier((values, after))[0]


class Spread:
    def __init__(self, exchange, first, second, row, pieces):
        self.exchange, self.first, self.second, self.row = exchange, first, second, row
        self.quad = jnp.stack(pieces)

    def go_first(self, after=None):
        quad = self.quad if after is None else tie(self.quad, after)
        self.one = self.exchange.along(self.first, quad)
        self.pair = jnp.stack([quad, self.one])
        return self.one

    def go_second(self):
        self.two = self.exchange.along(self.second, self.pair)
        return self.two

    def go_core(self, after=None):
        two = self.two if after is None else tie(self.two, after)
        self.far = [self.exchange.core(self.pair), self.exchange.core(two)]

    def units(self):
        spot = lambda near, side, core: (near, side, core) if self.first == "x" else (side, near, core)
        plan, arrays = [], []
        for core, (pair, two) in enumerate(((self.pair, self.two), self.far)):
            for side, value in enumerate((pair, two)):
                plan.append((self.row, [spot(0, side, core), spot(1, side, core)]))
                arrays.append(value)
        return plan, arrays


def near_weight(spreads):
    units = [spread.units() for spread in spreads]
    return (("near", sum([unit[0] for unit in units], [])), sum([unit[1] for unit in units], []))


class Reduce:
    def __init__(self, exchange, first, second, other, own):
        self.exchange, self.first, self.second, self.other, self.own = exchange, first, second, other, own

    def go_core(self):
        return [(self.exchange.core, self.other)]

    def took_core(self, came):
        self.came = came[0]

    def wide(self, value):
        return value.astype(F32)

    def go_second(self):
        value = (self.wide(self.own[1]) + self.wide(self.came[1])).astype(BF)
        return [(functools.partial(self.exchange.along, self.second), value)]

    def took_second(self, came):
        self.beside = came[0]

    def near(self, at):
        return self.wide(self.own[0, at]) + self.wide(self.came[0, at]) + self.wide(self.beside[at])

    def go_first(self):
        return [(functools.partial(self.exchange.along, self.first), self.near(1).astype(BF))]

    def took_first(self, came):
        self.ahead = came[0]
        self.layers = [
            self.wide(self.own[0, 0, z])
            + self.wide(self.came[0, 0, z])
            + self.wide(self.beside[0, z])
            + self.wide(self.ahead[z])
            for z in range(self.exchange.depth)
        ]


def depth_sends(exchange, reduces):
    return [
        (
            functools.partial(exchange.swap, "dp", 2 * z),
            jnp.concatenate([reduce.layers[z].astype(BF) for reduce in reduces], axis=0),
        )
        for z in range(1, exchange.depth)
    ]


def depth_total(reduces, came):
    total = jnp.concatenate([reduce.layers[0] for reduce in reduces], axis=0)
    for value in came:
        total = total + value.astype(F32)
    return total


class Lane:
    def __init__(self):
        self.last = None
        self.flying = []

    def send(self, sends):
        values = [value for _, value in sends]
        if self.last is not None:
            values = tie(values, self.last)
        came = [move(value) for (move, _), value in zip(sends, values)]
        return came

    def run(self, kernel, arrays, landed=()):
        if self.last is not None:
            arrays = tie(list(arrays), (self.last, list(landed)))
        result = kernel(*arrays)
        self.last = result[-1]
        return result


def shards(
    sizes,
    tokens, out_grad, slot_kind, slot_valid,
    qkv_weight, qkv_first, qkv_second,
    out_weight, out_first, out_second,
    up_weight, up_first, up_second,
    down_weight, down_first, down_second,
    gain_weight, gain_first, gain_second,
    bias_weight, bias_first, bias_second,
    hidden_weight, hidden_first, hidden_second,
):
    parts = sizes["tensor"]
    width = tokens.shape[1]
    cut = qkv_weight.shape[2]
    high = qkv_weight.shape[1]
    split = parts == 4 and high % 32 == 0 and sizes["dp"] in (4, 8, 16)
    exchange = Exchange(sizes)
    stripes = sizes["dp"] if high % 16 == 0 else 2
    me = jnp.stack([lax.axis_index("dp"), lax.axis_index("tensor")]).astype(jnp.int32)
    attn_pieces = jnp.concatenate([qkv_weight.astype(BF), out_weight.astype(BF)], axis=2)
    up_pieces = up_weight.astype(BF)
    down_pieces = jnp.swapaxes(down_weight.astype(BF), 1, 2)
    pages = slot_kind.shape[0]
    block_pages = 2 if pages % 2 == 0 else 1
    block = block_pages * slot_kind.shape[1]
    middle_page = block_pages
    masks = [pair_bias(slot_kind, slot_valid, index == 0) for index in range(2)]
    lane = Lane()
    gathered = lambda index: gather_rows(
        jnp.stack([up_pieces[index], down_pieces[index], attn_pieces[index]]), sizes
    )
    attn_w, up_w, down_w = ([None, None] for _ in range(3))
    attn_w[1], up_w[1], down_w[1] = gathered(1)
    if split:
        piece = attn_pieces[0]
        depth_attn = [piece] + exchange.depths([piece] * exchange.depth)
        own_small = jnp.concatenate(
            [gain_weight, bias_weight, hidden_weight.reshape(2, -1, gain_weight.shape[2])], axis=1
        )
        own_small = lax.reduce_precision(own_small, 8, 7)
        others = [exchange.swap("tensor", bits, own_small) for bits in range(1, 4)]
        mine = lax.axis_index("tensor")
        every = jnp.zeros((4,) + own_small.shape, F32)
        for bits, value in enumerate([own_small] + others):
            every = lax.dynamic_update_slice_in_dim(every, value[None], jnp.bitwise_xor(mine, bits), 0)
        small = jnp.moveaxis(every[:, :, :8], 0, 2).reshape(2, 8, width)
        hidden = jnp.moveaxis(every[:, :, 8:], 0, 1).reshape(2, -1)

        piece = jnp.concatenate([up_pieces[0], down_pieces[0]], axis=0)
        piece = tie(piece, depth_attn[1:])
        depth_ffn = [piece] + exchange.depths([piece] * exchange.depth)
        attn_a = Spread(exchange, "x", "y", 0, [part[: high // 2] for part in depth_attn])
        attn_b = Spread(exchange, "y", "x", high // 2, [part[high // 2 :] for part in depth_attn])
        up_a = Spread(exchange, "x", "y", 0, [part[:high] for part in depth_ffn])
        down_b = Spread(exchange, "y", "x", 0, [part[high:] for part in depth_ffn])
        attn_a.go_first(others), attn_b.go_first(others)
        second = [attn_a.go_second(), attn_b.go_second()]
        attn_a.go_core(), attn_b.go_core()
        ready = [up_a.go_first(second), down_b.go_first(second)]
        attn_w[0] = near_weight([attn_a, attn_b])
        tokens_in = tie(tokens, ready)
        up_a.go_second(), down_b.go_second()
    else:
        small = jnp.concatenate([gain_weight, bias_weight], axis=1).astype(BF)
        small = lax.all_gather(small, "tensor", axis=2, tiled=True).astype(F32)
        hidden = lax.all_gather(hidden_weight.astype(BF), "tensor", axis=1, tiled=True).astype(F32)
        attn_w[0], up_w[0], down_w[0] = gathered(0)
        tokens_in = tokens

    stream = tokens_in
    saved = []
    for index in range(2):
        middle, nffn, normed, proj, probs, mixed, qkv_w, out_w = attention_forward(
            me, stream, masks[index], small[index], attn_w[index], block_pages, parts
        )
        if split and index == 0:
            up_a.go_core(nffn), down_b.go_core(nffn)
            up_w[0] = near_weight([up_a])
            down_w[0] = near_weight([down_b])
        result, active, slope = ffn_forward(
            me, nffn, middle, small[index], hidden[index : index + 1], up_w[index], down_w[index], block, parts
        )
        saved.append((stream, middle, nffn, normed, proj, probs, mixed, active, slope, (qkv_w, out_w)))
        stream = result
    block_output = stream

    def run_ffn_backward(index, grad, landed=()):
        _, middle, _, _, _, _, _, _, slope, _ = saved[index]
        kernel = lambda grad: ffn_backward(
            me, grad, slope, middle, small[index], up_w[index], down_w[index], block, parts
        )
        return lane.run(kernel, [grad], landed)

    def run_ffn_weight(index, grad, gupper, landed=()):
        _, _, nffn, _, _, _, _, active, _, _ = saved[index]
        if split and index == 0:
            kernel = lambda gupper: ffn_weight_split(me, nffn, grad, gupper, active, exchange.depth)
        else:
            kernel = lambda gupper: (ffn_weight(nffn, grad, gupper, active, stripes, parts),)
        return lane.run(kernel, [gupper], landed)

    def run_attention_backward(index, gmiddle, begin, end, before, landed=()):
        stream, _, _, _, proj, probs, _, _, _, weight = saved[index]
        kernel = lambda gmiddle: attention_backward(
            gmiddle, stream, proj, probs, small[index], weight, block_pages, begin, end, before
        )
        return lane.run(kernel, [gmiddle], landed)

    def run_attention_weight(index, gproj, gmiddle, before=None, landed=()):
        _, _, _, normed, _, _, mixed, _, _, _ = saved[index]
        if split and index == 0:
            kernel = lambda gproj: attention_weight_split(me, normed, mixed, gproj, gmiddle, exchange.depth)
        else:
            kernel = lambda gproj: (attention_weight(normed, mixed, gproj, gmiddle, before),)
        return lane.run(kernel, [gproj], landed)

    attn_g, up_g, down_g, small_g, hidden_g = ([None, None] for _ in range(5))
    grad = out_grad
    for index in (1, 0):
        gupper, gmiddle, small_two, ghidden = run_ffn_backward(index, grad)
        if split and index == 0:
            up_one, up_zero, down_one, down_zero = run_ffn_weight(index, grad, gupper)
            ffn = [Reduce(exchange, "x", "y", up_one, up_zero), Reduce(exchange, "y", "x", down_one, down_zero)]
            came = lane.send(ffn[0].go_core() + ffn[1].go_core())
            before = run_attention_backward(index, gmiddle, 0, middle_page, None)
            ffn[0].took_core(came[:1]), ffn[1].took_core(came[1:])
            landed = came
            came = lane.send(ffn[0].go_second() + ffn[1].go_second())
            after = run_attention_backward(index, gmiddle, middle_page, pages, before[:2], landed)
            ffn[0].took_second(came[:1]), ffn[1].took_second(came[1:])
            next_grad, gproj = after[:2]
            small_one = before[2] + after[2]
            landed = came
            came = lane.send(ffn[0].go_first() + ffn[1].go_first())
            a_one, a_zero, b_one, b_zero = run_attention_weight(index, gproj, gmiddle, None, landed)
            ffn[0].took_first(came[:1]), ffn[1].took_first(came[1:2])
            attn = [Reduce(exchange, "x", "y", a_one, a_zero), Reduce(exchange, "y", "x", b_one, b_zero)]
        else:
            (gffn,) = run_ffn_weight(index, grad, gupper)
            next_grad, gproj, small_one = run_attention_backward(index, gmiddle, 0, pages, None)
            (both,) = run_attention_weight(index, gproj, gmiddle, gffn)
            up_g[index], down_g[index], attn_g[index] = scatter_rows(both, sizes)
        grad = next_grad
        small_g[index] = jnp.concatenate([small_one, small_two], axis=0)
        hidden_g[index] = ghidden
    input_grad = grad

    if split:
        whole = jnp.concatenate(small_g + [value.reshape(-1, width) for value in hidden_g], axis=0)
        along_z, plane, across = exchange.rounds()
        count = exchange.depth - 1
        came = lane.send(attn[0].go_core() + attn[1].go_core() + depth_sends(exchange, ffn) + [(move, whole) for move in along_z])
        attn[0].took_core(came[:1]), attn[1].took_core(came[1:2])
        total = depth_total(ffn, came[2 : 2 + count])
        up_g[0], down_g[0] = total[:high], total[high:]
        whole = tree_sum([whole] + came[2 + count :])
        came = lane.send(attn[0].go_second() + attn[1].go_second() + [(move, whole) for move in plane])
        attn[0].took_second(came[:1]), attn[1].took_second(came[1:2])
        whole = tree_sum([whole] + came[2:])
        came = lane.send(attn[0].go_first() + attn[1].go_first() + [(move, whole) for move in across])
        attn[0].took_first(came[:1]), attn[1].took_first(came[1:2])
        whole = tree_sum([whole] + came[2:])
        attn_g[0] = depth_total(attn, lane.send(depth_sends(exchange, attn)))
        vectors = whole[:32].reshape(2, 16, width)
        grad_hidden = whole[32:].reshape(2, -1)
    else:
        vectors, grad_hidden = lax.psum((jnp.stack(small_g), jnp.concatenate(hidden_g, axis=0)), ("dp", "tensor"))
    grad_gain = jnp.stack([vectors[:, 0], vectors[:, 8]], axis=1)
    grad_bias = jnp.stack([vectors[:, row] for row in (1, 2, 3, 11, 9, 10)], axis=1)
    shared_squares = (
        jnp.sum(grad_gain * grad_gain) + jnp.sum(grad_bias * grad_bias) + jnp.sum(grad_hidden * grad_hidden)
    )
    at = lax.axis_index("tensor")
    slice_of = lambda whole, axis: lax.dynamic_slice_in_dim(
        whole, at * (whole.shape[axis] // parts), whole.shape[axis] // parts, axis
    )
    grad_gain = slice_of(grad_gain, 2)
    grad_bias = slice_of(grad_bias, 2)
    grad_hidden = slice_of(grad_hidden, 1)
    grad_attn = jnp.stack(attn_g)
    grad_up = jnp.stack(up_g)
    grad_down = jnp.stack(down_g)
    local_squares = (
        jnp.sum(grad_attn * grad_attn) + jnp.sum(grad_up * grad_up) + jnp.sum(grad_down * grad_down)
    )
    grad_down = jnp.swapaxes(grad_down, 1, 2)
    if split:
        local_squares = exchange.total(local_squares.reshape(1, 1))[0, 0]
    else:
        local_squares = lax.psum(local_squares, ("dp", "tensor"))
    total_squares = local_squares + shared_squares
    grad_norm = jnp.sqrt(total_squares)
    factor = clip_norm / jnp.maximum(grad_norm, clip_norm)
    masters = (qkv_weight, out_weight, up_weight, down_weight, gain_weight, bias_weight, hidden_weight)
    firsts = (qkv_first, out_first, up_first, down_first, gain_first, bias_first, hidden_first)
    seconds = (qkv_second, out_second, up_second, down_second, gain_second, bias_second, hidden_second)
    gradients = (
        grad_attn[:, :, :cut], grad_attn[:, :, cut:], grad_up, grad_down, grad_gain, grad_bias, grad_hidden,
    )
    results = [block_output, input_grad, grad_norm]
    for member in range(7):
        update, first_new, second_new = adam_step(
            masters[member], gradients[member], firsts[member], seconds[member], factor, member < 4
        )
        results = results + [gradients[member], update, first_new, second_new]
    return tuple(results)


def solution(mesh):
    rows = P(("dp", "tensor"), None)
    matrix = P(None, "dp", "tensor")
    turned = P(None, "tensor", "dp")
    vectors = P(None, None, "tensor")
    hidden = P(None, "tensor")
    return jax.shard_map(
        functools.partial(shards, dict(mesh.shape)),
        mesh=mesh,
        in_specs=(rows,) * 4 + (matrix,) * 9 + (turned,) * 3 + (vectors,) * 6 + (hidden,) * 3,
        out_specs=(rows, rows, P()) + (matrix,) * 12 + (turned,) * 4 + (vectors,) * 8 + (hidden,) * 4,
        check_vma=False,
    )
```

```python
import functools

import jax
import jax.numpy as jnp
from jax import lax
from jax.experimental import pallas as pl
from jax.experimental.pallas import tpu as pltpu
from jax.sharding import PartitionSpec as P

HEADS = 12
PAIRS = HEADS // 2

beta_one = 0.9
beta_two = 0.99
learn_rate = 0.01
weight_decay = 0.01
epsilon = 1e-08
clip_norm = 1.0
bias_one = 1.0 - beta_one**10
bias_two = 1.0 - beta_two**10

BF = jnp.bfloat16
F32 = jnp.float32
VMEM_LIMIT = 56 * 1024 * 1024


def dot_nn(a, b):
    return lax.dot_general(a, b, (((1,), (0,)), ((), ())), preferred_element_type=F32)


def dot_nt(a, b):
    return lax.dot_general(a, b, (((1,), (1,)), ((), ())), preferred_element_type=F32)


def dot_tn(a, b):
    return lax.dot_general(a, b, (((0,), (0,)), ((), ())), preferred_element_type=F32)


def normalize(stream):
    average = jnp.mean(stream, axis=-1, keepdims=True)
    centered = stream - average
    spread = jnp.mean(centered * centered, axis=-1, keepdims=True)
    root = lax.rsqrt(spread + 1e-05)
    return centered * root, root


def norm_backward(grad, unit, root, gain):
    scaled = grad * gain
    first = jnp.mean(scaled, axis=-1, keepdims=True)
    second = jnp.mean(scaled * unit, axis=-1, keepdims=True)
    return root * (scaled - first - unit * second)


def column_sum(value):
    return jnp.sum(value, axis=0, keepdims=True)


def split_heads(pair):
    lane = lax.broadcasted_iota(jnp.int32, pair.shape, 1)
    zero = jnp.zeros_like(pair)
    half = pair.shape[1] // 2
    return jnp.concatenate([jnp.where(lane < half, pair, zero), jnp.where(lane >= half, pair, zero)], axis=0)


def plane(me_ref, first, second, core):
    turned = jnp.bitwise_xor(jnp.bitwise_and(me_ref[1], 1), core) == 1
    return jnp.where(turned, second, first), jnp.where(turned, first, second)


def weight_copies(plan, refs, me_ref, full, sems):
    copies = []

    def add(source, target):
        copies.append(pltpu.make_async_copy(source, target, sems.at[len(copies)]))

    parts, width, _ = full.shape
    if plan[0] == "whole":
        add(refs[0], full)
    elif plan[0] == "rows":
        high = width * parts // refs[0].shape[0]
        for index in range(refs[0].shape[0]):
            stripe, part = divmod(index, parts)
            add(refs[0].at[index, pl.ds(plan[1], high), :], full.at[part, pl.ds(stripe * high, high), :])
    else:
        for ref, positions in zip(refs, plan[2]):
            depth = ref.shape[1]
            high = width // (2 * depth)
            for place, (first, second, core) in enumerate(positions):
                x, y = plane(me_ref, first, second, core)
                part = jnp.bitwise_xor(me_ref[1], 2 * y + core)
                origin = jnp.bitwise_and(me_ref[0], 1) if plan[3] else me_ref[0]
                for z in range(depth):
                    start = pl.multiple_of(jnp.bitwise_xor(origin, 2 * z + x) * high, 16)
                    add(ref.at[place, z, pl.ds(plan[1], high), :], full.at[part, pl.ds(start, high), :])
    return copies


def load_weights(groups):
    copies = [copy for group in groups for copy in weight_copies(*group)]
    for copy in copies:
        copy.start()
    for copy in copies:
        copy.wait()


def copy_count(plan, refs):
    if plan[0] == "whole":
        return 1
    if plan[0] == "rows":
        return refs[0].shape[0]
    return sum(ref.shape[0] * ref.shape[1] for ref in refs)


def split_attention(raw, qkv_s, out_s):
    parts = raw.shape[0]
    cut = qkv_s.shape[1] // parts
    step = 96

    def relay(index, _):
        rows = pl.ds(pl.multiple_of(index * step, step), step)
        pieces = [raw[part, rows, :] for part in range(parts)]
        qkv_s[rows, :] = jnp.concatenate([piece[:, :cut] for piece in pieces], axis=1)
        out_s[rows, :] = jnp.concatenate([piece[:, cut:] for piece in pieces], axis=1)
        return 0

    lax.fori_loop(0, raw.shape[1] // step, relay, 0)


def attention_forward_kernel(plan, me_ref, stream_ref, mask_ref, vec_ref, *refs):
    weight_refs = refs[:-10]
    middle_ref, nffn_ref, normed_ref, proj_ref, probs_ref, mixed_ref, qkv_s, out_s, raw, sems = refs[-10:]

    @pl.when(pl.program_id(0) == 0)
    def _():
        load_weights([(plan, weight_refs, me_ref, raw, sems)])
        split_attention(raw, qkv_s, out_s)

    width = stream_ref.shape[1]
    slots = mask_ref.shape[1]
    scale = (width // HEADS) ** (-0.5)
    stream = stream_ref[...].astype(F32)
    unit, _ = normalize(stream)
    normed = (unit * vec_ref[0:1, :] + vec_ref[2:3, :]).astype(BF)
    normed_ref[...] = normed
    projected = dot_nn(normed, qkv_s[...])
    proj_ref[:, :width] = (projected[:, :width] + vec_ref[3:4, :]).astype(BF)
    proj_ref[:, width : 2 * width] = projected[:, width : 2 * width].astype(BF)
    proj_ref[:, 2 * width :] = (projected[:, 2 * width :] + vec_ref[4:5, :]).astype(BF)
    lanes = 2 * (width // HEADS)
    for page in range(mask_ref.shape[0]):
        rows = slice(page * slots, (page + 1) * slots)
        bias = mask_ref[page]
        for pair in range(PAIRS):
            at = pair * lanes
            queries = proj_ref[rows, at : at + lanes] * jnp.asarray(scale, BF)
            keys_in = split_heads(proj_ref[rows, width + at : width + at + lanes])
            values = split_heads(proj_ref[rows, 2 * width + at : 2 * width + at + lanes])
            scores = dot_nt(queries, keys_in)
            soft = []
            for head in range(2):
                masked = scores[:, head * slots : (head + 1) * slots] + bias
                peak = jnp.max(masked, axis=-1, keepdims=True)
                exponent = jnp.exp(masked - peak)
                total = jnp.sum(exponent, axis=-1, keepdims=True)
                soft.append((exponent * (1.0 / total)).astype(BF))
            probs = jnp.concatenate(soft, axis=1)
            probs_ref[page, pair] = probs
            mixed_ref[rows, at : at + lanes] = dot_nn(probs, values).astype(BF)
    middle = stream + dot_nn(mixed_ref[...], out_s[...]) + vec_ref[5:6, :]
    middle_ref[...] = middle
    unit, _ = normalize(middle)
    nffn_ref[...] = (unit * vec_ref[1:2, :] + vec_ref[6:7, :]).astype(BF)


def attention_forward(me, stream, mask, vec, weight, block_pages, parts):
    plan, arrays = weight
    rows, width = stream.shape
    pages, slots, _ = mask.shape
    block = block_pages * slots
    row_spec = lambda cols: pl.BlockSpec((block, cols), lambda i: (i, 0))
    return pl.pallas_call(
        functools.partial(attention_forward_kernel, plan),
        grid=(pages // block_pages,),
        in_specs=[
            pl.BlockSpec(memory_space=pltpu.SMEM),
            row_spec(width),
            pl.BlockSpec((block_pages, slots, slots), lambda i: (i, 0, 0)),
            pl.BlockSpec(vec.shape, lambda i: (0, 0)),
        ]
        + [pl.BlockSpec(memory_space=pl.ANY)] * len(arrays),
        out_specs=[
            row_spec(width),
            row_spec(width),
            row_spec(width),
            row_spec(3 * width),
            pl.BlockSpec((block_pages, PAIRS, slots, 2 * slots), lambda i: (i, 0, 0, 0)),
            row_spec(width),
            pl.BlockSpec((width, 3 * width), lambda i: (0, 0)),
            pl.BlockSpec((width, width), lambda i: (0, 0)),
        ],
        out_shape=[
            jax.ShapeDtypeStruct((rows, width), F32),
            jax.ShapeDtypeStruct((rows, width), BF),
            jax.ShapeDtypeStruct((rows, width), BF),
            jax.ShapeDtypeStruct((rows, 3 * width), BF),
            jax.ShapeDtypeStruct((pages, PAIRS, slots, 2 * slots), BF),
            jax.ShapeDtypeStruct((rows, width), BF),
            jax.ShapeDtypeStruct((width, 3 * width), BF),
            jax.ShapeDtypeStruct((width, width), BF),
        ],
        scratch_shapes=[
            pltpu.VMEM((parts, width, width), BF),
            pltpu.SemaphoreType.DMA((copy_count(plan, arrays),)),
        ],
        compiler_params=pltpu.CompilerParams(vmem_limit_bytes=VMEM_LIMIT),
        cost_estimate=pl.CostEstimate(flops=20 * 10**9, bytes_accessed=30 * 10**6, transcendentals=0),
        name="attention_forward",
    )(me, stream, mask, vec, *arrays)


def ffn_forward_kernel(plans, me_ref, nffn_ref, middle_ref, vec_ref, hidden_ref, *refs):
    result_ref, active_ref, slope_ref, up_s, down_s, up_sems, down_sems = refs[-7:]
    up_refs = refs[: (len(refs) - 7) // 2]
    down_refs = refs[len(up_refs) : -7]

    @pl.when(pl.program_id(0) == 0)
    def _():
        load_weights([(plans[0], up_refs, me_ref, up_s, up_sems), (plans[1], down_refs, me_ref, down_s, down_sems)])

    nffn = nffn_ref[...]
    parts, _, chunk = up_s.shape
    total = middle_ref[...] + vec_ref[7:8, :]
    curve = 0.7978845608028654
    for part in range(parts):
        cols = slice(part * chunk, (part + 1) * chunk)
        upper = dot_nn(nffn, up_s[part]) + hidden_ref[:, cols]
        square = upper * upper
        angle = jnp.tanh(upper * (curve + (curve * 0.044715) * square))
        half = 0.5 * upper
        lift = 1.0 + angle
        active = (half * lift).astype(BF)
        slope = 0.5 * lift + half * (1.0 - angle * angle) * (curve + (3.0 * curve * 0.044715) * square)
        active_ref[:, cols] = active
        slope_ref[:, cols] = slope.astype(BF)
        total = total + dot_nt(active, down_s[part])
    result_ref[...] = total


def ffn_forward(me, nffn, middle, vec, hidden, up_w, down_w, block, parts):
    rows, width = nffn.shape
    ffn = hidden.shape[1]
    arrays = up_w[1] + down_w[1]
    row_spec = lambda cols: pl.BlockSpec((block, cols), lambda i: (i, 0))
    return pl.pallas_call(
        functools.partial(ffn_forward_kernel, (up_w[0], down_w[0])),
        grid=(rows // block,),
        in_specs=[
            pl.BlockSpec(memory_space=pltpu.SMEM),
            row_spec(width),
            row_spec(width),
            pl.BlockSpec(vec.shape, lambda i: (0, 0)),
            pl.BlockSpec(hidden.shape, lambda i: (0, 0)),
        ]
        + [pl.BlockSpec(memory_space=pl.ANY)] * len(arrays),
        out_specs=[row_spec(width), row_spec(ffn), row_spec(ffn)],
        out_shape=[
            jax.ShapeDtypeStruct((rows, width), F32),
            jax.ShapeDtypeStruct((rows, ffn), BF),
            jax.ShapeDtypeStruct((rows, ffn), BF),
        ],
        scratch_shapes=[
            pltpu.VMEM((parts, width, ffn // parts), BF),
            pltpu.VMEM((parts, width, ffn // parts), BF),
            pltpu.SemaphoreType.DMA((copy_count(*up_w),)),
            pltpu.SemaphoreType.DMA((copy_count(*down_w),)),
        ],
        compiler_params=pltpu.CompilerParams(vmem_limit_bytes=VMEM_LIMIT),
        cost_estimate=pl.CostEstimate(flops=15 * 10**9, bytes_accessed=30 * 10**6, transcendentals=0),
        name="ffn_forward",
    )(me, nffn, middle, vec, hidden, *arrays)


def ffn_backward_kernel(plans, me_ref, grad_ref, slope_ref, middle_ref, vec_ref, *refs):
    gupper_ref, gmiddle_ref, small_ref, ghidden_ref, up_s, down_s, up_sems, down_sems = refs[-8:]
    up_refs = refs[: (len(refs) - 8) // 2]
    down_refs = refs[len(up_refs) : -8]

    @pl.when(pl.program_id(0) == 0)
    def _():
        small_ref[...] = jnp.zeros_like(small_ref)
        ghidden_ref[...] = jnp.zeros_like(ghidden_ref)
        load_weights([(plans[0], up_refs, me_ref, up_s, up_sems), (plans[1], down_refs, me_ref, down_s, down_sems)])

    grad = grad_ref[...].astype(F32)
    lower = grad.astype(BF)
    parts, _, chunk = up_s.shape
    gnormed = jnp.zeros(grad.shape, F32)
    for part in range(parts):
        cols = slice(part * chunk, (part + 1) * chunk)
        gupper = (dot_nn(lower, down_s[part]) * slope_ref[:, cols].astype(F32)).astype(BF)
        gupper_ref[:, cols] = gupper
        ghidden_ref[:, cols] += column_sum(gupper.astype(F32))
        gnormed = gnormed + dot_nt(gupper, up_s[part])
    unit, root = normalize(middle_ref[...])
    gmiddle = grad + norm_backward(gnormed, unit, root, vec_ref[1:2, :])
    gmiddle_ref[...] = gmiddle
    small_ref[0:1, :] += column_sum(gnormed * unit)
    small_ref[1:2, :] += column_sum(gnormed)
    small_ref[2:3, :] += column_sum(lower.astype(F32))
    small_ref[3:4, :] += column_sum(gmiddle.astype(BF).astype(F32))


def ffn_backward(me, grad, slope, middle, vec, up_w, down_w, block, parts):
    rows, width = grad.shape
    ffn = slope.shape[1]
    arrays = up_w[1] + down_w[1]
    row_spec = lambda cols: pl.BlockSpec((block, cols), lambda i: (i, 0))
    return pl.pallas_call(
        functools.partial(ffn_backward_kernel, (up_w[0], down_w[0])),
        grid=(rows // block,),
        in_specs=[
            pl.BlockSpec(memory_space=pltpu.SMEM),
            row_spec(width),
            row_spec(ffn),
            row_spec(width),
            pl.BlockSpec(vec.shape, lambda i: (0, 0)),
        ]
        + [pl.BlockSpec(memory_space=pl.ANY)] * len(arrays),
        out_specs=[
            row_spec(ffn),
            row_spec(width),
            pl.BlockSpec((8, width), lambda i: (0, 0)),
            pl.BlockSpec((1, ffn), lambda i: (0, 0)),
        ],
        out_shape=[
            jax.ShapeDtypeStruct((rows, ffn), BF),
            jax.ShapeDtypeStruct((rows, width), F32),
            jax.ShapeDtypeStruct((8, width), F32),
            jax.ShapeDtypeStruct((1, ffn), F32),
        ],
        scratch_shapes=[
            pltpu.VMEM((parts, width, ffn // parts), BF),
            pltpu.VMEM((parts, width, ffn // parts), BF),
            pltpu.SemaphoreType.DMA((copy_count(*up_w),)),
            pltpu.SemaphoreType.DMA((copy_count(*down_w),)),
        ],
        compiler_params=pltpu.CompilerParams(vmem_limit_bytes=VMEM_LIMIT),
        cost_estimate=pl.CostEstimate(flops=15 * 10**9, bytes_accessed=30 * 10**6, transcendentals=0),
        name="ffn_backward",
    )(me, grad, slope, middle, vec, *arrays)


def ffn_weight_kernel(nffn_ref, grad_ref, gupper_ref, active_ref, out_ref, nffn_t, grad_t):
    @pl.when(pl.program_id(0) == 0)
    def _():
        nffn_t[...] = nffn_ref[...].T
        grad_t[...] = grad_ref[...].astype(BF).T

    shape = (out_ref.shape[0],) + out_ref.shape[3:]
    out_ref[:, 0, 0] = dot_nn(nffn_t[...], gupper_ref[...]).astype(BF).reshape(shape)
    out_ref[:, 0, 1] = dot_nn(grad_t[...], active_ref[...]).astype(BF).reshape(shape)


def ffn_weight(nffn, grad, gupper, active, stripes, parts):
    rows, width = nffn.shape
    piece = gupper.shape[1] // parts
    high = width // stripes
    whole = pl.BlockSpec((rows, width), lambda i: (0, 0))
    return pl.pallas_call(
        ffn_weight_kernel,
        grid=(parts,),
        in_specs=[
            whole,
            whole,
            pl.BlockSpec((rows, piece), lambda i: (0, i)),
            pl.BlockSpec((rows, piece), lambda i: (0, i)),
        ],
        out_specs=pl.BlockSpec((stripes, 1, 2, high, piece), lambda i: (0, i, 0, 0, 0)),
        out_shape=jax.ShapeDtypeStruct((stripes, parts, 2, high, piece), BF),
        scratch_shapes=[pltpu.VMEM((width, rows), BF), pltpu.VMEM((width, rows), BF)],
        compiler_params=pltpu.CompilerParams(vmem_limit_bytes=VMEM_LIMIT),
        cost_estimate=pl.CostEstimate(flops=15 * 10**9, bytes_accessed=30 * 10**6, transcendentals=0),
        name="ffn_weight",
    )(nffn, grad, gupper, active)


def attention_backward_kernel(gmiddle_ref, stream_ref, proj_ref, probs_ref, vec_ref, qkv_s, out_s, *refs):
    gstream_ref, gproj_ref, small_ref, gmixed_s = refs[-4:]

    @pl.when(pl.program_id(0) == 0)
    def _():
        small_ref[...] = jnp.zeros_like(small_ref)

    width = stream_ref.shape[1]
    block_pages, _, slots, _ = probs_ref.shape
    scale = (width // HEADS) ** (-0.5)
    gmiddle = gmiddle_ref[...]
    gmixed_s[...] = dot_nt(gmiddle.astype(BF), out_s[...]).astype(BF)
    lanes = 2 * (width // HEADS)
    for page in range(block_pages):
        rows = slice(page * slots, (page + 1) * slots)
        for pair in range(PAIRS):
            at = pair * lanes
            gmixed = gmixed_s[rows, at : at + lanes]
            queries = split_heads(proj_ref[rows, at : at + lanes])
            keys_in = split_heads(proj_ref[rows, width + at : width + at + lanes])
            values = split_heads(proj_ref[rows, 2 * width + at : 2 * width + at + lanes])
            probs = probs_ref[page, pair]
            gsoft = dot_nt(gmixed, values)
            gscore = []
            for head in range(2):
                cols = slice(head * slots, (head + 1) * slots)
                soft = probs[:, cols].astype(F32)
                grad = gsoft[:, cols]
                inner = jnp.sum(soft * grad, axis=-1, keepdims=True)
                gscore.append((soft * (grad - inner)).astype(BF))
            stacked = jnp.concatenate([probs[:, :slots], probs[:, slots:]], axis=0)
            gvalues = dot_tn(stacked, split_heads(gmixed))
            gqueries = dot_nn(jnp.concatenate(gscore, axis=1), keys_in) * scale
            gkeys = dot_tn(jnp.concatenate(gscore, axis=0), queries) * scale
            gproj_ref[rows, at : at + lanes] = gqueries.astype(BF)
            gproj_ref[rows, width + at : width + at + lanes] = gkeys.astype(BF)
            gproj_ref[rows, 2 * width + at : 2 * width + at + lanes] = gvalues.astype(BF)
    gnormed = dot_nt(gproj_ref[...], qkv_s[...])
    unit, root = normalize(stream_ref[...].astype(F32))
    gstream_ref[...] = gmiddle + norm_backward(gnormed, unit, root, vec_ref[0:1, :])
    small_ref[0:1, :] += column_sum(gnormed * unit)
    small_ref[1:2, :] += column_sum(gnormed)
    small_ref[2:3, :] += column_sum(gproj_ref[:, :width].astype(F32))
    small_ref[3:4, :] += column_sum(gproj_ref[:, 2 * width :].astype(F32))


def attention_backward(gmiddle, stream, proj, probs, vec, weight, block_pages, begin, end, before):
    rows, width = stream.shape
    _, _, slots, _ = probs.shape
    block = block_pages * slots
    first = begin // block_pages
    row_spec = lambda cols: pl.BlockSpec((block, cols), lambda i: (i + first, 0))
    whole = lambda array: pl.BlockSpec(array.shape, lambda i: (0, 0))
    before = [] if before is None else list(before)
    operands = [gmiddle, stream, proj, probs, vec, weight[0], weight[1]]
    return pl.pallas_call(
        attention_backward_kernel,
        grid=((end - begin) // block_pages,),
        in_specs=[
            row_spec(width),
            row_spec(width),
            row_spec(3 * width),
            pl.BlockSpec((block_pages, PAIRS, slots, 2 * slots), lambda i: (i + first, 0, 0, 0)),
            whole(vec),
            whole(weight[0]),
            whole(weight[1]),
        ]
        + [pl.BlockSpec(memory_space=pl.ANY)] * len(before),
        out_specs=[row_spec(width), row_spec(3 * width), pl.BlockSpec((8, width), lambda i: (0, 0))],
        out_shape=[
            jax.ShapeDtypeStruct((rows, width), F32),
            jax.ShapeDtypeStruct((rows, 3 * width), BF),
            jax.ShapeDtypeStruct((8, width), F32),
        ],
        scratch_shapes=[pltpu.VMEM((block, width), BF)],
        input_output_aliases={len(operands) + index: index for index in range(len(before))},
        compiler_params=pltpu.CompilerParams(vmem_limit_bytes=VMEM_LIMIT),
        cost_estimate=pl.CostEstimate(flops=15 * 10**9, bytes_accessed=20 * 10**6, transcendentals=0),
        name="attention_backward",
    )(*operands, *before)


def attention_weight_kernel(normed_ref, mixed_ref, gproj_ref, gmiddle_ref, grad_ref):
    gqkv = dot_tn(normed_ref[...], gproj_ref[...])
    gout = dot_tn(mixed_ref[...], gmiddle_ref[...].astype(BF))
    parts = grad_ref.shape[1]
    cut = gqkv.shape[1] // parts
    rest = gout.shape[1] // parts
    shape = (grad_ref.shape[0],) + grad_ref.shape[3:]
    for part in range(parts):
        qkv_part = gqkv[:, part * cut : (part + 1) * cut].astype(BF)
        out_part = gout[:, part * rest : (part + 1) * rest].astype(BF)
        grad_ref[:, part, 0] = jnp.concatenate([qkv_part, out_part], axis=1).reshape(shape)


def attention_weight(normed, mixed, gproj, gmiddle, stripes, parts):
    rows, width = normed.shape
    block = width // 2
    high = width // stripes
    return pl.pallas_call(
        attention_weight_kernel,
        grid=(2,),
        in_specs=[
            pl.BlockSpec((rows, block), lambda i: (0, i)),
            pl.BlockSpec((rows, block), lambda i: (0, i)),
            pl.BlockSpec((rows, 3 * width), lambda i: (0, 0)),
            pl.BlockSpec((rows, width), lambda i: (0, 0)),
        ],
        out_specs=pl.BlockSpec((stripes // 2, parts, 1, high, width), lambda i: (i, 0, 0, 0, 0)),
        out_shape=jax.ShapeDtypeStruct((stripes, parts, 1, high, width), BF),
        compiler_params=pltpu.CompilerParams(vmem_limit_bytes=VMEM_LIMIT),
        cost_estimate=pl.CostEstimate(flops=10 * 10**9, bytes_accessed=20 * 10**6, transcendentals=0),
        name="attention_weight",
    )(normed, mixed, gproj, gmiddle)


def relative_rows(source, target, me, depth):
    high = source.shape[0] // (2 * depth)
    for x in range(2):
        for z in range(depth):
            start = pl.multiple_of(jnp.bitwise_xor(me, 2 * z + x) * high, 16)
            target[x, z * high : (z + 1) * high, :] = source[pl.ds(start, high), :]


def ffn_weight_split_kernel(
    me_ref, nffn_ref, grad_ref, gupper_ref, active_ref, other_ref, own_ref, turned, nffn_t, grad_t
):
    step = pl.program_id(0)
    _, _, depth, high, width = own_ref.shape
    high = high // 2

    @pl.when(step == 0)
    def _():
        turned[...] = nffn_ref[...].T
        relative_rows(turned, nffn_t, me_ref[0], depth)
        turned[...] = grad_ref[...].astype(BF).T
        relative_rows(turned, grad_t, me_ref[0], depth)

    x, _ = plane(me_ref, step % 2, step // 2 % 2, 1 - step // 4)
    gup = dot_nn(nffn_t[x], gupper_ref[...]).astype(BF).reshape(depth, high, width)
    gdown = dot_nn(grad_t[x], active_ref[...]).astype(BF).reshape(depth, high, width)

    @pl.when(step < 4)
    def _():
        other_ref[0, 0, :, :high, :] = gup
        other_ref[0, 0, :, high:, :] = gdown

    @pl.when(step >= 4)
    def _():
        own_ref[0, 0, :, :high, :] = gup
        own_ref[0, 0, :, high:, :] = gdown


def ffn_weight_split(me, nffn, grad, gupper, active, depth):
    rows, width = nffn.shape
    piece = gupper.shape[1] // 4
    high = width // (2 * depth)

    def column(step, me):
        core = 1 - step // 4
        _, y = plane(me, step % 2, step // 2 % 2, core)
        return (0, jnp.bitwise_xor(me[1], 2 * y + core))

    def place(begin):
        def at(step, me):
            step = jnp.clip(step - begin, 0, 3)
            return (step // 2, step % 2, 0, 0, 0)

        return at

    whole = pl.BlockSpec((rows, width), lambda i, me: (0, 0))
    block = (1, 1, depth, 2 * high, piece)
    return pl.pallas_call(
        ffn_weight_split_kernel,
        grid_spec=pltpu.PrefetchScalarGridSpec(
            num_scalar_prefetch=1,
            grid=(8,),
            in_specs=[whole, whole, pl.BlockSpec((rows, piece), column), pl.BlockSpec((rows, piece), column)],
            out_specs=[pl.BlockSpec(block, place(0)), pl.BlockSpec(block, place(4))],
            scratch_shapes=[pltpu.VMEM((width, rows), BF)] + [pltpu.VMEM((2, width // 2, rows), BF)] * 2,
        ),
        out_shape=[jax.ShapeDtypeStruct((2, 2, depth, 2 * high, piece), BF)] * 2,
        compiler_params=pltpu.CompilerParams(vmem_limit_bytes=VMEM_LIMIT),
        cost_estimate=pl.CostEstimate(flops=15 * 10**9, bytes_accessed=30 * 10**6, transcendentals=0),
        name="ffn_weight",
    )(me, nffn, grad, gupper, active)


def attention_weight_split_kernel(me_ref, normed_ref, mixed_ref, gproj_ref, gmiddle_ref, *refs):
    other_ref, own_ref, turned, normed_t, mixed_t, joined, extra_s = refs[-7:]
    extra_refs = refs[:-7]
    x = pl.program_id(0)
    _, _, depth, rows, width = own_ref.shape
    high = width // (2 * depth)

    @pl.when(x == 0)
    def _():
        turned[...] = normed_ref[...].T
        relative_rows(turned, normed_t, me_ref[0], depth)
        turned[...] = mixed_ref[...].T
        relative_rows(turned, mixed_t, me_ref[0], depth)
        if extra_refs:
            share = width // 4
            extra_s[...] = jnp.zeros_like(extra_s)
            for index in range(2):
                one_ref, more_ref, two_ref, hidden_ref = extra_refs[4 * index : 4 * index + 4]
                sums = jnp.concatenate([one_ref[:4, :] + more_ref[:4, :], two_ref[:4, :]], axis=0)
                for part in range(4):
                    at = index * (width // 3)
                    extra_s[part, :8, at : at + share] = sums[:, part * share : (part + 1) * share]
                    extra_s[part, 8 + index : 9 + index, :] = hidden_ref[:, part * width : (part + 1) * width]

    gqkv = dot_nn(normed_t[x], gproj_ref[...])
    gout = dot_nn(mixed_t[x], gmiddle_ref[...].astype(BF))
    cut = gqkv.shape[1] // 4
    rest = gout.shape[1] // 4
    for part in range(4):
        qkv_part = gqkv[:, part * cut : (part + 1) * cut].astype(BF)
        out_part = gout[:, part * rest : (part + 1) * rest].astype(BF)
        joined[jnp.bitwise_xor(me_ref[1], part)] = jnp.concatenate([qkv_part, out_part], axis=1)
    for near in range(4):
        y, core = divmod(near, 2)
        first, second = plane(me_ref, x, y, core)
        target = own_ref if core == 0 else other_ref
        target[second, first, :, :high, :] = joined[near].reshape(depth, high, width)
        if extra_refs:
            extra = extra_s[jnp.bitwise_xor(me_ref[1], near)].astype(BF)
            target[second, first, :, high:, :] = jnp.broadcast_to(extra[None], (depth,) + extra.shape)


def attention_weight_split(me, normed, mixed, gproj, gmiddle, depth, extra=None):
    rows, width = normed.shape
    high = width // (2 * depth)
    whole = lambda array: pl.BlockSpec(array.shape, lambda i: (0,) * array.ndim)
    extras = [] if extra is None else list(extra)
    shape = (2, 2, depth, high + (0 if extra is None else 16), width)
    operands = [normed, mixed, gproj, gmiddle] + extras
    return pl.pallas_call(
        attention_weight_split_kernel,
        grid=(2,),
        in_specs=[pl.BlockSpec(memory_space=pltpu.SMEM)] + [whole(operand) for operand in operands],
        out_specs=[pl.BlockSpec(shape, lambda i: (0, 0, 0, 0, 0))] * 2,
        out_shape=[jax.ShapeDtypeStruct(shape, BF)] * 2,
        scratch_shapes=[
            pltpu.VMEM((width, rows), BF),
            pltpu.VMEM((2, width // 2, rows), BF),
            pltpu.VMEM((2, width // 2, rows), BF),
            pltpu.VMEM((4, width // 2, width), BF),
            pltpu.VMEM((4, 16, width), F32),
        ],
        compiler_params=pltpu.CompilerParams(vmem_limit_bytes=VMEM_LIMIT),
        cost_estimate=pl.CostEstimate(flops=10 * 10**9, bytes_accessed=20 * 10**6, transcendentals=0),
        name="attention_weight",
    )(me, *operands)


def pair_bias(slot_kind, slot_valid, across):
    same_kind = slot_kind[:, :, None] == slot_kind[:, None, :]
    partner = jnp.logical_not(same_kind) if across else same_kind
    allowed = jnp.logical_and(partner, slot_valid[:, None, :] > 0)
    return jnp.where(allowed, 0.0, -1e30).astype(F32)


def ordered_vectors(small_one, small_two):
    picked = (small_one, 0), (small_two, 0), (small_one, 1), (small_one, 2)
    picked += (small_one, 3), (small_two, 3), (small_two, 1), (small_two, 2)
    return jnp.stack([sums[row] for sums, row in picked])


def adam_step(master, grad, moment_one, moment_two, factor, decayed):
    clipped = grad * factor
    first_new = beta_one * moment_one + (1.0 - beta_one) * clipped
    second_new = beta_two * moment_two + (1.0 - beta_two) * clipped * clipped
    change = first_new / bias_one / (jnp.sqrt(second_new / bias_two) + epsilon)
    if decayed:
        change = change + weight_decay * master
    return (-learn_rate * change, first_new, second_new)


def gather_rows(pieces, sizes):
    kinds, high, width = pieces.shape
    rows = lax.all_gather(pieces.reshape(-1, width), ("dp", "tensor"), axis=0, tiled=False)
    if high % 16 == 0:
        return [(("rows", kind * high), [rows]) for kind in range(kinds)]
    split = rows.reshape(sizes["dp"], sizes["tensor"], kinds, high, width)
    return [(("whole",), [jnp.swapaxes(split[:, :, kind], 0, 1).reshape(-1, width, width)]) for kind in range(kinds)]


def scatter_rows(grad, sizes):
    stripes, parts, kinds, high, width = grad.shape
    inner = sizes["dp"] // stripes
    if inner > 1:
        grad = jnp.moveaxis(grad.reshape(stripes, parts, kinds, inner, high // inner, width), 3, 1)
    mine = lax.psum_scatter(grad.reshape(-1, width), ("dp", "tensor"), scatter_dimension=0, tiled=True)
    return mine.reshape(kinds, -1, width).astype(F32)


class Exchange:
    def __init__(self, sizes):
        self.sizes = sizes
        self.depth = sizes["dp"] // 2

    def swap(self, value, partner):
        dp, tensor = self.sizes["dp"], self.sizes["tensor"]
        pairs = []
        for i in range(dp):
            for j in range(tensor):
                far_i, far_j = partner(i, j)
                pairs.append((i * tensor + j, far_i * tensor + far_j))
        return lax.ppermute(value, ("dp", "tensor"), pairs)

    def part(self, bits, value):
        return self.swap(value, lambda i, j: (i, j ^ bits))

    def core(self, value):
        return self.part(1, value)

    def x(self, value):
        return self.swap(value, lambda i, j: (i ^ 1, j))

    def y(self, value):
        return self.part(2, value)

    def diagonal(self, value):
        return self.swap(value, lambda i, j: (i ^ 1, j ^ 2))

    def first(self, value):
        return self.swap(value, lambda i, j: (i, j ^ 2) if j & 1 else (i ^ 1, j))

    def second(self, value):
        return self.swap(value, lambda i, j: (i ^ 1, j) if j & 1 else (i, j ^ 2))

    def z(self, distance, value):
        return self.swap(value, lambda i, j: (i ^ (2 * distance), j))

    def z_sends(self, values):
        return [(functools.partial(self.z, distance), values[distance]) for distance in range(1, self.depth)]

    def gather_z(self, piece):
        groups = [[2 * z + x for z in range(self.depth)] for x in range(2)]
        return lax.all_gather(piece, "dp", axis=0, tiled=False, axis_index_groups=groups)

    def total(self, value):
        value = value + self.core(value)
        value = value + self.y(value)
        value = value + self.x(value)
        bit = 1
        while bit < self.depth:
            value = value + self.z(bit, value)
            bit *= 2
        return value


def tie(values, after):
    return lax.optimization_barrier((values, after))[0]


class Spread:
    def __init__(self, exchange, quad, fixed):
        self.exchange, self.quad, self.fixed = exchange, quad, fixed

    def go_first(self):
        return [(self.exchange.first, self.quad)]

    def go_second(self, came):
        self.pair = jnp.stack([self.quad, came[0]])
        return [(self.exchange.second, self.pair), (self.exchange.core, self.pair)]

    def go_core(self, came):
        self.two, self.far_pair = came
        return [(self.exchange.core, self.two)]

    def weight(self, came, offset=0):
        positions = [[(0, second, core), (1, second, core)] for core in range(2) for second in range(2)]
        arrays = [self.pair, self.two, self.far_pair, came[0]]
        return (("near", offset, positions, self.fixed), arrays)


class Reduce:
    def __init__(self, exchange, other, own):
        self.exchange, self.other, self.own = exchange, other, own

    def wide(self, value):
        return value.astype(F32)

    def go_core(self):
        return [(self.exchange.core, self.other)]

    def go_second(self, came):
        self.came = came[0]
        value = (self.wide(self.own[1]) + self.wide(self.came[1])).astype(BF)
        return [(self.exchange.second, value)]

    def go_first(self, came):
        self.beside = came[0]
        value = self.wide(self.own[0, 1]) + self.wide(self.came[0, 1]) + self.wide(self.beside[1])
        return [(self.exchange.first, value.astype(BF))]

    def depths(self, came):
        ahead = came[0]
        return (
            self.wide(self.own[0, 0]) + self.wide(self.came[0, 0]) + self.wide(self.beside[0]) + self.wide(ahead)
        )


class Lane:
    def __init__(self):
        self.last = None

    def after_last(self, values):
        return values if self.last is None else tie(values, self.last)

    def step(self, sends, kernel=None, arrays=()):
        values = [value for _, value in sends]
        values, arrays = self.after_last((values, list(arrays)))
        came = [move(value) for (move, _), value in zip(sends, values)]
        results = [] if kernel is None else list(kernel(*arrays))
        came, results = lax.optimization_barrier((came, results))
        self.last = results[-1] if results else came[-1]
        return came, results


def shards(
    sizes,
    tokens, out_grad, slot_kind, slot_valid,
    qkv_weight, qkv_first, qkv_second,
    out_weight, out_first, out_second,
    up_weight, up_first, up_second,
    down_weight, down_first, down_second,
    gain_weight, gain_first, gain_second,
    bias_weight, bias_first, bias_second,
    hidden_weight, hidden_first, hidden_second,
):
    parts = sizes["tensor"]
    width = tokens.shape[1]
    cut = qkv_weight.shape[2]
    high = qkv_weight.shape[1]
    split = parts == 4 and high % 32 == 0 and sizes["dp"] in (4, 8, 16)
    exchange = Exchange(sizes)
    stripes = sizes["dp"] if high % 16 == 0 else 2
    me = jnp.stack([lax.axis_index("dp"), lax.axis_index("tensor")]).astype(jnp.int32)
    attn_pieces = jnp.concatenate([qkv_weight.astype(BF), out_weight.astype(BF)], axis=2)
    up_pieces = up_weight.astype(BF)
    down_pieces = jnp.swapaxes(down_weight.astype(BF), 1, 2)
    pages = slot_kind.shape[0]
    block_pages = 2 if pages % 2 == 0 else 1
    block = block_pages * slot_kind.shape[1]
    middle_page = block_pages
    masks = [pair_bias(slot_kind, slot_valid, index == 0) for index in range(2)]
    lane = Lane()
    gathered = lambda index: gather_rows(
        jnp.stack([attn_pieces[index], up_pieces[index], down_pieces[index]]), sizes
    )
    small = hidden = None
    saved = [None, None]

    def attention_forward_of(index, weight):
        return lambda stream: attention_forward(
            me, stream, masks[index], small[index], weight, block_pages, parts
        )

    def ffn_forward_of(index, up_w, down_w):
        return lambda nffn, middle: ffn_forward(
            me, nffn, middle, small[index], hidden[index : index + 1], up_w, down_w, block, parts
        )

    def ffn_backward_of(index):
        kept = saved[index]
        return lambda grad: ffn_backward(
            me, grad, kept["slope"], kept["middle"], small[index], kept["up_w"], kept["down_w"], block, parts
        )

    def ffn_weight_of(index, grad):
        kept = saved[index]
        if split:
            return lambda gupper: ffn_weight_split(
                me, kept["nffn"], grad, gupper, kept["active"], exchange.depth
            )
        return lambda gupper: (ffn_weight(kept["nffn"], grad, gupper, kept["active"], stripes, parts),)

    def attention_backward_of(index, begin, end, before=None):
        kept = saved[index]
        return lambda gmiddle: attention_backward(
            gmiddle, kept["stream"], kept["proj"], kept["probs"], small[index], kept["weight"],
            block_pages, begin, end, before,
        )

    def attention_weight_of(index, gmiddle, extra=None):
        kept = saved[index]
        if split:
            return lambda gproj: attention_weight_split(
                me, kept["normed"], kept["mixed"], gproj, gmiddle, exchange.depth, extra
            )
        return lambda gproj: (attention_weight(kept["normed"], kept["mixed"], gproj, gmiddle, stripes, parts),)

    def keep(index, stream, attention, ffn, up_w, down_w):
        middle, nffn, normed, proj, probs, mixed, qkv_w, out_w = attention
        saved[index] = dict(
            stream=stream, middle=middle, nffn=nffn, normed=normed, proj=proj, probs=probs, mixed=mixed,
            weight=(qkv_w, out_w), active=ffn[1], slope=ffn[2], up_w=up_w, down_w=down_w,
        )

    if split:
        depth = exchange.depth
        late = exchange.gather_z(jnp.concatenate([attn_pieces[1], up_pieces[1], down_pieces[1]], axis=0))
        own_small = jnp.concatenate(
            [gain_weight, bias_weight, hidden_weight.reshape(2, -1, gain_weight.shape[2])], axis=1
        )
        own_small = lax.reduce_precision(own_small, 8, 7)
        small_sends = [(functools.partial(exchange.part, bits), own_small) for bits in range(1, 4)]
        came, _ = lane.step(exchange.z_sends([attn_pieces[0]] * depth) + small_sends)
        attn_zero = Spread(exchange, jnp.stack([attn_pieces[0]] + came[: depth - 1]), False)
        mine = lax.axis_index("tensor")
        every = jnp.zeros((4,) + own_small.shape, F32)
        for bits, value in enumerate([own_small] + came[depth - 1 :]):
            every = lax.dynamic_update_slice_in_dim(every, value[None], jnp.bitwise_xor(mine, bits), 0)
        small = jnp.moveaxis(every[:, :, :8], 0, 2).reshape(2, 8, width)
        hidden = jnp.moveaxis(every[:, :, 8:], 0, 1).reshape(2, -1)
        ffn_piece = jnp.concatenate([up_pieces[0], down_pieces[0]], axis=0)
        ffn_sends = exchange.z_sends([ffn_piece] * depth)
        middle_at = depth // 2 - 1
        came, _ = lane.step(attn_zero.go_first() + ffn_sends[middle_at : middle_at + 1])
        ffn_came = came[1:]
        ffn_sends = ffn_sends[:middle_at] + ffn_sends[middle_at + 1 :]
        came, _ = lane.step(attn_zero.go_second(came[:1]) + ffn_sends)
        others = came[2:]
        others.insert(middle_at, ffn_came[0])
        ffn_zero = Spread(exchange, jnp.stack([ffn_piece] + others), False)
        came, _ = lane.step(attn_zero.go_core(came[:2]) + ffn_zero.go_first())
        attn_w = attn_zero.weight(came[:1])
        came, attention = lane.step(ffn_zero.go_second(came[1:]), attention_forward_of(0, attn_w), [tokens])
        attn_one = Spread(exchange, late[:, :high], True)
        ffn_one = Spread(exchange, late[:, high:], True)
        came, _ = lane.step(ffn_zero.go_core(came) + attn_one.go_first())
        up_w, down_w = ffn_zero.weight(came[:1]), ffn_zero.weight(came[:1], high)
        came, ffn = lane.step(
            attn_one.go_second(came[1:]) + ffn_one.go_first(), ffn_forward_of(0, up_w, down_w), attention[1::-1]
        )
        keep(0, tokens, attention, ffn, up_w, down_w)
        stream = ffn[0]
        ffn_came = came[2:]
        came, _ = lane.step(attn_one.go_core(came[:2]))
        attn_w = attn_one.weight(came)
        came, attention = lane.step(ffn_one.go_second(ffn_came), attention_forward_of(1, attn_w), [stream])
        came, _ = lane.step(ffn_one.go_core(came))
        up_w, down_w = ffn_one.weight(came), ffn_one.weight(came, high)
        _, ffn = lane.step([], ffn_forward_of(1, up_w, down_w), attention[1::-1])
        keep(1, stream, attention, ffn, up_w, down_w)
        block_output = ffn[0]

        _, (gupper, gmiddle, small_two, hidden_one) = lane.step([], ffn_backward_of(1), [out_grad])
        _, grads = lane.step([], ffn_weight_of(1, out_grad), [gupper])
        ffn_one = Reduce(exchange, *grads)
        came, before = lane.step(ffn_one.go_core(), attention_backward_of(1, 0, middle_page), [gmiddle])
        came, after = lane.step(
            ffn_one.go_second(came), attention_backward_of(1, middle_page, pages, before[:2]), [gmiddle]
        )
        grad, gproj = after[:2]
        sums_one = (before[2], after[2], small_two, hidden_one)
        came, grads = lane.step(ffn_one.go_first(came), attention_weight_of(1, gmiddle), [gproj])
        layers = ffn_one.depths(came)
        attn_one = Reduce(exchange, *grads)
        came, results = lane.step(attn_one.go_core(), ffn_backward_of(0), [grad])
        gupper, gmiddle, small_two, hidden_zero = results
        came, grads = lane.step(attn_one.go_second(came), ffn_weight_of(0, grad), [gupper])
        ffn_zero = Reduce(exchange, *grads)
        came, before = lane.step(
            ffn_zero.go_core() + attn_one.go_first(came), attention_backward_of(0, 0, middle_page), [gmiddle]
        )
        layers = jnp.concatenate([attn_one.depths(came[1:]), layers], axis=1)
        late_sends = exchange.z_sends([layers[z].astype(BF) for z in range(depth)])
        late_sends = late_sends[middle_at : middle_at + 1] + late_sends[:middle_at] + late_sends[middle_at + 1 :]
        came, after = lane.step(
            ffn_zero.go_second(came[:1]) + late_sends[:1],
            attention_backward_of(0, middle_page, pages, before[:2]),
            [gmiddle],
        )
        late_came = came[1:]
        input_grad, gproj = after[:2]
        came, grads = lane.step(
            ffn_zero.go_first(came[:1]) + late_sends[1:],
            attention_weight_of(0, gmiddle, (before[2], after[2], small_two, hidden_zero) + sums_one),
            [gproj],
        )
        total = layers[0] + sum(value.astype(F32) for value in late_came + came[1:])
        grad_attn, grad_up, grad_down = ([None, total[at : at + high]] for at in (0, high, 2 * high))
        layers = ffn_zero.depths(came[:1])
        ffn_sends = exchange.z_sends([layers[z].astype(BF) for z in range(depth)])
        ffn_sends = ffn_sends[middle_at : middle_at + 1] + ffn_sends[:middle_at] + ffn_sends[middle_at + 1 :]
        attn_zero = Reduce(exchange, *grads)
        came, _ = lane.step(attn_zero.go_core())
        came, _ = lane.step(attn_zero.go_second(came) + ffn_sends[:1])
        ffn_came = came[1:]
        came, _ = lane.step(attn_zero.go_first(came[:1]) + ffn_sends[1:])
        total = layers[0] + sum(value.astype(F32) for value in ffn_came + came[1:])
        grad_up[0], grad_down[0] = total[:high], total[high:]
        layers = attn_zero.depths(came[:1])
        came, _ = lane.step(exchange.z_sends([layers[z].astype(BF) for z in range(depth)]))
        total = layers[0] + sum(value.astype(F32) for value in came)
        grad_attn[0] = total[:high]
        share = width // parts
        vectors = []
        for at in (0, width // 3):
            sums = total[high : high + 8, at : at + share]
            vectors.append(ordered_vectors(sums[:4], sums[4:]))
        vectors = jnp.stack(vectors)
        grad_hidden = total[high + 8 : high + 10]
    else:
        small = jnp.concatenate([gain_weight, bias_weight], axis=1).astype(BF)
        small = lax.all_gather(small, "tensor", axis=2, tiled=True).astype(F32)
        hidden = lax.all_gather(hidden_weight.astype(BF), "tensor", axis=1, tiled=True).astype(F32)
        stream = tokens
        for index in range(2):
            attn_w, up_w, down_w = gathered(index)
            attention = attention_forward_of(index, attn_w)(stream)
            ffn = ffn_forward_of(index, up_w, down_w)(*attention[1::-1])
            keep(index, stream, attention, ffn, up_w, down_w)
            stream = ffn[0]
        block_output = stream
        grad = out_grad
        grad_attn, grad_up, grad_down, vectors, grad_hidden = ([None, None] for _ in range(5))
        for index in (1, 0):
            gupper, gmiddle, small_two, grad_hidden[index] = ffn_backward_of(index)(grad)
            (gffn,) = ffn_weight_of(index, grad)(gupper)
            grad_up[index], grad_down[index] = scatter_rows(gffn, sizes)
            grad, gproj, small_one = attention_backward_of(index, 0, pages)(gmiddle)
            (grad_attn[index],) = scatter_rows(attention_weight_of(index, gmiddle)(gproj)[0], sizes)
            vectors[index] = ordered_vectors(small_one, small_two)
        input_grad = grad
        vectors, grad_hidden = lax.psum((jnp.stack(vectors), jnp.concatenate(grad_hidden, axis=0)), ("dp", "tensor"))
        at = lax.axis_index("tensor")
        slice_of = lambda whole: lax.dynamic_slice_in_dim(
            whole, at * (whole.shape[-1] // parts), whole.shape[-1] // parts, whole.ndim - 1
        )
        vectors, grad_hidden = slice_of(vectors), slice_of(grad_hidden)
    grad_gain, grad_bias = vectors[:, :2], vectors[:, 2:]
    grad_attn, grad_up, grad_down = jnp.stack(grad_attn), jnp.stack(grad_up), jnp.stack(grad_down)
    shared_squares = jnp.sum(vectors * vectors) + jnp.sum(grad_hidden * grad_hidden)
    local_squares = (
        jnp.sum(grad_attn * grad_attn) + jnp.sum(grad_up * grad_up) + jnp.sum(grad_down * grad_down)
    ) + jnp.where(lax.axis_index("dp") == 0, shared_squares, 0.0)
    grad_down = jnp.swapaxes(grad_down, 1, 2)
    if split:
        total_squares = exchange.total(local_squares.reshape(1, 1))[0, 0]
    else:
        total_squares = lax.psum(local_squares, ("dp", "tensor"))
    grad_norm = jnp.sqrt(total_squares)
    factor = clip_norm / jnp.maximum(grad_norm, clip_norm)
    masters = (qkv_weight, out_weight, up_weight, down_weight, gain_weight, bias_weight, hidden_weight)
    firsts = (qkv_first, out_first, up_first, down_first, gain_first, bias_first, hidden_first)
    seconds = (qkv_second, out_second, up_second, down_second, gain_second, bias_second, hidden_second)
    gradients = (
        grad_attn[:, :, :cut], grad_attn[:, :, cut:], grad_up, grad_down, grad_gain, grad_bias, grad_hidden,
    )
    results = [block_output, input_grad, grad_norm]
    for member in range(7):
        update, first_new, second_new = adam_step(
            masters[member], gradients[member], firsts[member], seconds[member], factor, member < 4
        )
        results = results + [gradients[member], update, first_new, second_new]
    return tuple(results)


def solution(mesh):
    rows = P(("dp", "tensor"), None)
    matrix = P(None, "dp", "tensor")
    turned = P(None, "tensor", "dp")
    vectors = P(None, None, "tensor")
    hidden = P(None, "tensor")
    return jax.shard_map(
        functools.partial(shards, dict(mesh.shape)),
        mesh=mesh,
        in_specs=(rows,) * 4 + (matrix,) * 9 + (turned,) * 3 + (vectors,) * 6 + (hidden,) * 3,
        out_specs=(rows, rows, P()) + (matrix,) * 12 + (turned,) * 4 + (vectors,) * 8 + (hidden,) * 4,
        check_vma=False,
    )
```

```python
import functools

import jax
import jax.numpy as jnp
from jax import lax
from jax.experimental import pallas as pl
from jax.experimental.pallas import tpu as pltpu
from jax.sharding import PartitionSpec as P

HEADS = 12
PAIRS = HEADS // 2

beta_one = 0.9
beta_two = 0.99
learn_rate = 0.01
weight_decay = 0.01
epsilon = 1e-08
clip_norm = 1.0
bias_one = 1.0 - beta_one**10
bias_two = 1.0 - beta_two**10

BF = jnp.bfloat16
F32 = jnp.float32
VMEM_LIMIT = 56 * 1024 * 1024


def dot_nn(a, b):
    return lax.dot_general(a, b, (((1,), (0,)), ((), ())), preferred_element_type=F32)


def dot_nt(a, b):
    return lax.dot_general(a, b, (((1,), (1,)), ((), ())), preferred_element_type=F32)


def dot_tn(a, b):
    return lax.dot_general(a, b, (((0,), (0,)), ((), ())), preferred_element_type=F32)


def normalize(stream):
    average = jnp.mean(stream, axis=-1, keepdims=True)
    centered = stream - average
    spread = jnp.mean(centered * centered, axis=-1, keepdims=True)
    root = lax.rsqrt(spread + 1e-05)
    return centered * root, root


def norm_backward(grad, unit, root, gain):
    scaled = grad * gain
    first = jnp.mean(scaled, axis=-1, keepdims=True)
    second = jnp.mean(scaled * unit, axis=-1, keepdims=True)
    return root * (scaled - first - unit * second)


def column_sum(value):
    return jnp.sum(value, axis=0, keepdims=True)


def split_heads(pair):
    lane = lax.broadcasted_iota(jnp.int32, pair.shape, 1)
    zero = jnp.zeros_like(pair)
    half = pair.shape[1] // 2
    return jnp.concatenate([jnp.where(lane < half, pair, zero), jnp.where(lane >= half, pair, zero)], axis=0)


def plane(me_ref, first, second, core):
    turned = jnp.bitwise_xor(jnp.bitwise_and(me_ref[1], 1), core) == 1
    return jnp.where(turned, second, first), jnp.where(turned, first, second)


def weight_copies(plan, refs, me_ref, full, sems):
    copies = []

    def add(source, part, rows):
        copies.append(pltpu.make_async_copy(source, full.at[part, rows, :], sems.at[part]))

    parts, width, _ = full.shape
    if plan[0] == "whole":
        for part in range(parts):
            add(refs[0].at[part], part, pl.ds(0, width))
    elif plan[0] == "rows":
        high = width * parts // refs[0].shape[0]
        for index in range(refs[0].shape[0]):
            stripe, part = divmod(index, parts)
            add(refs[0].at[index, pl.ds(plan[1], high), :], part, pl.ds(stripe * high, high))
    else:
        for ref, positions in zip(refs, plan[2]):
            depth = ref.shape[1]
            high = width // (2 * depth)
            for place, (first, second, core) in enumerate(positions):
                x, y = plane(me_ref, first, second, core)
                part = jnp.bitwise_xor(me_ref[1], 2 * y + core)
                if plan[3]:
                    side = jnp.bitwise_xor(jnp.bitwise_and(me_ref[0], 1), x)
                    stripes = full.reshape(parts, depth, 2, high, width).at[part, :, side]
                    source = ref.at[place, :, pl.ds(plan[1], high), :]
                    copies.append(pltpu.make_async_copy(source, stripes, sems.at[part]))
                    continue
                for z in range(depth):
                    start = pl.multiple_of(jnp.bitwise_xor(me_ref[0], 2 * z + x) * high, 16)
                    add(ref.at[place, z, pl.ds(plan[1], high), :], part, pl.ds(start, high))
    return copies


def start_weights(groups):
    for copy in [copy for group in groups for copy in weight_copies(*group)]:
        copy.start()


def wait_weight(full, sems, part):
    pltpu.make_async_copy(full.at[part], full.at[part], sems.at[part]).wait()


def part_order(me_ref, plan, parts):
    if plan[0] != "near":
        return list(range(parts))
    return [jnp.bitwise_xor(me_ref[1], near) for near in (0, 2, 1, 3)]


def split_attention(raw, qkv_s, out_s):
    parts = raw.shape[0]
    cut = qkv_s.shape[1] // parts
    step = 96

    def relay(index, _):
        rows = pl.ds(pl.multiple_of(index * step, step), step)
        pieces = [raw[part, rows, :] for part in range(parts)]
        qkv_s[rows, :] = jnp.concatenate([piece[:, :cut] for piece in pieces], axis=1)
        out_s[rows, :] = jnp.concatenate([piece[:, cut:] for piece in pieces], axis=1)
        return 0

    lax.fori_loop(0, raw.shape[1] // step, relay, 0)


def attention_forward_kernel(plan, me_ref, stream_ref, mask_ref, vec_ref, *refs):
    weight_refs = refs[:-10]
    middle_ref, nffn_ref, normed_ref, proj_ref, probs_ref, mixed_ref, qkv_s, out_s, raw, sems = refs[-10:]

    @pl.when(pl.program_id(0) == 0)
    def _():
        start_weights([(plan, weight_refs, me_ref, raw, sems)])
        for part in range(raw.shape[0]):
            wait_weight(raw, sems, part)
        split_attention(raw, qkv_s, out_s)

    width = stream_ref.shape[1]
    slots = mask_ref.shape[1]
    scale = (width // HEADS) ** (-0.5)
    stream = stream_ref[...].astype(F32)
    unit, _ = normalize(stream)
    normed = (unit * vec_ref[0:1, :] + vec_ref[2:3, :]).astype(BF)
    normed_ref[...] = normed
    projected = dot_nn(normed, qkv_s[...])
    proj_ref[:, :width] = (projected[:, :width] + vec_ref[3:4, :]).astype(BF)
    proj_ref[:, width : 2 * width] = projected[:, width : 2 * width].astype(BF)
    proj_ref[:, 2 * width :] = (projected[:, 2 * width :] + vec_ref[4:5, :]).astype(BF)
    lanes = 2 * (width // HEADS)
    for page in range(mask_ref.shape[0]):
        rows = slice(page * slots, (page + 1) * slots)
        bias = mask_ref[page]
        for pair in range(PAIRS):
            at = pair * lanes
            queries = proj_ref[rows, at : at + lanes] * jnp.asarray(scale, BF)
            keys_in = split_heads(proj_ref[rows, width + at : width + at + lanes])
            values = split_heads(proj_ref[rows, 2 * width + at : 2 * width + at + lanes])
            scores = dot_nt(queries, keys_in)
            soft = []
            for head in range(2):
                masked = scores[:, head * slots : (head + 1) * slots] + bias
                peak = jnp.max(masked, axis=-1, keepdims=True)
                exponent = jnp.exp(masked - peak)
                total = jnp.sum(exponent, axis=-1, keepdims=True)
                soft.append((exponent * (1.0 / total)).astype(BF))
            probs = jnp.concatenate(soft, axis=1)
            probs_ref[page, pair] = probs
            mixed_ref[rows, at : at + lanes] = dot_nn(probs, values).astype(BF)
    middle = stream + dot_nn(mixed_ref[...], out_s[...]) + vec_ref[5:6, :]
    middle_ref[...] = middle
    unit, _ = normalize(middle)
    nffn_ref[...] = (unit * vec_ref[1:2, :] + vec_ref[6:7, :]).astype(BF)


def attention_forward(me, stream, mask, vec, weight, block_pages, parts):
    plan, arrays = weight
    rows, width = stream.shape
    pages, slots, _ = mask.shape
    block = block_pages * slots
    row_spec = lambda cols: pl.BlockSpec((block, cols), lambda i: (i, 0))
    return pl.pallas_call(
        functools.partial(attention_forward_kernel, plan),
        grid=(pages // block_pages,),
        in_specs=[
            pl.BlockSpec(memory_space=pltpu.SMEM),
            row_spec(width),
            pl.BlockSpec((block_pages, slots, slots), lambda i: (i, 0, 0)),
            pl.BlockSpec(vec.shape, lambda i: (0, 0)),
        ]
        + [pl.BlockSpec(memory_space=pl.ANY)] * len(arrays),
        out_specs=[
            row_spec(width),
            row_spec(width),
            row_spec(width),
            row_spec(3 * width),
            pl.BlockSpec((block_pages, PAIRS, slots, 2 * slots), lambda i: (i, 0, 0, 0)),
            row_spec(width),
            pl.BlockSpec((width, 3 * width), lambda i: (0, 0)),
            pl.BlockSpec((width, width), lambda i: (0, 0)),
        ],
        out_shape=[
            jax.ShapeDtypeStruct((rows, width), F32),
            jax.ShapeDtypeStruct((rows, width), BF),
            jax.ShapeDtypeStruct((rows, width), BF),
            jax.ShapeDtypeStruct((rows, 3 * width), BF),
            jax.ShapeDtypeStruct((pages, PAIRS, slots, 2 * slots), BF),
            jax.ShapeDtypeStruct((rows, width), BF),
            jax.ShapeDtypeStruct((width, 3 * width), BF),
            jax.ShapeDtypeStruct((width, width), BF),
        ],
        scratch_shapes=[
            pltpu.VMEM((parts, width, width), BF),
            pltpu.SemaphoreType.DMA((parts,)),
        ],
        compiler_params=pltpu.CompilerParams(vmem_limit_bytes=VMEM_LIMIT),
        cost_estimate=pl.CostEstimate(flops=20 * 10**9, bytes_accessed=30 * 10**6, transcendentals=0),
        name="attention_forward",
    )(me, stream, mask, vec, *arrays)


def ffn_forward_kernel(plans, me_ref, nffn_ref, middle_ref, vec_ref, hidden_ref, *refs):
    result_ref, active_ref, slope_ref, up_ref, down_ref, up_s, down_s, up_sems, down_sems = refs[-9:]
    up_refs = refs[: (len(refs) - 9) // 2]
    down_refs = refs[len(up_refs) : -9]
    kept = [pltpu.make_async_copy(up_s, up_ref, up_sems.at[0]), pltpu.make_async_copy(down_s, down_ref, down_sems.at[0])]

    first = pl.program_id(0) == 0
    parts, _, chunk = up_s.shape
    curve = 0.7978845608028654

    @pl.when(first)
    def _():
        start_weights([(plans[0], up_refs, me_ref, up_s, up_sems), (plans[1], down_refs, me_ref, down_s, down_sems)])

    def body(wait):
        nffn = nffn_ref[...]
        total = middle_ref[...] + vec_ref[7:8, :]
        for part in part_order(me_ref, plans[0], parts):
            cols = pl.ds(pl.multiple_of(part * chunk, chunk), chunk)
            if wait:
                wait_weight(up_s, up_sems, part)
            upper = dot_nn(nffn, up_s[part]) + hidden_ref[:, cols]
            square = upper * upper
            angle = jnp.tanh(upper * (curve + (curve * 0.044715) * square))
            half = 0.5 * upper
            lift = 1.0 + angle
            active = (half * lift).astype(BF)
            slope = 0.5 * lift + half * (1.0 - angle * angle) * (curve + (3.0 * curve * 0.044715) * square)
            active_ref[:, cols] = active
            slope_ref[:, cols] = slope.astype(BF)
            if wait:
                wait_weight(down_s, down_sems, part)
            total = total + dot_nt(active, down_s[part])
        result_ref[...] = total
        if wait:
            for copy in kept:
                copy.start()

    pl.when(first)(functools.partial(body, True))
    pl.when(jnp.logical_not(first))(functools.partial(body, False))

    @pl.when(pl.program_id(0) == pl.num_programs(0) - 1)
    def _():
        for copy in kept:
            copy.wait()


def ffn_forward(me, nffn, middle, vec, hidden, up_w, down_w, block, parts):
    rows, width = nffn.shape
    ffn = hidden.shape[1]
    arrays = up_w[1] + down_w[1]
    row_spec = lambda cols: pl.BlockSpec((block, cols), lambda i: (i, 0))
    return pl.pallas_call(
        functools.partial(ffn_forward_kernel, (up_w[0], down_w[0])),
        grid=(rows // block,),
        in_specs=[
            pl.BlockSpec(memory_space=pltpu.SMEM),
            row_spec(width),
            row_spec(width),
            pl.BlockSpec(vec.shape, lambda i: (0, 0)),
            pl.BlockSpec(hidden.shape, lambda i: (0, 0)),
        ]
        + [pl.BlockSpec(memory_space=pl.ANY)] * len(arrays),
        out_specs=[row_spec(width), row_spec(ffn), row_spec(ffn)] + [pl.BlockSpec(memory_space=pl.ANY)] * 2,
        out_shape=[
            jax.ShapeDtypeStruct((rows, width), F32),
            jax.ShapeDtypeStruct((rows, ffn), BF),
            jax.ShapeDtypeStruct((rows, ffn), BF),
        ]
        + [jax.ShapeDtypeStruct((parts, width, ffn // parts), BF)] * 2,
        scratch_shapes=[
            pltpu.VMEM((parts, width, ffn // parts), BF),
            pltpu.VMEM((parts, width, ffn // parts), BF),
            pltpu.SemaphoreType.DMA((parts,)),
            pltpu.SemaphoreType.DMA((parts,)),
        ],
        compiler_params=pltpu.CompilerParams(vmem_limit_bytes=VMEM_LIMIT),
        cost_estimate=pl.CostEstimate(flops=15 * 10**9, bytes_accessed=30 * 10**6, transcendentals=0),
        name="ffn_forward",
    )(me, nffn, middle, vec, hidden, *arrays)


def ffn_backward_kernel(plans, me_ref, grad_ref, slope_ref, middle_ref, vec_ref, *refs):
    gupper_ref, gmiddle_ref, small_ref, ghidden_ref, up_s, down_s, up_sems, down_sems = refs[-8:]
    up_refs = refs[: (len(refs) - 8) // 2]
    down_refs = refs[len(up_refs) : -8]

    first = pl.program_id(0) == 0
    parts, _, chunk = up_s.shape

    @pl.when(first)
    def _():
        start_weights([(plans[1], down_refs, me_ref, down_s, down_sems), (plans[0], up_refs, me_ref, up_s, up_sems)])
        small_ref[...] = jnp.zeros_like(small_ref)
        ghidden_ref[...] = jnp.zeros_like(ghidden_ref)

    def body(wait):
        grad = grad_ref[...].astype(F32)
        lower = grad.astype(BF)
        gnormed = jnp.zeros(grad.shape, F32)
        for part in part_order(me_ref, plans[0], parts):
            cols = pl.ds(pl.multiple_of(part * chunk, chunk), chunk)
            if wait:
                wait_weight(down_s, down_sems, part)
            gupper = (dot_nn(lower, down_s[part]) * slope_ref[:, cols].astype(F32)).astype(BF)
            gupper_ref[:, cols] = gupper
            ghidden_ref[:, cols] += column_sum(gupper.astype(F32))
            if wait:
                wait_weight(up_s, up_sems, part)
            gnormed = gnormed + dot_nt(gupper, up_s[part])
        unit, root = normalize(middle_ref[...])
        gmiddle = grad + norm_backward(gnormed, unit, root, vec_ref[1:2, :])
        gmiddle_ref[...] = gmiddle
        small_ref[0:1, :] += column_sum(gnormed * unit)
        small_ref[1:2, :] += column_sum(gnormed)
        small_ref[2:3, :] += column_sum(lower.astype(F32))
        small_ref[3:4, :] += column_sum(gmiddle.astype(BF).astype(F32))

    pl.when(first)(functools.partial(body, True))
    pl.when(jnp.logical_not(first))(functools.partial(body, False))


def ffn_backward(me, grad, slope, middle, vec, up_w, down_w, block, parts):
    rows, width = grad.shape
    ffn = slope.shape[1]
    arrays = up_w[1] + down_w[1]
    row_spec = lambda cols: pl.BlockSpec((block, cols), lambda i: (i, 0))
    return pl.pallas_call(
        functools.partial(ffn_backward_kernel, (up_w[0], down_w[0])),
        grid=(rows // block,),
        in_specs=[
            pl.BlockSpec(memory_space=pltpu.SMEM),
            row_spec(width),
            row_spec(ffn),
            row_spec(width),
            pl.BlockSpec(vec.shape, lambda i: (0, 0)),
        ]
        + [pl.BlockSpec(memory_space=pl.ANY)] * len(arrays),
        out_specs=[
            row_spec(ffn),
            row_spec(width),
            pl.BlockSpec((8, width), lambda i: (0, 0)),
            pl.BlockSpec((1, ffn), lambda i: (0, 0)),
        ],
        out_shape=[
            jax.ShapeDtypeStruct((rows, ffn), BF),
            jax.ShapeDtypeStruct((rows, width), F32),
            jax.ShapeDtypeStruct((8, width), F32),
            jax.ShapeDtypeStruct((1, ffn), F32),
        ],
        scratch_shapes=[
            pltpu.VMEM((parts, width, ffn // parts), BF),
            pltpu.VMEM((parts, width, ffn // parts), BF),
            pltpu.SemaphoreType.DMA((parts,)),
            pltpu.SemaphoreType.DMA((parts,)),
        ],
        compiler_params=pltpu.CompilerParams(vmem_limit_bytes=VMEM_LIMIT),
        cost_estimate=pl.CostEstimate(flops=15 * 10**9, bytes_accessed=30 * 10**6, transcendentals=0),
        name="ffn_backward",
    )(me, grad, slope, middle, vec, *arrays)


def ffn_weight_kernel(nffn_ref, grad_ref, gupper_ref, active_ref, out_ref, nffn_t, grad_t):
    @pl.when(pl.program_id(0) == 0)
    def _():
        nffn_t[...] = nffn_ref[...].T
        grad_t[...] = grad_ref[...].astype(BF).T

    shape = (out_ref.shape[0],) + out_ref.shape[3:]
    out_ref[:, 0, 0] = dot_nn(nffn_t[...], gupper_ref[...]).astype(BF).reshape(shape)
    out_ref[:, 0, 1] = dot_nn(grad_t[...], active_ref[...]).astype(BF).reshape(shape)


def ffn_weight(nffn, grad, gupper, active, stripes, parts):
    rows, width = nffn.shape
    piece = gupper.shape[1] // parts
    high = width // stripes
    whole = pl.BlockSpec((rows, width), lambda i: (0, 0))
    return pl.pallas_call(
        ffn_weight_kernel,
        grid=(parts,),
        in_specs=[
            whole,
            whole,
            pl.BlockSpec((rows, piece), lambda i: (0, i)),
            pl.BlockSpec((rows, piece), lambda i: (0, i)),
        ],
        out_specs=pl.BlockSpec((stripes, 1, 2, high, piece), lambda i: (0, i, 0, 0, 0)),
        out_shape=jax.ShapeDtypeStruct((stripes, parts, 2, high, piece), BF),
        scratch_shapes=[pltpu.VMEM((width, rows), BF), pltpu.VMEM((width, rows), BF)],
        compiler_params=pltpu.CompilerParams(vmem_limit_bytes=VMEM_LIMIT),
        cost_estimate=pl.CostEstimate(flops=15 * 10**9, bytes_accessed=30 * 10**6, transcendentals=0),
        name="ffn_weight",
    )(nffn, grad, gupper, active)


def attention_backward_kernel(gmiddle_ref, stream_ref, proj_ref, probs_ref, vec_ref, qkv_s, out_s, *refs):
    gstream_ref, gproj_ref, small_ref, gmixed_s = refs[-4:]

    @pl.when(pl.program_id(0) == 0)
    def _():
        small_ref[...] = jnp.zeros_like(small_ref)

    width = stream_ref.shape[1]
    block_pages, _, slots, _ = probs_ref.shape
    scale = (width // HEADS) ** (-0.5)
    gmiddle = gmiddle_ref[...]
    gmixed_s[...] = dot_nt(gmiddle.astype(BF), out_s[...]).astype(BF)
    lanes = 2 * (width // HEADS)
    for page in range(block_pages):
        rows = slice(page * slots, (page + 1) * slots)
        for pair in range(PAIRS):
            at = pair * lanes
            gmixed = gmixed_s[rows, at : at + lanes]
            queries = split_heads(proj_ref[rows, at : at + lanes])
            keys_in = split_heads(proj_ref[rows, width + at : width + at + lanes])
            values = split_heads(proj_ref[rows, 2 * width + at : 2 * width + at + lanes])
            probs = probs_ref[page, pair]
            gsoft = dot_nt(gmixed, values)
            gscore = []
            for head in range(2):
                cols = slice(head * slots, (head + 1) * slots)
                soft = probs[:, cols].astype(F32)
                grad = gsoft[:, cols]
                inner = jnp.sum(soft * grad, axis=-1, keepdims=True)
                gscore.append((soft * (grad - inner)).astype(BF))
            stacked = jnp.concatenate([probs[:, :slots], probs[:, slots:]], axis=0)
            gvalues = dot_tn(stacked, split_heads(gmixed))
            gqueries = dot_nn(jnp.concatenate(gscore, axis=1), keys_in) * scale
            gkeys = dot_tn(jnp.concatenate(gscore, axis=0), queries) * scale
            gproj_ref[rows, at : at + lanes] = gqueries.astype(BF)
            gproj_ref[rows, width + at : width + at + lanes] = gkeys.astype(BF)
            gproj_ref[rows, 2 * width + at : 2 * width + at + lanes] = gvalues.astype(BF)
    gnormed = dot_nt(gproj_ref[...], qkv_s[...])
    unit, root = normalize(stream_ref[...].astype(F32))
    gstream_ref[...] = gmiddle + norm_backward(gnormed, unit, root, vec_ref[0:1, :])
    small_ref[0:1, :] += column_sum(gnormed * unit)
    small_ref[1:2, :] += column_sum(gnormed)
    small_ref[2:3, :] += column_sum(gproj_ref[:, :width].astype(F32))
    small_ref[3:4, :] += column_sum(gproj_ref[:, 2 * width :].astype(F32))


def attention_backward(gmiddle, stream, proj, probs, vec, weight, block_pages, begin, end, before):
    rows, width = stream.shape
    _, _, slots, _ = probs.shape
    block = block_pages * slots
    first = begin // block_pages
    row_spec = lambda cols: pl.BlockSpec((block, cols), lambda i: (i + first, 0))
    whole = lambda array: pl.BlockSpec(array.shape, lambda i: (0, 0))
    before = [] if before is None else list(before)
    operands = [gmiddle, stream, proj, probs, vec, weight[0], weight[1]]
    return pl.pallas_call(
        attention_backward_kernel,
        grid=((end - begin) // block_pages,),
        in_specs=[
            row_spec(width),
            row_spec(width),
            row_spec(3 * width),
            pl.BlockSpec((block_pages, PAIRS, slots, 2 * slots), lambda i: (i + first, 0, 0, 0)),
            whole(vec),
            whole(weight[0]),
            whole(weight[1]),
        ]
        + [pl.BlockSpec(memory_space=pl.ANY)] * len(before),
        out_specs=[row_spec(width), row_spec(3 * width), pl.BlockSpec((8, width), lambda i: (0, 0))],
        out_shape=[
            jax.ShapeDtypeStruct((rows, width), F32),
            jax.ShapeDtypeStruct((rows, 3 * width), BF),
            jax.ShapeDtypeStruct((8, width), F32),
        ],
        scratch_shapes=[pltpu.VMEM((block, width), BF)],
        input_output_aliases={len(operands) + index: index for index in range(len(before))},
        compiler_params=pltpu.CompilerParams(vmem_limit_bytes=VMEM_LIMIT),
        cost_estimate=pl.CostEstimate(flops=15 * 10**9, bytes_accessed=20 * 10**6, transcendentals=0),
        name="attention_backward",
    )(*operands, *before)


def attention_weight_kernel(normed_ref, mixed_ref, gproj_ref, gmiddle_ref, grad_ref):
    gqkv = dot_tn(normed_ref[...], gproj_ref[...])
    gout = dot_tn(mixed_ref[...], gmiddle_ref[...].astype(BF))
    parts = grad_ref.shape[1]
    cut = gqkv.shape[1] // parts
    rest = gout.shape[1] // parts
    shape = (grad_ref.shape[0],) + grad_ref.shape[3:]
    for part in range(parts):
        qkv_part = gqkv[:, part * cut : (part + 1) * cut].astype(BF)
        out_part = gout[:, part * rest : (part + 1) * rest].astype(BF)
        grad_ref[:, part, 0] = jnp.concatenate([qkv_part, out_part], axis=1).reshape(shape)


def attention_weight(normed, mixed, gproj, gmiddle, stripes, parts):
    rows, width = normed.shape
    block = width // 2
    high = width // stripes
    return pl.pallas_call(
        attention_weight_kernel,
        grid=(2,),
        in_specs=[
            pl.BlockSpec((rows, block), lambda i: (0, i)),
            pl.BlockSpec((rows, block), lambda i: (0, i)),
            pl.BlockSpec((rows, 3 * width), lambda i: (0, 0)),
            pl.BlockSpec((rows, width), lambda i: (0, 0)),
        ],
        out_specs=pl.BlockSpec((stripes // 2, parts, 1, high, width), lambda i: (i, 0, 0, 0, 0)),
        out_shape=jax.ShapeDtypeStruct((stripes, parts, 1, high, width), BF),
        compiler_params=pltpu.CompilerParams(vmem_limit_bytes=VMEM_LIMIT),
        cost_estimate=pl.CostEstimate(flops=10 * 10**9, bytes_accessed=20 * 10**6, transcendentals=0),
        name="attention_weight",
    )(normed, mixed, gproj, gmiddle)


def relative_rows(source, target, me, depth):
    high = source.shape[0] // (2 * depth)
    for x in range(2):
        for z in range(depth):
            start = pl.multiple_of(jnp.bitwise_xor(me, 2 * z + x) * high, 16)
            at = (x * depth + z) * high
            target[at : at + high, :] = source[pl.ds(start, high), :]


def send_out(me_ref, core, y, staged, slot, own_ref, other_ref, sems):
    for x in range(2):
        first, second = plane(me_ref, x, y, core)

        @pl.when(core == 0)
        def _():
            pltpu.make_async_copy(staged.at[slot, x], own_ref.at[second, first], sems.at[slot, x]).start()

        @pl.when(core == 1)
        def _():
            pltpu.make_async_copy(staged.at[slot, x], other_ref.at[second, first], sems.at[slot, x]).start()


def wait_out(staged, slot, own_ref, sems):
    for x in range(2):
        pltpu.make_async_copy(staged.at[slot, x], own_ref.at[0, 0], sems.at[slot, x]).wait()


def ffn_weight_split_kernel(
    me_ref, nffn_ref, grad_ref, gupper_ref, active_ref, other_ref, own_ref, turned, nffn_t, grad_t, staged, sems
):
    step = pl.program_id(0)
    _, _, depth, high, width = staged.shape
    high = high // 2

    @pl.when(step == 0)
    def _():
        turned[...] = nffn_ref[...].T
        relative_rows(turned, nffn_t, me_ref[0], depth)
        turned[...] = grad_ref[...].astype(BF).T
        relative_rows(turned, grad_t, me_ref[0], depth)

    slot = step % 2

    @pl.when(step >= 2)
    def _():
        wait_out(staged, slot, own_ref, sems)

    shape = (2, depth, high, width)
    staged[slot, :, :, :high, :] = dot_nn(nffn_t[...], gupper_ref[...]).astype(BF).reshape(shape)
    staged[slot, :, :, high:, :] = dot_nn(grad_t[...], active_ref[...]).astype(BF).reshape(shape)
    send_out(me_ref, 1 - step // 2, step % 2, staged, slot, own_ref, other_ref, sems)

    @pl.when(step == 3)
    def _():
        wait_out(staged, 1 - slot, own_ref, sems)
        wait_out(staged, slot, own_ref, sems)


def ffn_weight_split(me, nffn, grad, gupper, active, depth):
    rows, width = nffn.shape
    piece = gupper.shape[1] // 4
    high = width // (2 * depth)

    def column(step, me):
        return (0, jnp.bitwise_xor(me[1], 2 * (step % 2) + 1 - step // 2))

    whole = pl.BlockSpec((rows, width), lambda i, me: (0, 0))
    return pl.pallas_call(
        ffn_weight_split_kernel,
        grid_spec=pltpu.PrefetchScalarGridSpec(
            num_scalar_prefetch=1,
            grid=(4,),
            in_specs=[whole, whole, pl.BlockSpec((rows, piece), column), pl.BlockSpec((rows, piece), column)],
            out_specs=[pl.BlockSpec(memory_space=pl.ANY)] * 2,
            scratch_shapes=[pltpu.VMEM((width, rows), BF)] * 3
            + [pltpu.VMEM((2, 2, depth, 2 * high, piece), BF), pltpu.SemaphoreType.DMA((2, 2))],
        ),
        out_shape=[jax.ShapeDtypeStruct((2, 2, depth, 2 * high, piece), BF)] * 2,
        compiler_params=pltpu.CompilerParams(vmem_limit_bytes=VMEM_LIMIT),
        cost_estimate=pl.CostEstimate(flops=15 * 10**9, bytes_accessed=30 * 10**6, transcendentals=0),
        name="ffn_weight",
    )(me, nffn, grad, gupper, active)


def attention_weight_split_kernel(me_ref, normed_ref, mixed_ref, gproj_ref, gmiddle_ref, *refs):
    other_ref, own_ref, turned, normed_t, mixed_t, found, staged, extra_s, sems = refs[-9:]
    extra_refs = refs[:-9]
    step = pl.program_id(0)
    _, _, depth, rows, width = staged.shape
    high = width // (2 * depth)
    share = width // 4
    shape = (2, depth, high, width)

    @pl.when(step == 0)
    def _():
        turned[...] = mixed_ref[...].T
        relative_rows(turned, mixed_t, me_ref[0], depth)
        found[:, 3 * width :] = dot_nn(mixed_t[...], gmiddle_ref[...].astype(BF)).astype(BF)
        turned[...] = normed_ref[...].T
        relative_rows(turned, normed_t, me_ref[0], depth)
        if extra_refs:
            extra_s[...] = jnp.zeros_like(extra_s)
            for index in range(2):
                one_ref, more_ref, two_ref, hidden_ref = extra_refs[4 * index : 4 * index + 4]
                sums = jnp.concatenate([one_ref[:4, :] + more_ref[:4, :], two_ref[:4, :]], axis=0)
                for part in range(4):
                    at = index * (width // 3)
                    extra_s[part, :8, at : at + share] = sums[:, part * share : (part + 1) * share]
                    extra_s[part, 8 + index : 9 + index, :] = hidden_ref[:, part * width : (part + 1) * width]
            for part in range(4):
                extra = extra_s[part].astype(BF)
                staged[part, :, :, high:, :] = jnp.broadcast_to(extra[None, None], (2, depth) + extra.shape)

    def finish(part):
        columns = slice(part * 3 * share, (part + 1) * 3 * share)
        rest = slice(3 * width + part * share, 3 * width + (part + 1) * share)
        staged[part, :, :, :high, :] = jnp.concatenate([found[:, columns], found[:, rest]], axis=1).reshape(shape)
        near = jnp.bitwise_xor(me_ref[1], part)
        send_out(me_ref, near % 2, near // 2, staged, part, own_ref, other_ref, sems)

    for third in range(3):

        @pl.when(step == third)
        def _():
            found[:, third * width : (third + 1) * width] = dot_nn(normed_t[...], gproj_ref[...]).astype(BF)
            for part in ((0,), (1,), (2, 3))[third]:
                finish(part)
            if third == 2:
                for part in range(4):
                    wait_out(staged, part, own_ref, sems)


def attention_weight_split(me, normed, mixed, gproj, gmiddle, depth, extra=None):
    rows, width = normed.shape
    high = width // (2 * depth)
    whole = lambda array: pl.BlockSpec(array.shape, lambda i: (0,) * array.ndim)
    extras = [] if extra is None else list(extra)
    shape = (2, 2, depth, high + (0 if extra is None else 16), width)
    operands = [normed, mixed, gproj, gmiddle] + extras
    return pl.pallas_call(
        attention_weight_split_kernel,
        grid=(3,),
        in_specs=[pl.BlockSpec(memory_space=pltpu.SMEM), whole(normed), whole(mixed)]
        + [pl.BlockSpec((rows, width), lambda i: (0, i))]
        + [whole(operand) for operand in operands[3:]],
        out_specs=[pl.BlockSpec(memory_space=pl.ANY)] * 2,
        out_shape=[jax.ShapeDtypeStruct(shape, BF)] * 2,
        scratch_shapes=[pltpu.VMEM((width, rows), BF)] * 3
        + [
            pltpu.VMEM((width, 4 * width), BF),
            pltpu.VMEM((4,) + shape[1:], BF),
            pltpu.VMEM((4, 16, width), F32),
            pltpu.SemaphoreType.DMA((4, 2)),
        ],
        compiler_params=pltpu.CompilerParams(vmem_limit_bytes=VMEM_LIMIT),
        cost_estimate=pl.CostEstimate(flops=10 * 10**9, bytes_accessed=20 * 10**6, transcendentals=0),
        name="attention_weight",
    )(me, *operands)


def pair_bias(slot_kind, slot_valid, across):
    same_kind = slot_kind[:, :, None] == slot_kind[:, None, :]
    partner = jnp.logical_not(same_kind) if across else same_kind
    allowed = jnp.logical_and(partner, slot_valid[:, None, :] > 0)
    return jnp.where(allowed, 0.0, -1e30).astype(F32)


def ordered_vectors(small_one, small_two):
    picked = (small_one, 0), (small_two, 0), (small_one, 1), (small_one, 2)
    picked += (small_one, 3), (small_two, 3), (small_two, 1), (small_two, 2)
    return jnp.stack([sums[row] for sums, row in picked])


def adam_step(master, grad, moment_one, moment_two, factor, decayed):
    clipped = grad * factor
    first_new = beta_one * moment_one + (1.0 - beta_one) * clipped
    second_new = beta_two * moment_two + (1.0 - beta_two) * clipped * clipped
    change = first_new / bias_one / (jnp.sqrt(second_new / bias_two) + epsilon)
    if decayed:
        change = change + weight_decay * master
    return (-learn_rate * change, first_new, second_new)


def gather_rows(pieces, sizes):
    kinds, high, width = pieces.shape
    rows = lax.all_gather(pieces.reshape(-1, width), ("dp", "tensor"), axis=0, tiled=False)
    if high % 16 == 0:
        return [(("rows", kind * high), [rows]) for kind in range(kinds)]
    split = rows.reshape(sizes["dp"], sizes["tensor"], kinds, high, width)
    return [(("whole",), [jnp.swapaxes(split[:, :, kind], 0, 1).reshape(-1, width, width)]) for kind in range(kinds)]


def scatter_rows(grad, sizes):
    stripes, parts, kinds, high, width = grad.shape
    inner = sizes["dp"] // stripes
    if inner > 1:
        grad = jnp.moveaxis(grad.reshape(stripes, parts, kinds, inner, high // inner, width), 3, 1)
    mine = lax.psum_scatter(grad.reshape(-1, width), ("dp", "tensor"), scatter_dimension=0, tiled=True)
    return mine.reshape(kinds, -1, width).astype(F32)


class Exchange:
    def __init__(self, sizes):
        self.sizes = sizes
        self.depth = sizes["dp"] // 2

    def swap(self, value, partner):
        dp, tensor = self.sizes["dp"], self.sizes["tensor"]
        pairs = []
        for i in range(dp):
            for j in range(tensor):
                far_i, far_j = partner(i, j)
                pairs.append((i * tensor + j, far_i * tensor + far_j))
        return lax.ppermute(value, ("dp", "tensor"), pairs)

    def part(self, bits, value):
        return self.swap(value, lambda i, j: (i, j ^ bits))

    def core(self, value):
        return self.part(1, value)

    def x(self, value):
        return self.swap(value, lambda i, j: (i ^ 1, j))

    def y(self, value):
        return self.part(2, value)

    def diagonal(self, value):
        return self.swap(value, lambda i, j: (i ^ 1, j ^ 2))

    def first(self, value):
        return self.swap(value, lambda i, j: (i, j ^ 2) if j & 1 else (i ^ 1, j))

    def second(self, value):
        return self.swap(value, lambda i, j: (i ^ 1, j) if j & 1 else (i, j ^ 2))

    def z(self, distance, value):
        return self.swap(value, lambda i, j: (i ^ (2 * distance), j))

    def z_sends(self, values):
        return [(functools.partial(self.z, distance), values[distance]) for distance in range(1, self.depth)]

    def gather_z(self, piece):
        groups = [[2 * z + x for z in range(self.depth)] for x in range(2)]
        return lax.all_gather(piece, "dp", axis=0, tiled=False, axis_index_groups=groups)

    def total(self, value):
        value = value + self.core(value)
        value = value + self.y(value)
        value = value + self.x(value)
        bit = 1
        while bit < self.depth:
            value = value + self.z(bit, value)
            bit *= 2
        return value


def tie(values, after):
    return lax.optimization_barrier((values, after))[0]


class Spread:
    def __init__(self, exchange, quad, fixed):
        self.exchange, self.quad, self.fixed = exchange, quad, fixed

    def go_first(self):
        return [(self.exchange.first, self.quad)]

    def go_second(self, came):
        self.pair = jnp.stack([self.quad, came[0]])
        return [(self.exchange.second, self.pair), (self.exchange.core, self.pair)]

    def go_core(self, came):
        self.two, self.far_pair = came
        return [(self.exchange.core, self.two)]

    def weight(self, came, offset=0):
        positions = [[(0, second, core), (1, second, core)] for core in range(2) for second in range(2)]
        arrays = [self.pair, self.two, self.far_pair, came[0]]
        return (("near", offset, positions, self.fixed), arrays)


class Reduce:
    def __init__(self, exchange, other, own):
        self.exchange, self.other, self.own = exchange, other, own

    def wide(self, value):
        return value.astype(F32)

    def go_core(self):
        return [(self.exchange.core, self.other)]

    def go_second(self, came):
        self.came = came[0]
        value = (self.wide(self.own[1]) + self.wide(self.came[1])).astype(BF)
        return [(self.exchange.second, value)]

    def go_first(self, came):
        self.beside = came[0]
        value = self.wide(self.own[0, 1]) + self.wide(self.came[0, 1]) + self.wide(self.beside[1])
        return [(self.exchange.first, value.astype(BF))]

    def depths(self, came):
        ahead = came[0]
        return (
            self.wide(self.own[0, 0]) + self.wide(self.came[0, 0]) + self.wide(self.beside[0]) + self.wide(ahead)
        )


class Lane:
    def __init__(self):
        self.last = None

    def after_last(self, values):
        return values if self.last is None else tie(values, self.last)

    def step(self, sends, kernel=None, arrays=()):
        values = [value for _, value in sends]
        values, arrays = self.after_last((values, list(arrays)))
        came = [move(value) for (move, _), value in zip(sends, values)]
        results = [] if kernel is None else list(kernel(*arrays))
        came, results = lax.optimization_barrier((came, results))
        self.last = results[-1] if results else came[-1]
        return came, results


def shards(
    sizes,
    tokens, out_grad, slot_kind, slot_valid,
    qkv_weight, qkv_first, qkv_second,
    out_weight, out_first, out_second,
    up_weight, up_first, up_second,
    down_weight, down_first, down_second,
    gain_weight, gain_first, gain_second,
    bias_weight, bias_first, bias_second,
    hidden_weight, hidden_first, hidden_second,
):
    parts = sizes["tensor"]
    width = tokens.shape[1]
    cut = qkv_weight.shape[2]
    high = qkv_weight.shape[1]
    split = parts == 4 and high % 32 == 0 and sizes["dp"] in (4, 8, 16)
    exchange = Exchange(sizes)
    stripes = sizes["dp"] if high % 16 == 0 else 2
    me = jnp.stack([lax.axis_index("dp"), lax.axis_index("tensor")]).astype(jnp.int32)
    attn_pieces = jnp.concatenate([qkv_weight.astype(BF), out_weight.astype(BF)], axis=2)
    up_pieces = up_weight.astype(BF)
    down_pieces = jnp.swapaxes(down_weight.astype(BF), 1, 2)
    pages = slot_kind.shape[0]
    block_pages = 2 if pages % 2 == 0 else 1
    block = block_pages * slot_kind.shape[1]
    middle_page = block_pages
    masks = [pair_bias(slot_kind, slot_valid, index == 0) for index in range(2)]
    lane = Lane()
    gathered = lambda index: gather_rows(
        jnp.stack([attn_pieces[index], up_pieces[index], down_pieces[index]]), sizes
    )
    small = hidden = None
    saved = [None, None]

    def attention_forward_of(index, weight):
        return lambda stream: attention_forward(
            me, stream, masks[index], small[index], weight, block_pages, parts
        )

    def ffn_forward_of(index, up_w, down_w):
        return lambda nffn, middle: ffn_forward(
            me, nffn, middle, small[index], hidden[index : index + 1], up_w, down_w, block, parts
        )

    def ffn_backward_of(index):
        kept = saved[index]
        return lambda grad: ffn_backward(
            me, grad, kept["slope"], kept["middle"], small[index], kept["up_w"], kept["down_w"], block, parts
        )

    def ffn_weight_of(index, grad):
        kept = saved[index]
        if split:
            return lambda gupper: ffn_weight_split(
                me, kept["nffn"], grad, gupper, kept["active"], exchange.depth
            )
        return lambda gupper: (ffn_weight(kept["nffn"], grad, gupper, kept["active"], stripes, parts),)

    def attention_backward_of(index, begin, end, before=None):
        kept = saved[index]
        return lambda gmiddle: attention_backward(
            gmiddle, kept["stream"], kept["proj"], kept["probs"], small[index], kept["weight"],
            block_pages, begin, end, before,
        )

    def attention_weight_of(index, gmiddle, extra=None):
        kept = saved[index]
        if split:
            return lambda gproj: attention_weight_split(
                me, kept["normed"], kept["mixed"], gproj, gmiddle, exchange.depth, extra
            )
        return lambda gproj: (attention_weight(kept["normed"], kept["mixed"], gproj, gmiddle, stripes, parts),)

    def keep(index, stream, attention, ffn):
        middle, nffn, normed, proj, probs, mixed, qkv_w, out_w = attention
        saved[index] = dict(
            stream=stream, middle=middle, nffn=nffn, normed=normed, proj=proj, probs=probs, mixed=mixed,
            weight=(qkv_w, out_w), active=ffn[1], slope=ffn[2], up_w=(("whole",), [ffn[3]]), down_w=(("whole",), [ffn[4]]),
        )

    if split:
        depth = exchange.depth
        late = jnp.concatenate([attn_pieces[1], up_pieces[1], down_pieces[1]], axis=0)
        own_small = jnp.concatenate(
            [gain_weight, bias_weight, hidden_weight.reshape(2, -1, gain_weight.shape[2])], axis=1
        )
        own_small = lax.reduce_precision(own_small, 8, 7)
        small_sends = [(functools.partial(exchange.part, bits), own_small) for bits in range(1, 4)]
        late = exchange.gather_z(late)
        came, _ = lane.step(exchange.z_sends([attn_pieces[0]] * depth) + small_sends)
        attn_zero = Spread(exchange, jnp.stack([attn_pieces[0]] + came[: depth - 1]), False)
        mine = lax.axis_index("tensor")
        every = jnp.zeros((4,) + own_small.shape, F32)
        for bits, value in enumerate([own_small] + came[depth - 1 :]):
            every = lax.dynamic_update_slice_in_dim(every, value[None], jnp.bitwise_xor(mine, bits), 0)
        small = jnp.moveaxis(every[:, :, :8], 0, 2).reshape(2, 8, width)
        hidden = jnp.moveaxis(every[:, :, 8:], 0, 1).reshape(2, -1)
        ffn_piece = jnp.concatenate([up_pieces[0], down_pieces[0]], axis=0)
        ffn_sends = exchange.z_sends([ffn_piece] * depth)
        middle_at = depth // 2 - 1
        came, _ = lane.step(attn_zero.go_first() + ffn_sends[middle_at : middle_at + 1])
        ffn_came = came[1:]
        ffn_sends = ffn_sends[:middle_at] + ffn_sends[middle_at + 1 :]
        came, _ = lane.step(attn_zero.go_second(came[:1]) + ffn_sends)
        others = came[2:]
        others.insert(middle_at, ffn_came[0])
        ffn_zero = Spread(exchange, jnp.stack([ffn_piece] + others), False)
        came, _ = lane.step(attn_zero.go_core(came[:2]) + ffn_zero.go_first())
        attn_w = attn_zero.weight(came[:1])
        came, attention = lane.step(ffn_zero.go_second(came[1:]), attention_forward_of(0, attn_w), [tokens])
        late = lane.after_last(late)
        attn_one = Spread(exchange, late[:, :high], True)
        ffn_one = Spread(exchange, late[:, high:], True)
        came, _ = lane.step(ffn_zero.go_core(came) + attn_one.go_first())
        up_w, down_w = ffn_zero.weight(came[:1]), ffn_zero.weight(came[:1], high)
        came, ffn = lane.step(
            attn_one.go_second(came[1:]) + ffn_one.go_first(), ffn_forward_of(0, up_w, down_w), attention[1::-1]
        )
        keep(0, tokens, attention, ffn)
        stream = ffn[0]
        ffn_came = came[2:]
        came, _ = lane.step(attn_one.go_core(came[:2]))
        attn_w = attn_one.weight(came)
        came, attention = lane.step(ffn_one.go_second(ffn_came), attention_forward_of(1, attn_w), [stream])
        came, _ = lane.step(ffn_one.go_core(came))
        up_w, down_w = ffn_one.weight(came), ffn_one.weight(came, high)
        _, ffn = lane.step([], ffn_forward_of(1, up_w, down_w), attention[1::-1])
        keep(1, stream, attention, ffn)
        block_output = ffn[0]

        _, (gupper, gmiddle, small_two, hidden_one) = lane.step([], ffn_backward_of(1), [out_grad])
        _, grads = lane.step([], ffn_weight_of(1, out_grad), [gupper])
        ffn_one = Reduce(exchange, *grads)
        came, before = lane.step(ffn_one.go_core(), attention_backward_of(1, 0, middle_page), [gmiddle])
        came, after = lane.step(
            ffn_one.go_second(came), attention_backward_of(1, middle_page, pages, before[:2]), [gmiddle]
        )
        grad, gproj = after[:2]
        sums_one = (before[2], after[2], small_two, hidden_one)
        came, grads = lane.step(ffn_one.go_first(came), attention_weight_of(1, gmiddle), [gproj])
        layers = ffn_one.depths(came)
        attn_one = Reduce(exchange, *grads)
        came, results = lane.step(attn_one.go_core(), ffn_backward_of(0), [grad])
        gupper, gmiddle, small_two, hidden_zero = results
        came, grads = lane.step(attn_one.go_second(came), ffn_weight_of(0, grad), [gupper])
        ffn_zero = Reduce(exchange, *grads)
        came, before = lane.step(
            ffn_zero.go_core() + attn_one.go_first(came), attention_backward_of(0, 0, middle_page), [gmiddle]
        )
        layers = jnp.concatenate([attn_one.depths(came[1:]), layers], axis=1)
        late_sends = exchange.z_sends([layers[z].astype(BF) for z in range(depth)])
        late_sends = late_sends[middle_at : middle_at + 1] + late_sends[:middle_at] + late_sends[middle_at + 1 :]
        came, after = lane.step(
            ffn_zero.go_second(came[:1]) + late_sends[:1],
            attention_backward_of(0, middle_page, pages, before[:2]),
            [gmiddle],
        )
        late_came = came[1:]
        input_grad, gproj = after[:2]
        came, grads = lane.step(
            ffn_zero.go_first(came[:1]) + late_sends[1:],
            attention_weight_of(0, gmiddle, (before[2], after[2], small_two, hidden_zero) + sums_one),
            [gproj],
        )
        total = layers[0] + sum(value.astype(F32) for value in late_came + came[1:])
        grad_attn, grad_up, grad_down = ([None, total[at : at + high]] for at in (0, high, 2 * high))
        layers = ffn_zero.depths(came[:1])
        ffn_sends = exchange.z_sends([layers[z].astype(BF) for z in range(depth)])
        ffn_sends = ffn_sends[middle_at : middle_at + 1] + ffn_sends[:middle_at] + ffn_sends[middle_at + 1 :]
        attn_zero = Reduce(exchange, *grads)
        came, _ = lane.step(attn_zero.go_core())
        came, _ = lane.step(attn_zero.go_second(came) + ffn_sends[:1])
        ffn_came = came[1:]
        came, _ = lane.step(attn_zero.go_first(came[:1]) + ffn_sends[1:])
        total = layers[0] + sum(value.astype(F32) for value in ffn_came + came[1:])
        grad_up[0], grad_down[0] = total[:high], total[high:]
        layers = attn_zero.depths(came[:1])
        came, _ = lane.step(exchange.z_sends([layers[z].astype(BF) for z in range(depth)]))
        total = layers[0] + sum(value.astype(F32) for value in came)
        grad_attn[0] = total[:high]
        share = width // parts
        vectors = []
        for at in (0, width // 3):
            sums = total[high : high + 8, at : at + share]
            vectors.append(ordered_vectors(sums[:4], sums[4:]))
        vectors = jnp.stack(vectors)
        grad_hidden = total[high + 8 : high + 10]
    else:
        small = jnp.concatenate([gain_weight, bias_weight], axis=1).astype(BF)
        small = lax.all_gather(small, "tensor", axis=2, tiled=True).astype(F32)
        hidden = lax.all_gather(hidden_weight.astype(BF), "tensor", axis=1, tiled=True).astype(F32)
        stream = tokens
        for index in range(2):
            attn_w, up_w, down_w = gathered(index)
            attention = attention_forward_of(index, attn_w)(stream)
            ffn = ffn_forward_of(index, up_w, down_w)(*attention[1::-1])
            keep(index, stream, attention, ffn)
            stream = ffn[0]
        block_output = stream
        grad = out_grad
        grad_attn, grad_up, grad_down, vectors, grad_hidden = ([None, None] for _ in range(5))
        for index in (1, 0):
            gupper, gmiddle, small_two, grad_hidden[index] = ffn_backward_of(index)(grad)
            (gffn,) = ffn_weight_of(index, grad)(gupper)
            grad_up[index], grad_down[index] = scatter_rows(gffn, sizes)
            grad, gproj, small_one = attention_backward_of(index, 0, pages)(gmiddle)
            (grad_attn[index],) = scatter_rows(attention_weight_of(index, gmiddle)(gproj)[0], sizes)
            vectors[index] = ordered_vectors(small_one, small_two)
        input_grad = grad
        vectors, grad_hidden = lax.psum((jnp.stack(vectors), jnp.concatenate(grad_hidden, axis=0)), ("dp", "tensor"))
        at = lax.axis_index("tensor")
        slice_of = lambda whole: lax.dynamic_slice_in_dim(
            whole, at * (whole.shape[-1] // parts), whole.shape[-1] // parts, whole.ndim - 1
        )
        vectors, grad_hidden = slice_of(vectors), slice_of(grad_hidden)
    grad_gain, grad_bias = vectors[:, :2], vectors[:, 2:]
    grad_attn, grad_up, grad_down = jnp.stack(grad_attn), jnp.stack(grad_up), jnp.stack(grad_down)
    shared_squares = jnp.sum(vectors * vectors) + jnp.sum(grad_hidden * grad_hidden)
    local_squares = (
        jnp.sum(grad_attn * grad_attn) + jnp.sum(grad_up * grad_up) + jnp.sum(grad_down * grad_down)
    ) + jnp.where(lax.axis_index("dp") == 0, shared_squares, 0.0)
    grad_down = jnp.swapaxes(grad_down, 1, 2)
    if split:
        total_squares = exchange.total(local_squares.reshape(1, 1))[0, 0]
    else:
        total_squares = lax.psum(local_squares, ("dp", "tensor"))
    grad_norm = jnp.sqrt(total_squares)
    factor = clip_norm / jnp.maximum(grad_norm, clip_norm)
    masters = (qkv_weight, out_weight, up_weight, down_weight, gain_weight, bias_weight, hidden_weight)
    firsts = (qkv_first, out_first, up_first, down_first, gain_first, bias_first, hidden_first)
    seconds = (qkv_second, out_second, up_second, down_second, gain_second, bias_second, hidden_second)
    gradients = (
        grad_attn[:, :, :cut], grad_attn[:, :, cut:], grad_up, grad_down, grad_gain, grad_bias, grad_hidden,
    )
    results = [block_output, input_grad, grad_norm]
    for member in range(7):
        update, first_new, second_new = adam_step(
            masters[member], gradients[member], firsts[member], seconds[member], factor, member < 4
        )
        results = results + [gradients[member], update, first_new, second_new]
    return tuple(results)


def solution(mesh):
    rows = P(("dp", "tensor"), None)
    matrix = P(None, "dp", "tensor")
    turned = P(None, "tensor", "dp")
    vectors = P(None, None, "tensor")
    hidden = P(None, "tensor")
    return jax.shard_map(
        functools.partial(shards, dict(mesh.shape)),
        mesh=mesh,
        in_specs=(rows,) * 4 + (matrix,) * 9 + (turned,) * 3 + (vectors,) * 6 + (hidden,) * 3,
        out_specs=(rows, rows, P()) + (matrix,) * 12 + (turned,) * 4 + (vectors,) * 8 + (hidden,) * 4,
        check_vma=False,
    )
```

```python
import functools

import jax
import jax.numpy as jnp
from jax import lax
from jax.experimental import pallas as pl
from jax.experimental.pallas import tpu as pltpu
from jax.sharding import PartitionSpec as P

HEADS = 12
PAIRS = HEADS // 2

beta_one = 0.9
beta_two = 0.99
learn_rate = 0.01
weight_decay = 0.01
epsilon = 1e-08
clip_norm = 1.0
bias_one = 1.0 - beta_one**10
bias_two = 1.0 - beta_two**10

BF = jnp.bfloat16
F32 = jnp.float32
VMEM_LIMIT = 56 * 1024 * 1024


def dot_nn(a, b):
    return lax.dot_general(a, b, (((1,), (0,)), ((), ())), preferred_element_type=F32)


def dot_nt(a, b):
    return lax.dot_general(a, b, (((1,), (1,)), ((), ())), preferred_element_type=F32)


def dot_tn(a, b):
    return lax.dot_general(a, b, (((0,), (0,)), ((), ())), preferred_element_type=F32)


def normalize(stream):
    average = jnp.mean(stream, axis=-1, keepdims=True)
    centered = stream - average
    spread = jnp.mean(centered * centered, axis=-1, keepdims=True)
    root = lax.rsqrt(spread + 1e-05)
    return centered * root, root


def norm_backward(grad, unit, root, gain):
    scaled = grad * gain
    first = jnp.mean(scaled, axis=-1, keepdims=True)
    second = jnp.mean(scaled * unit, axis=-1, keepdims=True)
    return root * (scaled - first - unit * second)


def column_sum(value):
    return jnp.sum(value, axis=0, keepdims=True)


def split_heads(pair):
    lane = lax.broadcasted_iota(jnp.int32, pair.shape, 1)
    zero = jnp.zeros_like(pair)
    half = pair.shape[1] // 2
    return jnp.concatenate([jnp.where(lane < half, pair, zero), jnp.where(lane >= half, pair, zero)], axis=0)


def plane(me_ref, first, second, core):
    turned = jnp.bitwise_xor(jnp.bitwise_and(me_ref[1], 1), core) == 1
    return jnp.where(turned, second, first), jnp.where(turned, first, second)


def weight_copies(plan, refs, me_ref, full, sems):
    copies = []

    def add(source, part, rows):
        copies.append(pltpu.make_async_copy(source, full.at[part, rows, :], sems.at[part]))

    parts, width, _ = full.shape
    if plan[0] == "whole":
        for part in range(parts):
            add(refs[0].at[part], part, pl.ds(0, width))
    elif plan[0] == "rows":
        high = width * parts // refs[0].shape[0]
        for index in range(refs[0].shape[0]):
            stripe, part = divmod(index, parts)
            add(refs[0].at[index, pl.ds(plan[1], high), :], part, pl.ds(stripe * high, high))
    else:
        for ref, positions in zip(refs, plan[2]):
            depth = ref.shape[1]
            high = width // (2 * depth)
            for place, (first, second, core) in enumerate(positions):
                x, y = plane(me_ref, first, second, core)
                part = jnp.bitwise_xor(me_ref[1], 2 * y + core)
                if plan[3]:
                    side = jnp.bitwise_xor(jnp.bitwise_and(me_ref[0], 1), x)
                    stripes = full.reshape(parts, depth, 2, high, width).at[part, :, side]
                    source = ref.at[place, :, pl.ds(plan[1], high), :]
                    copies.append(pltpu.make_async_copy(source, stripes, sems.at[part]))
                    continue
                for z in range(depth):
                    start = pl.multiple_of(jnp.bitwise_xor(me_ref[0], 2 * z + x) * high, 16)
                    add(ref.at[place, z, pl.ds(plan[1], high), :], part, pl.ds(start, high))
    return copies


def start_weights(groups):
    for together in zip(*[weight_copies(*group) for group in groups]):
        for copy in together:
            copy.start()


def wait_weight(full, sems, part):
    pltpu.make_async_copy(full.at[part], full.at[part], sems.at[part]).wait()


def part_order(me_ref, plan, parts):
    if plan[0] != "near":
        return list(range(parts))
    return [jnp.bitwise_xor(me_ref[1], near) for near in (0, 2, 1, 3)]


def split_attention(raw, qkv_s, out_s):
    parts = raw.shape[0]
    cut = qkv_s.shape[1] // parts
    step = 96

    def relay(index, _):
        rows = pl.ds(pl.multiple_of(index * step, step), step)
        pieces = [raw[part, rows, :] for part in range(parts)]
        qkv_s[rows, :] = jnp.concatenate([piece[:, :cut] for piece in pieces], axis=1)
        out_s[rows, :] = jnp.concatenate([piece[:, cut:] for piece in pieces], axis=1)
        return 0

    lax.fori_loop(0, raw.shape[1] // step, relay, 0)


def attention_forward_kernel(plan, me_ref, stream_ref, mask_ref, vec_ref, *refs):
    weight_refs = refs[:-10]
    middle_ref, nffn_ref, normed_ref, proj_ref, probs_ref, mixed_ref, qkv_s, out_s, raw, sems = refs[-10:]

    @pl.when(pl.program_id(0) == 0)
    def _():
        start_weights([(plan, weight_refs, me_ref, raw, sems)])
        for part in range(raw.shape[0]):
            wait_weight(raw, sems, part)
        split_attention(raw, qkv_s, out_s)

    width = stream_ref.shape[1]
    slots = mask_ref.shape[1]
    scale = (width // HEADS) ** (-0.5)
    stream = stream_ref[...].astype(F32)
    unit, _ = normalize(stream)
    normed = (unit * vec_ref[0:1, :] + vec_ref[2:3, :]).astype(BF)
    normed_ref[...] = normed
    projected = dot_nn(normed, qkv_s[...])
    proj_ref[:, :width] = (projected[:, :width] + vec_ref[3:4, :]).astype(BF)
    proj_ref[:, width : 2 * width] = projected[:, width : 2 * width].astype(BF)
    proj_ref[:, 2 * width :] = (projected[:, 2 * width :] + vec_ref[4:5, :]).astype(BF)
    lanes = 2 * (width // HEADS)
    for page in range(mask_ref.shape[0]):
        rows = slice(page * slots, (page + 1) * slots)
        bias = mask_ref[page]
        for pair in range(PAIRS):
            at = pair * lanes
            queries = proj_ref[rows, at : at + lanes] * jnp.asarray(scale, BF)
            keys_in = split_heads(proj_ref[rows, width + at : width + at + lanes])
            values = split_heads(proj_ref[rows, 2 * width + at : 2 * width + at + lanes])
            scores = dot_nt(queries, keys_in)
            soft = []
            for head in range(2):
                masked = scores[:, head * slots : (head + 1) * slots] + bias
                peak = jnp.max(masked, axis=-1, keepdims=True)
                exponent = jnp.exp(masked - peak)
                total = jnp.sum(exponent, axis=-1, keepdims=True)
                soft.append((exponent * (1.0 / total)).astype(BF))
            probs = jnp.concatenate(soft, axis=1)
            probs_ref[page, pair] = probs
            mixed_ref[rows, at : at + lanes] = dot_nn(probs, values).astype(BF)
    middle = stream + dot_nn(mixed_ref[...], out_s[...]) + vec_ref[5:6, :]
    middle_ref[...] = middle
    unit, _ = normalize(middle)
    nffn_ref[...] = (unit * vec_ref[1:2, :] + vec_ref[6:7, :]).astype(BF)


def attention_forward(me, stream, mask, vec, weight, block_pages, parts):
    plan, arrays = weight
    rows, width = stream.shape
    pages, slots, _ = mask.shape
    block = block_pages * slots
    row_spec = lambda cols: pl.BlockSpec((block, cols), lambda i: (i, 0))
    return pl.pallas_call(
        functools.partial(attention_forward_kernel, plan),
        grid=(pages // block_pages,),
        in_specs=[
            pl.BlockSpec(memory_space=pltpu.SMEM),
            row_spec(width),
            pl.BlockSpec((block_pages, slots, slots), lambda i: (i, 0, 0)),
            pl.BlockSpec(vec.shape, lambda i: (0, 0)),
        ]
        + [pl.BlockSpec(memory_space=pl.ANY)] * len(arrays),
        out_specs=[
            row_spec(width),
            row_spec(width),
            row_spec(width),
            row_spec(3 * width),
            pl.BlockSpec((block_pages, PAIRS, slots, 2 * slots), lambda i: (i, 0, 0, 0)),
            row_spec(width),
            pl.BlockSpec((width, 3 * width), lambda i: (0, 0)),
            pl.BlockSpec((width, width), lambda i: (0, 0)),
        ],
        out_shape=[
            jax.ShapeDtypeStruct((rows, width), F32),
            jax.ShapeDtypeStruct((rows, width), BF),
            jax.ShapeDtypeStruct((rows, width), BF),
            jax.ShapeDtypeStruct((rows, 3 * width), BF),
            jax.ShapeDtypeStruct((pages, PAIRS, slots, 2 * slots), BF),
            jax.ShapeDtypeStruct((rows, width), BF),
            jax.ShapeDtypeStruct((width, 3 * width), BF),
            jax.ShapeDtypeStruct((width, width), BF),
        ],
        scratch_shapes=[
            pltpu.VMEM((parts, width, width), BF),
            pltpu.SemaphoreType.DMA((parts,)),
        ],
        compiler_params=pltpu.CompilerParams(vmem_limit_bytes=VMEM_LIMIT),
        cost_estimate=pl.CostEstimate(flops=20 * 10**9, bytes_accessed=30 * 10**6, transcendentals=0),
        name="attention_forward",
    )(me, stream, mask, vec, *arrays)


def ffn_forward_kernel(plans, me_ref, nffn_ref, middle_ref, vec_ref, hidden_ref, *refs):
    result_ref, active_ref, slope_ref, up_ref, down_ref, up_s, down_s, up_sems, down_sems = refs[-9:]
    up_refs = refs[: (len(refs) - 9) // 2]
    down_refs = refs[len(up_refs) : -9]
    kept = [pltpu.make_async_copy(up_s, up_ref, up_sems.at[0]), pltpu.make_async_copy(down_s, down_ref, down_sems.at[0])]

    first = pl.program_id(0) == 0
    parts, _, chunk = up_s.shape
    curve = 0.7978845608028654

    @pl.when(first)
    def _():
        start_weights([(plans[0], up_refs, me_ref, up_s, up_sems), (plans[1], down_refs, me_ref, down_s, down_sems)])

    def body(wait):
        nffn = nffn_ref[...]
        total = middle_ref[...] + vec_ref[7:8, :]
        for part in part_order(me_ref, plans[0], parts):
            cols = pl.ds(pl.multiple_of(part * chunk, chunk), chunk)
            if wait:
                wait_weight(up_s, up_sems, part)
            upper = dot_nn(nffn, up_s[part]) + hidden_ref[:, cols]
            square = upper * upper
            angle = jnp.tanh(upper * (curve + (curve * 0.044715) * square))
            half = 0.5 * upper
            lift = 1.0 + angle
            active = (half * lift).astype(BF)
            slope = 0.5 * lift + half * (1.0 - angle * angle) * (curve + (3.0 * curve * 0.044715) * square)
            active_ref[:, cols] = active
            slope_ref[:, cols] = slope.astype(BF)
            if wait:
                wait_weight(down_s, down_sems, part)
            total = total + dot_nt(active, down_s[part])
        result_ref[...] = total
        if wait:
            for copy in kept:
                copy.start()

    pl.when(first)(functools.partial(body, True))
    pl.when(jnp.logical_not(first))(functools.partial(body, False))

    @pl.when(pl.program_id(0) == pl.num_programs(0) - 1)
    def _():
        for copy in kept:
            copy.wait()


def ffn_forward(me, nffn, middle, vec, hidden, up_w, down_w, block, parts):
    rows, width = nffn.shape
    ffn = hidden.shape[1]
    arrays = up_w[1] + down_w[1]
    row_spec = lambda cols: pl.BlockSpec((block, cols), lambda i: (i, 0))
    return pl.pallas_call(
        functools.partial(ffn_forward_kernel, (up_w[0], down_w[0])),
        grid=(rows // block,),
        in_specs=[
            pl.BlockSpec(memory_space=pltpu.SMEM),
            row_spec(width),
            row_spec(width),
            pl.BlockSpec(vec.shape, lambda i: (0, 0)),
            pl.BlockSpec(hidden.shape, lambda i: (0, 0)),
        ]
        + [pl.BlockSpec(memory_space=pl.ANY)] * len(arrays),
        out_specs=[row_spec(width), row_spec(ffn), row_spec(ffn)] + [pl.BlockSpec(memory_space=pl.ANY)] * 2,
        out_shape=[
            jax.ShapeDtypeStruct((rows, width), F32),
            jax.ShapeDtypeStruct((rows, ffn), BF),
            jax.ShapeDtypeStruct((rows, ffn), BF),
        ]
        + [jax.ShapeDtypeStruct((parts, width, ffn // parts), BF)] * 2,
        scratch_shapes=[
            pltpu.VMEM((parts, width, ffn // parts), BF),
            pltpu.VMEM((parts, width, ffn // parts), BF),
            pltpu.SemaphoreType.DMA((parts,)),
            pltpu.SemaphoreType.DMA((parts,)),
        ],
        compiler_params=pltpu.CompilerParams(vmem_limit_bytes=VMEM_LIMIT),
        cost_estimate=pl.CostEstimate(flops=15 * 10**9, bytes_accessed=30 * 10**6, transcendentals=0),
        name="ffn_forward",
    )(me, nffn, middle, vec, hidden, *arrays)


def ffn_backward_kernel(plans, me_ref, grad_ref, slope_ref, middle_ref, vec_ref, *refs):
    gupper_ref, gmiddle_ref, small_ref, ghidden_ref, up_s, down_s, up_sems, down_sems = refs[-8:]
    up_refs = refs[: (len(refs) - 8) // 2]
    down_refs = refs[len(up_refs) : -8]

    first = pl.program_id(0) == 0
    parts, _, chunk = up_s.shape

    @pl.when(first)
    def _():
        start_weights([(plans[1], down_refs, me_ref, down_s, down_sems), (plans[0], up_refs, me_ref, up_s, up_sems)])
        small_ref[...] = jnp.zeros_like(small_ref)
        ghidden_ref[...] = jnp.zeros_like(ghidden_ref)

    def body(wait):
        grad = grad_ref[...].astype(F32)
        lower = grad.astype(BF)
        gnormed = jnp.zeros(grad.shape, F32)
        for part in part_order(me_ref, plans[0], parts):
            cols = pl.ds(pl.multiple_of(part * chunk, chunk), chunk)
            if wait:
                wait_weight(down_s, down_sems, part)
            gupper = (dot_nn(lower, down_s[part]) * slope_ref[:, cols].astype(F32)).astype(BF)
            gupper_ref[:, cols] = gupper
            ghidden_ref[:, cols] += column_sum(gupper.astype(F32))
            if wait:
                wait_weight(up_s, up_sems, part)
            gnormed = gnormed + dot_nt(gupper, up_s[part])
        unit, root = normalize(middle_ref[...])
        gmiddle = grad + norm_backward(gnormed, unit, root, vec_ref[1:2, :])
        gmiddle_ref[...] = gmiddle
        small_ref[0:1, :] += column_sum(gnormed * unit)
        small_ref[1:2, :] += column_sum(gnormed)
        small_ref[2:3, :] += column_sum(lower.astype(F32))
        small_ref[3:4, :] += column_sum(gmiddle.astype(BF).astype(F32))

    pl.when(first)(functools.partial(body, True))
    pl.when(jnp.logical_not(first))(functools.partial(body, False))


def ffn_backward(me, grad, slope, middle, vec, up_w, down_w, block, parts):
    rows, width = grad.shape
    ffn = slope.shape[1]
    arrays = up_w[1] + down_w[1]
    row_spec = lambda cols: pl.BlockSpec((block, cols), lambda i: (i, 0))
    return pl.pallas_call(
        functools.partial(ffn_backward_kernel, (up_w[0], down_w[0])),
        grid=(rows // block,),
        in_specs=[
            pl.BlockSpec(memory_space=pltpu.SMEM),
            row_spec(width),
            row_spec(ffn),
            row_spec(width),
            pl.BlockSpec(vec.shape, lambda i: (0, 0)),
        ]
        + [pl.BlockSpec(memory_space=pl.ANY)] * len(arrays),
        out_specs=[
            row_spec(ffn),
            row_spec(width),
            pl.BlockSpec((8, width), lambda i: (0, 0)),
            pl.BlockSpec((1, ffn), lambda i: (0, 0)),
        ],
        out_shape=[
            jax.ShapeDtypeStruct((rows, ffn), BF),
            jax.ShapeDtypeStruct((rows, width), F32),
            jax.ShapeDtypeStruct((8, width), F32),
            jax.ShapeDtypeStruct((1, ffn), F32),
        ],
        scratch_shapes=[
            pltpu.VMEM((parts, width, ffn // parts), BF),
            pltpu.VMEM((parts, width, ffn // parts), BF),
            pltpu.SemaphoreType.DMA((parts,)),
            pltpu.SemaphoreType.DMA((parts,)),
        ],
        compiler_params=pltpu.CompilerParams(vmem_limit_bytes=VMEM_LIMIT),
        cost_estimate=pl.CostEstimate(flops=15 * 10**9, bytes_accessed=30 * 10**6, transcendentals=0),
        name="ffn_backward",
    )(me, grad, slope, middle, vec, *arrays)


def ffn_weight_kernel(nffn_ref, grad_ref, gupper_ref, active_ref, out_ref, nffn_t, grad_t):
    @pl.when(pl.program_id(0) == 0)
    def _():
        nffn_t[...] = nffn_ref[...].T
        grad_t[...] = grad_ref[...].astype(BF).T

    shape = (out_ref.shape[0],) + out_ref.shape[3:]
    out_ref[:, 0, 0] = dot_nn(nffn_t[...], gupper_ref[...]).astype(BF).reshape(shape)
    out_ref[:, 0, 1] = dot_nn(grad_t[...], active_ref[...]).astype(BF).reshape(shape)


def ffn_weight(nffn, grad, gupper, active, stripes, parts):
    rows, width = nffn.shape
    piece = gupper.shape[1] // parts
    high = width // stripes
    whole = pl.BlockSpec((rows, width), lambda i: (0, 0))
    return pl.pallas_call(
        ffn_weight_kernel,
        grid=(parts,),
        in_specs=[
            whole,
            whole,
            pl.BlockSpec((rows, piece), lambda i: (0, i)),
            pl.BlockSpec((rows, piece), lambda i: (0, i)),
        ],
        out_specs=pl.BlockSpec((stripes, 1, 2, high, piece), lambda i: (0, i, 0, 0, 0)),
        out_shape=jax.ShapeDtypeStruct((stripes, parts, 2, high, piece), BF),
        scratch_shapes=[pltpu.VMEM((width, rows), BF), pltpu.VMEM((width, rows), BF)],
        compiler_params=pltpu.CompilerParams(vmem_limit_bytes=VMEM_LIMIT),
        cost_estimate=pl.CostEstimate(flops=15 * 10**9, bytes_accessed=30 * 10**6, transcendentals=0),
        name="ffn_weight",
    )(nffn, grad, gupper, active)


def attention_backward_kernel(gmiddle_ref, stream_ref, proj_ref, probs_ref, vec_ref, qkv_s, out_s, *refs):
    gstream_ref, gproj_ref, small_ref, gmixed_s = refs[-4:]

    @pl.when(pl.program_id(0) == 0)
    def _():
        small_ref[...] = jnp.zeros_like(small_ref)

    width = stream_ref.shape[1]
    block_pages, _, slots, _ = probs_ref.shape
    scale = (width // HEADS) ** (-0.5)
    gmiddle = gmiddle_ref[...]
    gmixed_s[...] = dot_nt(gmiddle.astype(BF), out_s[...]).astype(BF)
    lanes = 2 * (width // HEADS)
    for page in range(block_pages):
        rows = slice(page * slots, (page + 1) * slots)
        for pair in range(PAIRS):
            at = pair * lanes
            gmixed = gmixed_s[rows, at : at + lanes]
            queries = split_heads(proj_ref[rows, at : at + lanes])
            keys_in = split_heads(proj_ref[rows, width + at : width + at + lanes])
            values = split_heads(proj_ref[rows, 2 * width + at : 2 * width + at + lanes])
            probs = probs_ref[page, pair]
            gsoft = dot_nt(gmixed, values)
            gscore = []
            for head in range(2):
                cols = slice(head * slots, (head + 1) * slots)
                soft = probs[:, cols].astype(F32)
                grad = gsoft[:, cols]
                inner = jnp.sum(soft * grad, axis=-1, keepdims=True)
                gscore.append((soft * (grad - inner)).astype(BF))
            stacked = jnp.concatenate([probs[:, :slots], probs[:, slots:]], axis=0)
            gvalues = dot_tn(stacked, split_heads(gmixed))
            gqueries = dot_nn(jnp.concatenate(gscore, axis=1), keys_in) * scale
            gkeys = dot_tn(jnp.concatenate(gscore, axis=0), queries) * scale
            gproj_ref[rows, at : at + lanes] = gqueries.astype(BF)
            gproj_ref[rows, width + at : width + at + lanes] = gkeys.astype(BF)
            gproj_ref[rows, 2 * width + at : 2 * width + at + lanes] = gvalues.astype(BF)
    gnormed = dot_nt(gproj_ref[...], qkv_s[...])
    unit, root = normalize(stream_ref[...].astype(F32))
    gstream_ref[...] = gmiddle + norm_backward(gnormed, unit, root, vec_ref[0:1, :])
    small_ref[0:1, :] += column_sum(gnormed * unit)
    small_ref[1:2, :] += column_sum(gnormed)
    small_ref[2:3, :] += column_sum(gproj_ref[:, :width].astype(F32))
    small_ref[3:4, :] += column_sum(gproj_ref[:, 2 * width :].astype(F32))


def attention_backward(gmiddle, stream, proj, probs, vec, weight, block_pages, begin, end, before):
    rows, width = stream.shape
    _, _, slots, _ = probs.shape
    block = block_pages * slots
    first = begin // block_pages
    row_spec = lambda cols: pl.BlockSpec((block, cols), lambda i: (i + first, 0))
    whole = lambda array: pl.BlockSpec(array.shape, lambda i: (0, 0))
    before = [] if before is None else list(before)
    operands = [gmiddle, stream, proj, probs, vec, weight[0], weight[1]]
    return pl.pallas_call(
        attention_backward_kernel,
        grid=((end - begin) // block_pages,),
        in_specs=[
            row_spec(width),
            row_spec(width),
            row_spec(3 * width),
            pl.BlockSpec((block_pages, PAIRS, slots, 2 * slots), lambda i: (i + first, 0, 0, 0)),
            whole(vec),
            whole(weight[0]),
            whole(weight[1]),
        ]
        + [pl.BlockSpec(memory_space=pl.ANY)] * len(before),
        out_specs=[row_spec(width), row_spec(3 * width), pl.BlockSpec((8, width), lambda i: (0, 0))],
        out_shape=[
            jax.ShapeDtypeStruct((rows, width), F32),
            jax.ShapeDtypeStruct((rows, 3 * width), BF),
            jax.ShapeDtypeStruct((8, width), F32),
        ],
        scratch_shapes=[pltpu.VMEM((block, width), BF)],
        input_output_aliases={len(operands) + index: index for index in range(len(before))},
        compiler_params=pltpu.CompilerParams(vmem_limit_bytes=VMEM_LIMIT),
        cost_estimate=pl.CostEstimate(flops=15 * 10**9, bytes_accessed=20 * 10**6, transcendentals=0),
        name="attention_backward",
    )(*operands, *before)


def attention_weight_kernel(normed_ref, mixed_ref, gproj_ref, gmiddle_ref, grad_ref):
    gqkv = dot_tn(normed_ref[...], gproj_ref[...])
    gout = dot_tn(mixed_ref[...], gmiddle_ref[...].astype(BF))
    parts = grad_ref.shape[1]
    cut = gqkv.shape[1] // parts
    rest = gout.shape[1] // parts
    shape = (grad_ref.shape[0],) + grad_ref.shape[3:]
    for part in range(parts):
        qkv_part = gqkv[:, part * cut : (part + 1) * cut].astype(BF)
        out_part = gout[:, part * rest : (part + 1) * rest].astype(BF)
        grad_ref[:, part, 0] = jnp.concatenate([qkv_part, out_part], axis=1).reshape(shape)


def attention_weight(normed, mixed, gproj, gmiddle, stripes, parts):
    rows, width = normed.shape
    block = width // 2
    high = width // stripes
    return pl.pallas_call(
        attention_weight_kernel,
        grid=(2,),
        in_specs=[
            pl.BlockSpec((rows, block), lambda i: (0, i)),
            pl.BlockSpec((rows, block), lambda i: (0, i)),
            pl.BlockSpec((rows, 3 * width), lambda i: (0, 0)),
            pl.BlockSpec((rows, width), lambda i: (0, 0)),
        ],
        out_specs=pl.BlockSpec((stripes // 2, parts, 1, high, width), lambda i: (i, 0, 0, 0, 0)),
        out_shape=jax.ShapeDtypeStruct((stripes, parts, 1, high, width), BF),
        compiler_params=pltpu.CompilerParams(vmem_limit_bytes=VMEM_LIMIT),
        cost_estimate=pl.CostEstimate(flops=10 * 10**9, bytes_accessed=20 * 10**6, transcendentals=0),
        name="attention_weight",
    )(normed, mixed, gproj, gmiddle)


def relative_rows(source, target, me, depth):
    high = source.shape[0] // (2 * depth)
    for x in range(2):
        for z in range(depth):
            start = pl.multiple_of(jnp.bitwise_xor(me, 2 * z + x) * high, 16)
            at = (x * depth + z) * high
            target[at : at + high, :] = source[pl.ds(start, high), :]


def send_out(me_ref, core, y, staged, slot, own_ref, other_ref, sems):
    for x in range(2):
        first, second = plane(me_ref, x, y, core)

        @pl.when(core == 0)
        def _():
            pltpu.make_async_copy(staged.at[slot, x], own_ref.at[second, first], sems.at[slot, x]).start()

        @pl.when(core == 1)
        def _():
            pltpu.make_async_copy(staged.at[slot, x], other_ref.at[second, first], sems.at[slot, x]).start()


def wait_out(staged, slot, own_ref, sems):
    for x in range(2):
        pltpu.make_async_copy(staged.at[slot, x], own_ref.at[0, 0], sems.at[slot, x]).wait()


def ffn_weight_split_kernel(core, me_ref, nffn_ref, grad_ref, gupper_ref, active_ref, out_ref, *refs):
    step = pl.program_id(0)
    staged, sems = refs[-2:]
    _, _, depth, high, width = staged.shape
    high = high // 2
    if core == 1:
        nffn_out, grad_out, turned, nffn_t, grad_t = refs[:-2]
        kept = [
            pltpu.make_async_copy(nffn_t, nffn_out, sems.at[2, 0]),
            pltpu.make_async_copy(grad_t, grad_out, sems.at[2, 1]),
        ]

        @pl.when(step == 0)
        def _():
            turned[...] = nffn_ref[...].T
            relative_rows(turned, nffn_t, me_ref[0], depth)
            turned[...] = grad_ref[...].astype(BF).T
            relative_rows(turned, grad_t, me_ref[0], depth)
            for copy in kept:
                copy.start()
    else:
        nffn_t, grad_t, kept = nffn_ref, grad_ref, []

    shape = (2, depth, high, width)
    staged[step, :, :, :high, :] = dot_nn(nffn_t[...], gupper_ref[...]).astype(BF).reshape(shape)
    staged[step, :, :, high:, :] = dot_nn(grad_t[...], active_ref[...]).astype(BF).reshape(shape)
    for x in range(2):
        first, second = plane(me_ref, x, step, core)
        pltpu.make_async_copy(staged.at[step, x], out_ref.at[second, first], sems.at[step, x]).start()

    @pl.when(step == 1)
    def _():
        wait_out(staged, 0, out_ref, sems)
        wait_out(staged, 1, out_ref, sems)
        for copy in kept:
            copy.wait()


def ffn_weight_split(me, nffn, grad, gupper, active, depth, core):
    rows, piece = gupper.shape[0], gupper.shape[1] // 4
    width = piece
    high = width // (2 * depth)
    whole = lambda array: pl.BlockSpec(array.shape, lambda i, me: (0, 0))
    column = pl.BlockSpec((rows, piece), lambda i, me: (0, jnp.bitwise_xor(me[1], 2 * i + core)))
    shape = (2, 2, depth, 2 * high, piece)
    return pl.pallas_call(
        functools.partial(ffn_weight_split_kernel, core),
        grid_spec=pltpu.PrefetchScalarGridSpec(
            num_scalar_prefetch=1,
            grid=(2,),
            in_specs=[whole(nffn), whole(grad), column, column],
            out_specs=[pl.BlockSpec(memory_space=pl.ANY)] * (1 + 2 * core),
            scratch_shapes=[pltpu.VMEM((width, rows), BF)] * (3 * core)
            + [pltpu.VMEM(shape, BF), pltpu.SemaphoreType.DMA((3, 2))],
        ),
        out_shape=[jax.ShapeDtypeStruct(shape, BF)] + [jax.ShapeDtypeStruct((width, rows), BF)] * (2 * core),
        compiler_params=pltpu.CompilerParams(vmem_limit_bytes=VMEM_LIMIT),
        cost_estimate=pl.CostEstimate(flops=8 * 10**9, bytes_accessed=15 * 10**6, transcendentals=0),
        name="ffn_weight",
    )(me, nffn, grad, gupper, active)


def attention_weight_split_kernel(me_ref, normed_ref, mixed_ref, gproj_ref, gmiddle_ref, *refs):
    other_ref, own_ref, turned, normed_t, mixed_t, found, staged, extra_s, sems = refs[-9:]
    extra_refs = refs[:-9]
    step = pl.program_id(0)
    _, _, depth, rows, width = staged.shape
    high = width // (2 * depth)
    share = width // 4
    shape = (2, depth, high, width)

    @pl.when(step == 0)
    def _():
        turned[...] = mixed_ref[...].T
        relative_rows(turned, mixed_t, me_ref[0], depth)
        found[:, 3 * width :] = dot_nn(mixed_t[...], gmiddle_ref[...].astype(BF)).astype(BF)
        turned[...] = normed_ref[...].T
        relative_rows(turned, normed_t, me_ref[0], depth)
        if extra_refs:
            extra_s[...] = jnp.zeros_like(extra_s)
            for index in range(2):
                one_ref, two_ref, hidden_ref = extra_refs[3 * index : 3 * index + 3]
                sums = jnp.concatenate([one_ref[:4, :], two_ref[:4, :]], axis=0)
                for part in range(4):
                    at = index * (width // 3)
                    extra_s[part, :8, at : at + share] = sums[:, part * share : (part + 1) * share]
                    extra_s[part, 8 + index : 9 + index, :] = hidden_ref[:, part * width : (part + 1) * width]
            for part in range(4):
                extra = extra_s[part].astype(BF)
                staged[part, :, :, high:, :] = jnp.broadcast_to(extra[None, None], (2, depth) + extra.shape)

    def finish(part):
        columns = slice(part * 3 * share, (part + 1) * 3 * share)
        rest = slice(3 * width + part * share, 3 * width + (part + 1) * share)
        staged[part, :, :, :high, :] = jnp.concatenate([found[:, columns], found[:, rest]], axis=1).reshape(shape)
        near = jnp.bitwise_xor(me_ref[1], part)
        send_out(me_ref, near % 2, near // 2, staged, part, own_ref, other_ref, sems)

    for third in range(3):

        @pl.when(step == third)
        def _():
            found[:, third * width : (third + 1) * width] = dot_nn(normed_t[...], gproj_ref[...]).astype(BF)
            for part in ((0,), (1,), (2, 3))[third]:
                finish(part)
            if third == 2:
                for part in range(4):
                    wait_out(staged, part, own_ref, sems)


def attention_weight_split(me, normed, mixed, gproj, gmiddle, depth, extra=None):
    rows, width = normed.shape
    high = width // (2 * depth)
    whole = lambda array: pl.BlockSpec(array.shape, lambda i: (0,) * array.ndim)
    extras = [] if extra is None else list(extra)
    shape = (2, 2, depth, high + (0 if extra is None else 16), width)
    operands = [normed, mixed, gproj, gmiddle] + extras
    return pl.pallas_call(
        attention_weight_split_kernel,
        grid=(3,),
        in_specs=[pl.BlockSpec(memory_space=pltpu.SMEM), whole(normed), whole(mixed)]
        + [pl.BlockSpec((rows, width), lambda i: (0, i))]
        + [whole(operand) for operand in operands[3:]],
        out_specs=[pl.BlockSpec(memory_space=pl.ANY)] * 2,
        out_shape=[jax.ShapeDtypeStruct(shape, BF)] * 2,
        scratch_shapes=[pltpu.VMEM((width, rows), BF)] * 3
        + [
            pltpu.VMEM((width, 4 * width), BF),
            pltpu.VMEM((4,) + shape[1:], BF),
            pltpu.VMEM((4, 16, width), F32),
            pltpu.SemaphoreType.DMA((4, 2)),
        ],
        compiler_params=pltpu.CompilerParams(vmem_limit_bytes=VMEM_LIMIT),
        cost_estimate=pl.CostEstimate(flops=10 * 10**9, bytes_accessed=20 * 10**6, transcendentals=0),
        name="attention_weight",
    )(me, *operands)


def pair_bias(slot_kind, slot_valid, across):
    same_kind = slot_kind[:, :, None] == slot_kind[:, None, :]
    partner = jnp.logical_not(same_kind) if across else same_kind
    allowed = jnp.logical_and(partner, slot_valid[:, None, :] > 0)
    return jnp.where(allowed, 0.0, -1e30).astype(F32)


def ordered_vectors(small_one, small_two):
    picked = (small_one, 0), (small_two, 0), (small_one, 1), (small_one, 2)
    picked += (small_one, 3), (small_two, 3), (small_two, 1), (small_two, 2)
    return jnp.stack([sums[row] for sums, row in picked])


def adam_step(master, grad, moment_one, moment_two, factor, decayed):
    clipped = grad * factor
    first_new = beta_one * moment_one + (1.0 - beta_one) * clipped
    second_new = beta_two * moment_two + (1.0 - beta_two) * clipped * clipped
    change = first_new / bias_one / (jnp.sqrt(second_new / bias_two) + epsilon)
    if decayed:
        change = change + weight_decay * master
    return (-learn_rate * change, first_new, second_new)


def gather_rows(pieces, sizes):
    kinds, high, width = pieces.shape
    rows = lax.all_gather(pieces.reshape(-1, width), ("dp", "tensor"), axis=0, tiled=False)
    if high % 16 == 0:
        return [(("rows", kind * high), [rows]) for kind in range(kinds)]
    split = rows.reshape(sizes["dp"], sizes["tensor"], kinds, high, width)
    return [(("whole",), [jnp.swapaxes(split[:, :, kind], 0, 1).reshape(-1, width, width)]) for kind in range(kinds)]


def scatter_rows(grad, sizes):
    stripes, parts, kinds, high, width = grad.shape
    inner = sizes["dp"] // stripes
    if inner > 1:
        grad = jnp.moveaxis(grad.reshape(stripes, parts, kinds, inner, high // inner, width), 3, 1)
    mine = lax.psum_scatter(grad.reshape(-1, width), ("dp", "tensor"), scatter_dimension=0, tiled=True)
    return mine.reshape(kinds, -1, width).astype(F32)


class Exchange:
    def __init__(self, sizes):
        self.sizes = sizes
        self.depth = sizes["dp"] // 2

    def swap(self, value, partner):
        dp, tensor = self.sizes["dp"], self.sizes["tensor"]
        pairs = []
        for i in range(dp):
            for j in range(tensor):
                far_i, far_j = partner(i, j)
                pairs.append((i * tensor + j, far_i * tensor + far_j))
        return lax.ppermute(value, ("dp", "tensor"), pairs)

    def part(self, bits, value):
        return self.swap(value, lambda i, j: (i, j ^ bits))

    def core(self, value):
        return self.part(1, value)

    def x(self, value):
        return self.swap(value, lambda i, j: (i ^ 1, j))

    def y(self, value):
        return self.part(2, value)

    def diagonal(self, value):
        return self.swap(value, lambda i, j: (i ^ 1, j ^ 2))

    def first(self, value):
        return self.swap(value, lambda i, j: (i, j ^ 2) if j & 1 else (i ^ 1, j))

    def second(self, value):
        return self.swap(value, lambda i, j: (i ^ 1, j) if j & 1 else (i, j ^ 2))

    def z(self, distance, value):
        return self.swap(value, lambda i, j: (i ^ (2 * distance), j))

    def z_sends(self, values):
        return [(functools.partial(self.z, distance), values[distance]) for distance in range(1, self.depth)]

    def gather_z(self, piece):
        groups = [[2 * z + x for z in range(self.depth)] for x in range(2)]
        return lax.all_gather(piece, "dp", axis=0, tiled=False, axis_index_groups=groups)

    def total(self, value):
        value = value + self.core(value)
        value = value + self.y(value)
        value = value + self.x(value)
        bit = 1
        while bit < self.depth:
            value = value + self.z(bit, value)
            bit *= 2
        return value


def tie(values, after):
    return lax.optimization_barrier((values, after))[0]


class Spread:
    def __init__(self, exchange, quad, fixed):
        self.exchange, self.quad, self.fixed = exchange, quad, fixed

    def go_first(self):
        return [(self.exchange.first, self.quad)]

    def go_second(self, came):
        self.pair = jnp.stack([self.quad, came[0]])
        return [(self.exchange.second, self.pair), (self.exchange.core, self.pair)]

    def go_core(self, came):
        self.two, self.far_pair = came
        return [(self.exchange.core, self.two)]

    def weight(self, came, offset=0):
        positions = [[(0, second, core), (1, second, core)] for core in range(2) for second in range(2)]
        arrays = [self.pair, self.two, self.far_pair, came[0]]
        return (("near", offset, positions, self.fixed), arrays)


class Reduce:
    def __init__(self, exchange, other, own):
        self.exchange, self.other, self.own = exchange, other, own

    def wide(self, value):
        return value.astype(F32)

    def go_core(self):
        return [(self.exchange.core, self.other)]

    def go_second(self, came):
        self.came = came[0]
        value = (self.wide(self.own[1]) + self.wide(self.came[1])).astype(BF)
        return [(self.exchange.second, value)]

    def go_first(self, came):
        self.beside = came[0]
        value = self.wide(self.own[0, 1]) + self.wide(self.came[0, 1]) + self.wide(self.beside[1])
        return [(self.exchange.first, value.astype(BF))]

    def depths(self, came):
        ahead = came[0]
        return (
            self.wide(self.own[0, 0]) + self.wide(self.came[0, 0]) + self.wide(self.beside[0]) + self.wide(ahead)
        )


def mid_first(sends):
    at = (len(sends) + 1) // 2 - 1
    return sends[at : at + 1] + sends[:at] + sends[at + 1 :]


class Lane:
    def __init__(self):
        self.last = None

    def after_last(self, values):
        return values if self.last is None else tie(values, self.last)

    def step(self, sends, kernel=None, arrays=()):
        values = [value for _, value in sends]
        values, arrays = self.after_last((values, list(arrays)))
        came = [move(value) for (move, _), value in zip(sends, values)]
        results = [] if kernel is None else list(kernel(*arrays))
        came, results = lax.optimization_barrier((came, results))
        self.last = results[-1] if results else came[-1]
        return came, results


def shards(
    sizes,
    tokens, out_grad, slot_kind, slot_valid,
    qkv_weight, qkv_first, qkv_second,
    out_weight, out_first, out_second,
    up_weight, up_first, up_second,
    down_weight, down_first, down_second,
    gain_weight, gain_first, gain_second,
    bias_weight, bias_first, bias_second,
    hidden_weight, hidden_first, hidden_second,
):
    parts = sizes["tensor"]
    width = tokens.shape[1]
    cut = qkv_weight.shape[2]
    high = qkv_weight.shape[1]
    split = parts == 4 and high % 32 == 0 and sizes["dp"] in (4, 8, 16)
    exchange = Exchange(sizes)
    stripes = sizes["dp"] if high % 16 == 0 else 2
    me = jnp.stack([lax.axis_index("dp"), lax.axis_index("tensor")]).astype(jnp.int32)
    attn_pieces = jnp.concatenate([qkv_weight.astype(BF), out_weight.astype(BF)], axis=2)
    up_pieces = up_weight.astype(BF)
    down_pieces = jnp.swapaxes(down_weight.astype(BF), 1, 2)
    pages = slot_kind.shape[0]
    block_pages = 2 if pages % 2 == 0 else 1
    block = block_pages * slot_kind.shape[1]
    masks = [pair_bias(slot_kind, slot_valid, index == 0) for index in range(2)]
    lane = Lane()
    gathered = lambda index: gather_rows(
        jnp.stack([attn_pieces[index], up_pieces[index], down_pieces[index]]), sizes
    )
    small = hidden = None
    saved = [None, None]

    def attention_forward_of(index, weight):
        return lambda stream: attention_forward(
            me, stream, masks[index], small[index], weight, block_pages, parts
        )

    def ffn_forward_of(index, up_w, down_w):
        return lambda nffn, middle: ffn_forward(
            me, nffn, middle, small[index], hidden[index : index + 1], up_w, down_w, block, parts
        )

    def ffn_backward_of(index):
        kept = saved[index]
        return lambda grad: ffn_backward(
            me, grad, kept["slope"], kept["middle"], small[index], kept["up_w"], kept["down_w"], block, parts
        )

    def ffn_weight_of(index, grad, turned=None):
        kept = saved[index]
        if not split:
            return lambda gupper: (ffn_weight(kept["nffn"], grad, gupper, kept["active"], stripes, parts),)
        core = 1 if turned is None else 0
        left, right = (kept["nffn"], grad) if turned is None else turned
        return lambda gupper: ffn_weight_split(me, left, right, gupper, kept["active"], exchange.depth, core)

    def attention_backward_of(index, begin, end, before=None):
        kept = saved[index]
        return lambda gmiddle: attention_backward(
            gmiddle, kept["stream"], kept["proj"], kept["probs"], small[index], kept["weight"],
            block_pages, begin, end, before,
        )

    def attention_weight_of(index, gmiddle, extra=None):
        kept = saved[index]
        if split:
            return lambda gproj: attention_weight_split(
                me, kept["normed"], kept["mixed"], gproj, gmiddle, exchange.depth, extra
            )
        return lambda gproj: (attention_weight(kept["normed"], kept["mixed"], gproj, gmiddle, stripes, parts),)

    def keep(index, stream, attention, ffn):
        middle, nffn, normed, proj, probs, mixed, qkv_w, out_w = attention
        saved[index] = dict(
            stream=stream, middle=middle, nffn=nffn, normed=normed, proj=proj, probs=probs, mixed=mixed,
            weight=(qkv_w, out_w), active=ffn[1], slope=ffn[2], up_w=(("whole",), [ffn[3]]), down_w=(("whole",), [ffn[4]]),
        )

    if split:
        depth = exchange.depth
        late = jnp.concatenate([attn_pieces[1], up_pieces[1], down_pieces[1]], axis=0)
        own_small = jnp.concatenate(
            [gain_weight, bias_weight, hidden_weight.reshape(2, -1, gain_weight.shape[2])], axis=1
        )
        own_small = lax.reduce_precision(own_small, 8, 7)
        small_sends = [(functools.partial(exchange.part, bits), own_small) for bits in range(1, 4)]
        late = exchange.gather_z(late)
        came, _ = lane.step(exchange.z_sends([attn_pieces[0]] * depth))
        attn_zero = Spread(exchange, jnp.stack([attn_pieces[0]] + came), False)
        ffn_piece = jnp.concatenate([up_pieces[0], down_pieces[0]], axis=0)
        ffn_sends = exchange.z_sends([ffn_piece] * depth)
        middle_at = depth // 2 - 1
        came, _ = lane.step(attn_zero.go_first() + ffn_sends[middle_at : middle_at + 1] + small_sends)
        ffn_came = came[1:2]
        mine = lax.axis_index("tensor")

        def order_small(*values):
            every = jnp.zeros((4,) + own_small.shape, F32)
            for bits, value in enumerate(values):
                every = lax.dynamic_update_slice_in_dim(every, value[None], jnp.bitwise_xor(mine, bits), 0)
            small = jnp.moveaxis(every[:, :, :8], 0, 2).reshape(2, 8, width)
            return small[0], small[1], jnp.moveaxis(every[:, :, 8:], 0, 1).reshape(2, -1)

        ffn_sends = ffn_sends[:middle_at] + ffn_sends[middle_at + 1 :]
        came, results = lane.step(attn_zero.go_second(came[:1]) + ffn_sends, order_small, [own_small] + came[2:])
        small, hidden = results[:2], results[2]
        others = came[2:]
        others.insert(middle_at, ffn_came[0])
        ffn_zero = Spread(exchange, jnp.stack([ffn_piece] + others), False)
        came, _ = lane.step(attn_zero.go_core(came[:2]) + ffn_zero.go_first())
        attn_w = attn_zero.weight(came[:1])
        came, attention = lane.step(ffn_zero.go_second(came[1:]), attention_forward_of(0, attn_w), [tokens])
        late = lane.after_last(late)
        attn_one = Spread(exchange, late[:, :high], True)
        ffn_one = Spread(exchange, late[:, high:], True)
        came, _ = lane.step(ffn_zero.go_core(came) + attn_one.go_first())
        up_w, down_w = ffn_zero.weight(came[:1]), ffn_zero.weight(came[:1], high)
        came, ffn = lane.step(
            attn_one.go_second(came[1:]) + ffn_one.go_first(), ffn_forward_of(0, up_w, down_w), attention[1::-1]
        )
        keep(0, tokens, attention, ffn)
        stream = ffn[0]
        ffn_came = came[2:]
        came, _ = lane.step(attn_one.go_core(came[:2]))
        attn_w = attn_one.weight(came)
        came, attention = lane.step(ffn_one.go_second(ffn_came), attention_forward_of(1, attn_w), [stream])
        came, _ = lane.step(ffn_one.go_core(came))
        up_w, down_w = ffn_one.weight(came), ffn_one.weight(came, high)
        _, ffn = lane.step([], ffn_forward_of(1, up_w, down_w), attention[1::-1])
        keep(1, stream, attention, ffn)
        block_output = ffn[0]

        _, (gupper, gmiddle, small_two, hidden_one) = lane.step([], ffn_backward_of(1), [out_grad])
        _, (other, *turned) = lane.step([], ffn_weight_of(1, out_grad), [gupper])
        came, (own,) = lane.step([(exchange.core, other)], ffn_weight_of(1, out_grad, turned), [gupper])
        ffn_one = Reduce(exchange, other, own)
        came, (grad, gproj, small_one) = lane.step(
            ffn_one.go_second(came), attention_backward_of(1, 0, pages), [gmiddle]
        )
        sums_one = (small_one, small_two, hidden_one)
        came, grads = lane.step(ffn_one.go_first(came), attention_weight_of(1, gmiddle), [gproj])
        ffn_layers = ffn_one.depths(came)
        ffn_sends = mid_first(exchange.z_sends([ffn_layers[z].astype(BF) for z in range(depth)]))
        attn_one = Reduce(exchange, *grads)
        came, results = lane.step(attn_one.go_core() + ffn_sends[:1], ffn_backward_of(0), [grad])
        ffn_came = came[1:]
        gupper, gmiddle, small_two, hidden_zero = results
        came, (other, *turned) = lane.step(
            attn_one.go_second(came[:1]) + ffn_sends[1:], ffn_weight_of(0, grad), [gupper]
        )
        ffn_came = ffn_came + came[1:]
        total = ffn_layers[0] + sum(value.astype(F32) for value in ffn_came)
        grad_up, grad_down = [None, total[:high]], [None, total[high:]]
        came, (own,) = lane.step(
            [(exchange.core, other)] + attn_one.go_first(came[:1]), ffn_weight_of(0, grad, turned), [gupper]
        )
        ffn_zero = Reduce(exchange, other, own)
        attn_layers = attn_one.depths(came[1:])
        attn_sends = mid_first(exchange.z_sends([attn_layers[z].astype(BF) for z in range(depth)]))
        came, (input_grad, gproj, small_one) = lane.step(
            ffn_zero.go_second(came[:1]) + attn_sends[:1], attention_backward_of(0, 0, pages), [gmiddle]
        )
        attn_came = came[1:]
        came, grads = lane.step(
            ffn_zero.go_first(came[:1]) + attn_sends[1:],
            attention_weight_of(0, gmiddle, (small_one, small_two, hidden_zero) + sums_one),
            [gproj],
        )
        grad_attn = [None, attn_layers[0] + sum(value.astype(F32) for value in attn_came + came[1:])]
        layers = ffn_zero.depths(came[:1])
        ffn_sends = exchange.z_sends([layers[z].astype(BF) for z in range(depth)])
        ffn_sends = mid_first(ffn_sends)
        attn_zero = Reduce(exchange, *grads)
        came, _ = lane.step(attn_zero.go_core())
        came, _ = lane.step(attn_zero.go_second(came) + ffn_sends[:1])
        ffn_came = came[1:]
        came, _ = lane.step(attn_zero.go_first(came[:1]) + ffn_sends[1:])
        total = layers[0] + sum(value.astype(F32) for value in ffn_came + came[1:])
        grad_up[0], grad_down[0] = total[:high], total[high:]
        layers = attn_zero.depths(came[:1])
        came, _ = lane.step(exchange.z_sends([layers[z].astype(BF) for z in range(depth)]))
        total = layers[0] + sum(value.astype(F32) for value in came)
        grad_attn[0] = total[:high]
        shared_squares = jnp.sum(total[high:] * total[high:])
        share = width // parts
        vectors = []
        for at in (0, width // 3):
            sums = total[high : high + 8, at : at + share]
            vectors.append(ordered_vectors(sums[:4], sums[4:]))
        vectors = jnp.stack(vectors)
        grad_hidden = total[high + 8 : high + 10]
    else:
        small = jnp.concatenate([gain_weight, bias_weight], axis=1).astype(BF)
        small = lax.all_gather(small, "tensor", axis=2, tiled=True).astype(F32)
        hidden = lax.all_gather(hidden_weight.astype(BF), "tensor", axis=1, tiled=True).astype(F32)
        stream = tokens
        for index in range(2):
            attn_w, up_w, down_w = gathered(index)
            attention = attention_forward_of(index, attn_w)(stream)
            ffn = ffn_forward_of(index, up_w, down_w)(*attention[1::-1])
            keep(index, stream, attention, ffn)
            stream = ffn[0]
        block_output = stream
        grad = out_grad
        grad_attn, grad_up, grad_down, vectors, grad_hidden = ([None, None] for _ in range(5))
        for index in (1, 0):
            gupper, gmiddle, small_two, grad_hidden[index] = ffn_backward_of(index)(grad)
            (gffn,) = ffn_weight_of(index, grad)(gupper)
            grad_up[index], grad_down[index] = scatter_rows(gffn, sizes)
            grad, gproj, small_one = attention_backward_of(index, 0, pages)(gmiddle)
            (grad_attn[index],) = scatter_rows(attention_weight_of(index, gmiddle)(gproj)[0], sizes)
            vectors[index] = ordered_vectors(small_one, small_two)
        input_grad = grad
        vectors, grad_hidden = lax.psum((jnp.stack(vectors), jnp.concatenate(grad_hidden, axis=0)), ("dp", "tensor"))
        at = lax.axis_index("tensor")
        slice_of = lambda whole: lax.dynamic_slice_in_dim(
            whole, at * (whole.shape[-1] // parts), whole.shape[-1] // parts, whole.ndim - 1
        )
        vectors, grad_hidden = slice_of(vectors), slice_of(grad_hidden)
        shared_squares = jnp.sum(vectors * vectors) + jnp.sum(grad_hidden * grad_hidden)
    grad_gain, grad_bias = vectors[:, :2], vectors[:, 2:]
    local_squares = sum(jnp.sum(grad * grad) for pair in (grad_up, grad_down, grad_attn) for grad in pair[::-1])
    grad_attn, grad_up, grad_down = jnp.stack(grad_attn), jnp.stack(grad_up), jnp.stack(grad_down)
    local_squares = local_squares + jnp.where(lax.axis_index("dp") == 0, shared_squares, 0.0)
    grad_down = jnp.swapaxes(grad_down, 1, 2)
    if split:
        total_squares = exchange.total(local_squares.reshape(1, 1))[0, 0]
    else:
        total_squares = lax.psum(local_squares, ("dp", "tensor"))
    grad_norm = jnp.sqrt(total_squares)
    factor = clip_norm / jnp.maximum(grad_norm, clip_norm)
    masters = (qkv_weight, out_weight, up_weight, down_weight, gain_weight, bias_weight, hidden_weight)
    firsts = (qkv_first, out_first, up_first, down_first, gain_first, bias_first, hidden_first)
    seconds = (qkv_second, out_second, up_second, down_second, gain_second, bias_second, hidden_second)
    gradients = (
        grad_attn[:, :, :cut], grad_attn[:, :, cut:], grad_up, grad_down, grad_gain, grad_bias, grad_hidden,
    )
    results = [block_output, input_grad, grad_norm]
    for member in range(7):
        update, first_new, second_new = adam_step(
            masters[member], gradients[member], firsts[member], seconds[member], factor, member < 4
        )
        results = results + [gradients[member], update, first_new, second_new]
    return tuple(results)


def solution(mesh):
    rows = P(("dp", "tensor"), None)
    matrix = P(None, "dp", "tensor")
    turned = P(None, "tensor", "dp")
    vectors = P(None, None, "tensor")
    hidden = P(None, "tensor")
    return jax.shard_map(
        functools.partial(shards, dict(mesh.shape)),
        mesh=mesh,
        in_specs=(rows,) * 4 + (matrix,) * 9 + (turned,) * 3 + (vectors,) * 6 + (hidden,) * 3,
        out_specs=(rows, rows, P()) + (matrix,) * 12 + (turned,) * 4 + (vectors,) * 8 + (hidden,) * 4,
        check_vma=False,
    )
```

```python
import functools

import jax
import jax.numpy as jnp
from jax import lax
from jax.experimental import pallas as pl
from jax.experimental.pallas import tpu as pltpu
from jax.sharding import PartitionSpec as P

HEADS = 12
PAIRS = HEADS // 2

beta_one = 0.9
beta_two = 0.99
learn_rate = 0.01
weight_decay = 0.01
epsilon = 1e-08
clip_norm = 1.0
bias_one = 1.0 - beta_one**10
bias_two = 1.0 - beta_two**10

BF = jnp.bfloat16
F32 = jnp.float32
VMEM_LIMIT = 56 * 1024 * 1024


def dot_nn(a, b):
    return lax.dot_general(a, b, (((1,), (0,)), ((), ())), preferred_element_type=F32)


def dot_nt(a, b):
    return lax.dot_general(a, b, (((1,), (1,)), ((), ())), preferred_element_type=F32)


def dot_tn(a, b):
    return lax.dot_general(a, b, (((0,), (0,)), ((), ())), preferred_element_type=F32)


def normalize(stream):
    average = jnp.mean(stream, axis=-1, keepdims=True)
    centered = stream - average
    spread = jnp.mean(centered * centered, axis=-1, keepdims=True)
    root = lax.rsqrt(spread + 1e-05)
    return centered * root, root


def norm_backward(grad, unit, root, gain):
    scaled = grad * gain
    first = jnp.mean(scaled, axis=-1, keepdims=True)
    second = jnp.mean(scaled * unit, axis=-1, keepdims=True)
    return root * (scaled - first - unit * second)


def column_sum(value):
    return jnp.sum(value, axis=0, keepdims=True)


def split_heads(pair):
    lane = lax.broadcasted_iota(jnp.int32, pair.shape, 1)
    zero = jnp.zeros_like(pair)
    half = pair.shape[1] // 2
    return jnp.concatenate([jnp.where(lane < half, pair, zero), jnp.where(lane >= half, pair, zero)], axis=0)


def plane(me_ref, first, second, core):
    turned = jnp.bitwise_xor(jnp.bitwise_and(me_ref[1], 1), core) == 1
    return jnp.where(turned, second, first), jnp.where(turned, first, second)


def weight_copies(plan, refs, me_ref, full, sems):
    copies = []

    def add(source, part, rows):
        copies.append(pltpu.make_async_copy(source, full.at[part, rows, :], sems.at[part]))

    parts, width, _ = full.shape
    if plan[0] == "whole":
        for part in range(parts):
            add(refs[0].at[part], part, pl.ds(0, width))
    elif plan[0] == "rows":
        high = width * parts // refs[0].shape[0]
        for index in range(refs[0].shape[0]):
            stripe, part = divmod(index, parts)
            add(refs[0].at[index, pl.ds(plan[1], high), :], part, pl.ds(stripe * high, high))
    else:
        for ref, positions in zip(refs, plan[2]):
            depth = ref.shape[1]
            high = width // (2 * depth)
            for place, (first, second, core) in enumerate(positions):
                x, y = plane(me_ref, first, second, core)
                part = jnp.bitwise_xor(me_ref[1], 2 * y + core)
                if plan[3]:
                    side = jnp.bitwise_xor(jnp.bitwise_and(me_ref[0], 1), x)
                    stripes = full.reshape(parts, depth, 2, high, width).at[part, :, side]
                    source = ref.at[place, :, pl.ds(plan[1], high), :]
                    copies.append(pltpu.make_async_copy(source, stripes, sems.at[part]))
                    continue
                for z in range(depth):
                    start = pl.multiple_of(jnp.bitwise_xor(me_ref[0], 2 * z + x) * high, 16)
                    add(ref.at[place, z, pl.ds(plan[1], high), :], part, pl.ds(start, high))
    return copies


def start_weights(groups):
    for together in zip(*[weight_copies(*group) for group in groups]):
        for copy in together:
            copy.start()


def wait_weight(full, sems, part):
    pltpu.make_async_copy(full.at[part], full.at[part], sems.at[part]).wait()


def part_order(me_ref, plan, parts):
    if plan[0] != "near":
        return list(range(parts))
    return [jnp.bitwise_xor(me_ref[1], near) for near in (0, 2, 1, 3)]


def split_attention(raw, qkv_s, out_s):
    parts = raw.shape[0]
    cut = qkv_s.shape[1] // parts
    step = 96

    def relay(index, _):
        rows = pl.ds(pl.multiple_of(index * step, step), step)
        pieces = [raw[part, rows, :] for part in range(parts)]
        qkv_s[rows, :] = jnp.concatenate([piece[:, :cut] for piece in pieces], axis=1)
        out_s[rows, :] = jnp.concatenate([piece[:, cut:] for piece in pieces], axis=1)
        return 0

    lax.fori_loop(0, raw.shape[1] // step, relay, 0)


def attention_forward_kernel(plan, me_ref, stream_ref, mask_ref, vec_ref, *refs):
    weight_refs = refs[:-10]
    middle_ref, nffn_ref, normed_ref, proj_ref, probs_ref, mixed_ref, qkv_s, out_s, raw, sems = refs[-10:]

    @pl.when(pl.program_id(0) == 0)
    def _():
        start_weights([(plan, weight_refs, me_ref, raw, sems)])
        for part in range(raw.shape[0]):
            wait_weight(raw, sems, part)
        split_attention(raw, qkv_s, out_s)

    width = stream_ref.shape[1]
    slots = mask_ref.shape[1]
    scale = (width // HEADS) ** (-0.5)
    stream = stream_ref[...].astype(F32)
    unit, _ = normalize(stream)
    normed = (unit * vec_ref[0:1, :] + vec_ref[2:3, :]).astype(BF)
    normed_ref[...] = normed
    projected = dot_nn(normed, qkv_s[...])
    proj_ref[:, :width] = (projected[:, :width] + vec_ref[3:4, :]).astype(BF)
    proj_ref[:, width : 2 * width] = projected[:, width : 2 * width].astype(BF)
    proj_ref[:, 2 * width :] = (projected[:, 2 * width :] + vec_ref[4:5, :]).astype(BF)
    lanes = 2 * (width // HEADS)
    for page in range(mask_ref.shape[0]):
        rows = slice(page * slots, (page + 1) * slots)
        bias = mask_ref[page]
        for pair in range(PAIRS):
            at = pair * lanes
            queries = proj_ref[rows, at : at + lanes] * jnp.asarray(scale, BF)
            keys_in = split_heads(proj_ref[rows, width + at : width + at + lanes])
            values = split_heads(proj_ref[rows, 2 * width + at : 2 * width + at + lanes])
            scores = dot_nt(queries, keys_in)
            soft = []
            for head in range(2):
                masked = scores[:, head * slots : (head + 1) * slots] + bias
                peak = jnp.max(masked, axis=-1, keepdims=True)
                exponent = jnp.exp(masked - peak)
                total = jnp.sum(exponent, axis=-1, keepdims=True)
                soft.append((exponent * (1.0 / total)).astype(BF))
            probs = jnp.concatenate(soft, axis=1)
            probs_ref[page, pair] = probs
            mixed_ref[rows, at : at + lanes] = dot_nn(probs, values).astype(BF)
    middle = stream + dot_nn(mixed_ref[...], out_s[...]) + vec_ref[5:6, :]
    middle_ref[...] = middle
    unit, _ = normalize(middle)
    nffn_ref[...] = (unit * vec_ref[1:2, :] + vec_ref[6:7, :]).astype(BF)


def attention_forward(me, stream, mask, vec, weight, block_pages, parts):
    plan, arrays = weight
    rows, width = stream.shape
    pages, slots, _ = mask.shape
    block = block_pages * slots
    row_spec = lambda cols: pl.BlockSpec((block, cols), lambda i: (i, 0))
    return pl.pallas_call(
        functools.partial(attention_forward_kernel, plan),
        grid=(pages // block_pages,),
        in_specs=[
            pl.BlockSpec(memory_space=pltpu.SMEM),
            row_spec(width),
            pl.BlockSpec((block_pages, slots, slots), lambda i: (i, 0, 0)),
            pl.BlockSpec(vec.shape, lambda i: (0, 0)),
        ]
        + [pl.BlockSpec(memory_space=pl.ANY)] * len(arrays),
        out_specs=[
            row_spec(width),
            row_spec(width),
            row_spec(width),
            row_spec(3 * width),
            pl.BlockSpec((block_pages, PAIRS, slots, 2 * slots), lambda i: (i, 0, 0, 0)),
            row_spec(width),
            pl.BlockSpec((width, 3 * width), lambda i: (0, 0)),
            pl.BlockSpec((width, width), lambda i: (0, 0)),
        ],
        out_shape=[
            jax.ShapeDtypeStruct((rows, width), F32),
            jax.ShapeDtypeStruct((rows, width), BF),
            jax.ShapeDtypeStruct((rows, width), BF),
            jax.ShapeDtypeStruct((rows, 3 * width), BF),
            jax.ShapeDtypeStruct((pages, PAIRS, slots, 2 * slots), BF),
            jax.ShapeDtypeStruct((rows, width), BF),
            jax.ShapeDtypeStruct((width, 3 * width), BF),
            jax.ShapeDtypeStruct((width, width), BF),
        ],
        scratch_shapes=[
            pltpu.VMEM((parts, width, width), BF),
            pltpu.SemaphoreType.DMA((parts,)),
        ],
        compiler_params=pltpu.CompilerParams(vmem_limit_bytes=VMEM_LIMIT),
        cost_estimate=pl.CostEstimate(flops=20 * 10**9, bytes_accessed=30 * 10**6, transcendentals=0),
        name="attention_forward",
    )(me, stream, mask, vec, *arrays)


def ffn_forward_kernel(plans, me_ref, nffn_ref, middle_ref, vec_ref, hidden_ref, *refs):
    result_ref, active_ref, slope_ref, up_ref, down_ref, up_s, down_s, up_sems, down_sems = refs[-9:]
    up_refs = refs[: (len(refs) - 9) // 2]
    down_refs = refs[len(up_refs) : -9]
    kept = [pltpu.make_async_copy(up_s, up_ref, up_sems.at[0]), pltpu.make_async_copy(down_s, down_ref, down_sems.at[0])]

    first = pl.program_id(0) == 0
    parts, _, chunk = up_s.shape
    curve = 0.7978845608028654

    @pl.when(first)
    def _():
        start_weights([(plans[0], up_refs, me_ref, up_s, up_sems), (plans[1], down_refs, me_ref, down_s, down_sems)])

    def body(wait):
        nffn = nffn_ref[...]
        total = middle_ref[...] + vec_ref[7:8, :]
        for part in part_order(me_ref, plans[0], parts):
            cols = pl.ds(pl.multiple_of(part * chunk, chunk), chunk)
            if wait:
                wait_weight(up_s, up_sems, part)
            upper = dot_nn(nffn, up_s[part]) + hidden_ref[:, cols]
            square = upper * upper
            angle = jnp.tanh(upper * (curve + (curve * 0.044715) * square))
            half = 0.5 * upper
            lift = 1.0 + angle
            active = (half * lift).astype(BF)
            slope = 0.5 * lift + half * (1.0 - angle * angle) * (curve + (3.0 * curve * 0.044715) * square)
            active_ref[:, cols] = active
            slope_ref[:, cols] = slope.astype(BF)
            if wait:
                wait_weight(down_s, down_sems, part)
            total = total + dot_nt(active, down_s[part])
        result_ref[...] = total
        if wait:
            for copy in kept:
                copy.start()

    pl.when(first)(functools.partial(body, True))
    pl.when(jnp.logical_not(first))(functools.partial(body, False))

    @pl.when(pl.program_id(0) == pl.num_programs(0) - 1)
    def _():
        for copy in kept:
            copy.wait()


def ffn_forward(me, nffn, middle, vec, hidden, up_w, down_w, block, parts):
    rows, width = nffn.shape
    ffn = hidden.shape[1]
    arrays = up_w[1] + down_w[1]
    row_spec = lambda cols: pl.BlockSpec((block, cols), lambda i: (i, 0))
    return pl.pallas_call(
        functools.partial(ffn_forward_kernel, (up_w[0], down_w[0])),
        grid=(rows // block,),
        in_specs=[
            pl.BlockSpec(memory_space=pltpu.SMEM),
            row_spec(width),
            row_spec(width),
            pl.BlockSpec(vec.shape, lambda i: (0, 0)),
            pl.BlockSpec(hidden.shape, lambda i: (0, 0)),
        ]
        + [pl.BlockSpec(memory_space=pl.ANY)] * len(arrays),
        out_specs=[row_spec(width), row_spec(ffn), row_spec(ffn)] + [pl.BlockSpec(memory_space=pl.ANY)] * 2,
        out_shape=[
            jax.ShapeDtypeStruct((rows, width), F32),
            jax.ShapeDtypeStruct((rows, ffn), BF),
            jax.ShapeDtypeStruct((rows, ffn), BF),
        ]
        + [jax.ShapeDtypeStruct((parts, width, ffn // parts), BF)] * 2,
        scratch_shapes=[
            pltpu.VMEM((parts, width, ffn // parts), BF),
            pltpu.VMEM((parts, width, ffn // parts), BF),
            pltpu.SemaphoreType.DMA((parts,)),
            pltpu.SemaphoreType.DMA((parts,)),
        ],
        compiler_params=pltpu.CompilerParams(vmem_limit_bytes=VMEM_LIMIT),
        cost_estimate=pl.CostEstimate(flops=15 * 10**9, bytes_accessed=30 * 10**6, transcendentals=0),
        name="ffn_forward",
    )(me, nffn, middle, vec, hidden, *arrays)


def ffn_backward_kernel(plans, me_ref, grad_ref, slope_ref, middle_ref, vec_ref, *refs):
    gupper_ref, gmiddle_ref, small_ref, ghidden_ref, up_s, down_s, up_sems, down_sems = refs[-8:]
    up_refs = refs[: (len(refs) - 8) // 2]
    down_refs = refs[len(up_refs) : -8]

    first = pl.program_id(0) == 0
    parts, _, chunk = up_s.shape

    @pl.when(first)
    def _():
        start_weights([(plans[1], down_refs, me_ref, down_s, down_sems), (plans[0], up_refs, me_ref, up_s, up_sems)])
        small_ref[...] = jnp.zeros_like(small_ref)
        ghidden_ref[...] = jnp.zeros_like(ghidden_ref)

    def body(wait):
        grad = grad_ref[...].astype(F32)
        lower = grad.astype(BF)
        gnormed = jnp.zeros(grad.shape, F32)
        for part in part_order(me_ref, plans[0], parts):
            cols = pl.ds(pl.multiple_of(part * chunk, chunk), chunk)
            if wait:
                wait_weight(down_s, down_sems, part)
            gupper = (dot_nn(lower, down_s[part]) * slope_ref[:, cols].astype(F32)).astype(BF)
            gupper_ref[:, cols] = gupper
            ghidden_ref[:, cols] += column_sum(gupper.astype(F32))
            if wait:
                wait_weight(up_s, up_sems, part)
            gnormed = gnormed + dot_nt(gupper, up_s[part])
        unit, root = normalize(middle_ref[...])
        gmiddle = grad + norm_backward(gnormed, unit, root, vec_ref[1:2, :])
        gmiddle_ref[...] = gmiddle
        small_ref[0:1, :] += column_sum(gnormed * unit)
        small_ref[1:2, :] += column_sum(gnormed)
        small_ref[2:3, :] += column_sum(lower.astype(F32))
        small_ref[3:4, :] += column_sum(gmiddle.astype(BF).astype(F32))

    pl.when(first)(functools.partial(body, True))
    pl.when(jnp.logical_not(first))(functools.partial(body, False))


def ffn_backward(me, grad, slope, middle, vec, up_w, down_w, block, parts):
    rows, width = grad.shape
    ffn = slope.shape[1]
    arrays = up_w[1] + down_w[1]
    row_spec = lambda cols: pl.BlockSpec((block, cols), lambda i: (i, 0))
    return pl.pallas_call(
        functools.partial(ffn_backward_kernel, (up_w[0], down_w[0])),
        grid=(rows // block,),
        in_specs=[
            pl.BlockSpec(memory_space=pltpu.SMEM),
            row_spec(width),
            row_spec(ffn),
            row_spec(width),
            pl.BlockSpec(vec.shape, lambda i: (0, 0)),
        ]
        + [pl.BlockSpec(memory_space=pl.ANY)] * len(arrays),
        out_specs=[
            row_spec(ffn),
            row_spec(width),
            pl.BlockSpec((8, width), lambda i: (0, 0)),
            pl.BlockSpec((1, ffn), lambda i: (0, 0)),
        ],
        out_shape=[
            jax.ShapeDtypeStruct((rows, ffn), BF),
            jax.ShapeDtypeStruct((rows, width), F32),
            jax.ShapeDtypeStruct((8, width), F32),
            jax.ShapeDtypeStruct((1, ffn), F32),
        ],
        scratch_shapes=[
            pltpu.VMEM((parts, width, ffn // parts), BF),
            pltpu.VMEM((parts, width, ffn // parts), BF),
            pltpu.SemaphoreType.DMA((parts,)),
            pltpu.SemaphoreType.DMA((parts,)),
        ],
        compiler_params=pltpu.CompilerParams(vmem_limit_bytes=VMEM_LIMIT),
        cost_estimate=pl.CostEstimate(flops=15 * 10**9, bytes_accessed=30 * 10**6, transcendentals=0),
        name="ffn_backward",
    )(me, grad, slope, middle, vec, *arrays)


def ffn_both_kernel(plans, me_ref, nffn_ref, middle_ref, grad_ref, vec_ref, hidden_ref, *refs):
    result_ref, active_ref, gupper_ref, gmiddle_ref, small_ref, ghidden_ref, up_s, down_s, up_sems, down_sems = refs[-10:]
    up_refs = refs[: (len(refs) - 10) // 2]
    down_refs = refs[len(up_refs) : -10]
    first = pl.program_id(0) == 0
    parts, _, chunk = up_s.shape
    curve = 0.7978845608028654

    @pl.when(first)
    def _():
        start_weights([(plans[0], up_refs, me_ref, up_s, up_sems), (plans[1], down_refs, me_ref, down_s, down_sems)])
        small_ref[...] = jnp.zeros_like(small_ref)
        ghidden_ref[...] = jnp.zeros_like(ghidden_ref)

    def body(wait):
        nffn = nffn_ref[...]
        middle = middle_ref[...]
        grad = grad_ref[...].astype(F32)
        lower = grad.astype(BF)
        total = middle + vec_ref[7:8, :]
        gnormed = jnp.zeros(grad.shape, F32)
        for part in part_order(me_ref, plans[0], parts):
            cols = pl.ds(pl.multiple_of(part * chunk, chunk), chunk)
            if wait:
                wait_weight(up_s, up_sems, part)
                wait_weight(down_s, down_sems, part)
            gactive = dot_nn(lower, down_s[part])
            upper = dot_nn(nffn, up_s[part]) + hidden_ref[:, cols]
            square = upper * upper
            angle = jnp.tanh(upper * (curve + (curve * 0.044715) * square))
            half = 0.5 * upper
            lift = 1.0 + angle
            active = (half * lift).astype(BF)
            slope = 0.5 * lift + half * (1.0 - angle * angle) * (curve + (3.0 * curve * 0.044715) * square)
            gupper = (gactive * slope).astype(BF)
            active_ref[:, cols] = active
            gupper_ref[:, cols] = gupper
            ghidden_ref[:, cols] += column_sum(gupper.astype(F32))
            total = total + dot_nt(active, down_s[part])
            gnormed = gnormed + dot_nt(gupper, up_s[part])
        result_ref[...] = total
        unit, root = normalize(middle)
        gmiddle = grad + norm_backward(gnormed, unit, root, vec_ref[1:2, :])
        gmiddle_ref[...] = gmiddle
        small_ref[0:1, :] += column_sum(gnormed * unit)
        small_ref[1:2, :] += column_sum(gnormed)
        small_ref[2:3, :] += column_sum(lower.astype(F32))
        small_ref[3:4, :] += column_sum(gmiddle.astype(BF).astype(F32))

    pl.when(first)(functools.partial(body, True))
    pl.when(jnp.logical_not(first))(functools.partial(body, False))


def ffn_both(me, nffn, middle, grad, vec, hidden, up_w, down_w, block, parts):
    rows, width = nffn.shape
    ffn = hidden.shape[1]
    arrays = up_w[1] + down_w[1]
    row_spec = lambda cols: pl.BlockSpec((block, cols), lambda i: (i, 0))
    return pl.pallas_call(
        functools.partial(ffn_both_kernel, (up_w[0], down_w[0])),
        grid=(rows // block,),
        in_specs=[
            pl.BlockSpec(memory_space=pltpu.SMEM),
            row_spec(width),
            row_spec(width),
            row_spec(width),
            pl.BlockSpec(vec.shape, lambda i: (0, 0)),
            pl.BlockSpec(hidden.shape, lambda i: (0, 0)),
        ]
        + [pl.BlockSpec(memory_space=pl.ANY)] * len(arrays),
        out_specs=[
            row_spec(width),
            row_spec(ffn),
            row_spec(ffn),
            row_spec(width),
            pl.BlockSpec((8, width), lambda i: (0, 0)),
            pl.BlockSpec((1, ffn), lambda i: (0, 0)),
        ],
        out_shape=[
            jax.ShapeDtypeStruct((rows, width), F32),
            jax.ShapeDtypeStruct((rows, ffn), BF),
            jax.ShapeDtypeStruct((rows, ffn), BF),
            jax.ShapeDtypeStruct((rows, width), F32),
            jax.ShapeDtypeStruct((8, width), F32),
            jax.ShapeDtypeStruct((1, ffn), F32),
        ],
        scratch_shapes=[
            pltpu.VMEM((parts, width, ffn // parts), BF),
            pltpu.VMEM((parts, width, ffn // parts), BF),
            pltpu.SemaphoreType.DMA((parts,)),
            pltpu.SemaphoreType.DMA((parts,)),
        ],
        compiler_params=pltpu.CompilerParams(vmem_limit_bytes=VMEM_LIMIT),
        cost_estimate=pl.CostEstimate(flops=25 * 10**9, bytes_accessed=40 * 10**6, transcendentals=0),
        name="ffn_both",
    )(me, nffn, middle, grad, vec, hidden, *arrays)


def ffn_weight_kernel(nffn_ref, grad_ref, gupper_ref, active_ref, out_ref, nffn_t, grad_t):
    @pl.when(pl.program_id(0) == 0)
    def _():
        nffn_t[...] = nffn_ref[...].T
        grad_t[...] = grad_ref[...].astype(BF).T

    shape = (out_ref.shape[0],) + out_ref.shape[3:]
    out_ref[:, 0, 0] = dot_nn(nffn_t[...], gupper_ref[...]).astype(BF).reshape(shape)
    out_ref[:, 0, 1] = dot_nn(grad_t[...], active_ref[...]).astype(BF).reshape(shape)


def ffn_weight(nffn, grad, gupper, active, stripes, parts):
    rows, width = nffn.shape
    piece = gupper.shape[1] // parts
    high = width // stripes
    whole = pl.BlockSpec((rows, width), lambda i: (0, 0))
    return pl.pallas_call(
        ffn_weight_kernel,
        grid=(parts,),
        in_specs=[
            whole,
            whole,
            pl.BlockSpec((rows, piece), lambda i: (0, i)),
            pl.BlockSpec((rows, piece), lambda i: (0, i)),
        ],
        out_specs=pl.BlockSpec((stripes, 1, 2, high, piece), lambda i: (0, i, 0, 0, 0)),
        out_shape=jax.ShapeDtypeStruct((stripes, parts, 2, high, piece), BF),
        scratch_shapes=[pltpu.VMEM((width, rows), BF), pltpu.VMEM((width, rows), BF)],
        compiler_params=pltpu.CompilerParams(vmem_limit_bytes=VMEM_LIMIT),
        cost_estimate=pl.CostEstimate(flops=15 * 10**9, bytes_accessed=30 * 10**6, transcendentals=0),
        name="ffn_weight",
    )(nffn, grad, gupper, active)


def attention_backward_kernel(gmiddle_ref, stream_ref, proj_ref, probs_ref, vec_ref, qkv_s, out_s, *refs):
    gstream_ref, gproj_ref, small_ref, gmixed_s = refs[-4:]

    @pl.when(pl.program_id(0) == 0)
    def _():
        small_ref[...] = jnp.zeros_like(small_ref)

    width = stream_ref.shape[1]
    block_pages, _, slots, _ = probs_ref.shape
    scale = (width // HEADS) ** (-0.5)
    gmiddle = gmiddle_ref[...]
    gmixed_s[...] = dot_nt(gmiddle.astype(BF), out_s[...]).astype(BF)
    lanes = 2 * (width // HEADS)
    for page in range(block_pages):
        rows = slice(page * slots, (page + 1) * slots)
        for pair in range(PAIRS):
            at = pair * lanes
            gmixed = gmixed_s[rows, at : at + lanes]
            queries = split_heads(proj_ref[rows, at : at + lanes])
            keys_in = split_heads(proj_ref[rows, width + at : width + at + lanes])
            values = split_heads(proj_ref[rows, 2 * width + at : 2 * width + at + lanes])
            probs = probs_ref[page, pair]
            gsoft = dot_nt(gmixed, values)
            gscore = []
            for head in range(2):
                cols = slice(head * slots, (head + 1) * slots)
                soft = probs[:, cols].astype(F32)
                grad = gsoft[:, cols]
                inner = jnp.sum(soft * grad, axis=-1, keepdims=True)
                gscore.append((soft * (grad - inner)).astype(BF))
            stacked = jnp.concatenate([probs[:, :slots], probs[:, slots:]], axis=0)
            gvalues = dot_tn(stacked, split_heads(gmixed))
            gqueries = dot_nn(jnp.concatenate(gscore, axis=1), keys_in) * scale
            gkeys = dot_tn(jnp.concatenate(gscore, axis=0), queries) * scale
            gproj_ref[rows, at : at + lanes] = gqueries.astype(BF)
            gproj_ref[rows, width + at : width + at + lanes] = gkeys.astype(BF)
            gproj_ref[rows, 2 * width + at : 2 * width + at + lanes] = gvalues.astype(BF)
    gnormed = dot_nt(gproj_ref[...], qkv_s[...])
    unit, root = normalize(stream_ref[...].astype(F32))
    gstream_ref[...] = gmiddle + norm_backward(gnormed, unit, root, vec_ref[0:1, :])
    small_ref[0:1, :] += column_sum(gnormed * unit)
    small_ref[1:2, :] += column_sum(gnormed)
    small_ref[2:3, :] += column_sum(gproj_ref[:, :width].astype(F32))
    small_ref[3:4, :] += column_sum(gproj_ref[:, 2 * width :].astype(F32))


def attention_backward(gmiddle, stream, proj, probs, vec, weight, block_pages, begin, end, before):
    rows, width = stream.shape
    _, _, slots, _ = probs.shape
    block = block_pages * slots
    first = begin // block_pages
    row_spec = lambda cols: pl.BlockSpec((block, cols), lambda i: (i + first, 0))
    whole = lambda array: pl.BlockSpec(array.shape, lambda i: (0, 0))
    before = [] if before is None else list(before)
    operands = [gmiddle, stream, proj, probs, vec, weight[0], weight[1]]
    return pl.pallas_call(
        attention_backward_kernel,
        grid=((end - begin) // block_pages,),
        in_specs=[
            row_spec(width),
            row_spec(width),
            row_spec(3 * width),
            pl.BlockSpec((block_pages, PAIRS, slots, 2 * slots), lambda i: (i + first, 0, 0, 0)),
            whole(vec),
            whole(weight[0]),
            whole(weight[1]),
        ]
        + [pl.BlockSpec(memory_space=pl.ANY)] * len(before),
        out_specs=[row_spec(width), row_spec(3 * width), pl.BlockSpec((8, width), lambda i: (0, 0))],
        out_shape=[
            jax.ShapeDtypeStruct((rows, width), F32),
            jax.ShapeDtypeStruct((rows, 3 * width), BF),
            jax.ShapeDtypeStruct((8, width), F32),
        ],
        scratch_shapes=[pltpu.VMEM((block, width), BF)],
        input_output_aliases={len(operands) + index: index for index in range(len(before))},
        compiler_params=pltpu.CompilerParams(vmem_limit_bytes=VMEM_LIMIT),
        cost_estimate=pl.CostEstimate(flops=15 * 10**9, bytes_accessed=20 * 10**6, transcendentals=0),
        name="attention_backward",
    )(*operands, *before)


def attention_weight_kernel(normed_ref, mixed_ref, gproj_ref, gmiddle_ref, grad_ref):
    gqkv = dot_tn(normed_ref[...], gproj_ref[...])
    gout = dot_tn(mixed_ref[...], gmiddle_ref[...].astype(BF))
    parts = grad_ref.shape[1]
    cut = gqkv.shape[1] // parts
    rest = gout.shape[1] // parts
    shape = (grad_ref.shape[0],) + grad_ref.shape[3:]
    for part in range(parts):
        qkv_part = gqkv[:, part * cut : (part + 1) * cut].astype(BF)
        out_part = gout[:, part * rest : (part + 1) * rest].astype(BF)
        grad_ref[:, part, 0] = jnp.concatenate([qkv_part, out_part], axis=1).reshape(shape)


def attention_weight(normed, mixed, gproj, gmiddle, stripes, parts):
    rows, width = normed.shape
    block = width // 2
    high = width // stripes
    return pl.pallas_call(
        attention_weight_kernel,
        grid=(2,),
        in_specs=[
            pl.BlockSpec((rows, block), lambda i: (0, i)),
            pl.BlockSpec((rows, block), lambda i: (0, i)),
            pl.BlockSpec((rows, 3 * width), lambda i: (0, 0)),
            pl.BlockSpec((rows, width), lambda i: (0, 0)),
        ],
        out_specs=pl.BlockSpec((stripes // 2, parts, 1, high, width), lambda i: (i, 0, 0, 0, 0)),
        out_shape=jax.ShapeDtypeStruct((stripes, parts, 1, high, width), BF),
        compiler_params=pltpu.CompilerParams(vmem_limit_bytes=VMEM_LIMIT),
        cost_estimate=pl.CostEstimate(flops=10 * 10**9, bytes_accessed=20 * 10**6, transcendentals=0),
        name="attention_weight",
    )(normed, mixed, gproj, gmiddle)


def relative_rows(source, target, me, depth):
    high = source.shape[0] // (2 * depth)
    for x in range(2):
        for z in range(depth):
            start = pl.multiple_of(jnp.bitwise_xor(me, 2 * z + x) * high, 16)
            at = (x * depth + z) * high
            target[at : at + high, :] = source[pl.ds(start, high), :]


def send_out(me_ref, core, y, staged, slot, own_ref, other_ref, sems):
    for x in range(2):
        first, second = plane(me_ref, x, y, core)

        @pl.when(core == 0)
        def _():
            pltpu.make_async_copy(staged.at[slot, x], own_ref.at[second, first], sems.at[slot, x]).start()

        @pl.when(core == 1)
        def _():
            pltpu.make_async_copy(staged.at[slot, x], other_ref.at[second, first], sems.at[slot, x]).start()


def wait_out(staged, slot, own_ref, sems):
    for x in range(2):
        pltpu.make_async_copy(staged.at[slot, x], own_ref.at[0, 0], sems.at[slot, x]).wait()


def ffn_weight_split_kernel(core, me_ref, nffn_ref, grad_ref, gupper_ref, active_ref, out_ref, *refs):
    step = pl.program_id(0)
    staged, sems = refs[-2:]
    _, _, depth, high, width = staged.shape
    high = high // 2
    if core == 1:
        nffn_out, grad_out, turned, nffn_t, grad_t = refs[:-2]
        kept = [
            pltpu.make_async_copy(nffn_t, nffn_out, sems.at[2, 0]),
            pltpu.make_async_copy(grad_t, grad_out, sems.at[2, 1]),
        ]

        @pl.when(step == 0)
        def _():
            turned[...] = nffn_ref[...].T
            relative_rows(turned, nffn_t, me_ref[0], depth)
            turned[...] = grad_ref[...].astype(BF).T
            relative_rows(turned, grad_t, me_ref[0], depth)
            for copy in kept:
                copy.start()
    else:
        nffn_t, grad_t, kept = nffn_ref, grad_ref, []

    shape = (2, depth, high, width)
    staged[step, :, :, :high, :] = dot_nn(nffn_t[...], gupper_ref[...]).astype(BF).reshape(shape)
    staged[step, :, :, high:, :] = dot_nn(grad_t[...], active_ref[...]).astype(BF).reshape(shape)
    for x in range(2):
        first, second = plane(me_ref, x, step, core)
        pltpu.make_async_copy(staged.at[step, x], out_ref.at[second, first], sems.at[step, x]).start()

    @pl.when(step == 1)
    def _():
        wait_out(staged, 0, out_ref, sems)
        wait_out(staged, 1, out_ref, sems)
        for copy in kept:
            copy.wait()


def ffn_weight_split(me, nffn, grad, gupper, active, depth, core):
    rows, piece = gupper.shape[0], gupper.shape[1] // 4
    width = piece
    high = width // (2 * depth)
    whole = lambda array: pl.BlockSpec(array.shape, lambda i, me: (0, 0))
    column = pl.BlockSpec((rows, piece), lambda i, me: (0, jnp.bitwise_xor(me[1], 2 * i + core)))
    shape = (2, 2, depth, 2 * high, piece)
    return pl.pallas_call(
        functools.partial(ffn_weight_split_kernel, core),
        grid_spec=pltpu.PrefetchScalarGridSpec(
            num_scalar_prefetch=1,
            grid=(2,),
            in_specs=[whole(nffn), whole(grad), column, column],
            out_specs=[pl.BlockSpec(memory_space=pl.ANY)] * (1 + 2 * core),
            scratch_shapes=[pltpu.VMEM((width, rows), BF)] * (3 * core)
            + [pltpu.VMEM(shape, BF), pltpu.SemaphoreType.DMA((3, 2))],
        ),
        out_shape=[jax.ShapeDtypeStruct(shape, BF)] + [jax.ShapeDtypeStruct((width, rows), BF)] * (2 * core),
        compiler_params=pltpu.CompilerParams(vmem_limit_bytes=VMEM_LIMIT),
        cost_estimate=pl.CostEstimate(flops=8 * 10**9, bytes_accessed=15 * 10**6, transcendentals=0),
        name="ffn_weight",
    )(me, nffn, grad, gupper, active)


def attention_weight_split_kernel(me_ref, normed_ref, mixed_ref, gproj_ref, gmiddle_ref, *refs):
    other_ref, own_ref, turned, normed_t, mixed_t, found, staged, extra_s, sems = refs[-9:]
    extra_refs = refs[:-9]
    step = pl.program_id(0)
    _, _, depth, rows, width = staged.shape
    high = width // (2 * depth)
    share = width // 4
    shape = (2, depth, high, width)

    @pl.when(step == 0)
    def _():
        turned[...] = mixed_ref[...].T
        relative_rows(turned, mixed_t, me_ref[0], depth)
        found[:, 3 * width :] = dot_nn(mixed_t[...], gmiddle_ref[...].astype(BF)).astype(BF)
        turned[...] = normed_ref[...].T
        relative_rows(turned, normed_t, me_ref[0], depth)
        if extra_refs:
            extra_s[...] = jnp.zeros_like(extra_s)
            for index in range(2):
                one_ref, two_ref, hidden_ref = extra_refs[3 * index : 3 * index + 3]
                sums = jnp.concatenate([one_ref[:4, :], two_ref[:4, :]], axis=0)
                for part in range(4):
                    at = index * (width // 3)
                    extra_s[part, :8, at : at + share] = sums[:, part * share : (part + 1) * share]
                    extra_s[part, 8 + index : 9 + index, :] = hidden_ref[:, part * width : (part + 1) * width]
            for part in range(4):
                extra = extra_s[part].astype(BF)
                staged[part, :, :, high:, :] = jnp.broadcast_to(extra[None, None], (2, depth) + extra.shape)

    def finish(part):
        columns = slice(part * 3 * share, (part + 1) * 3 * share)
        rest = slice(3 * width + part * share, 3 * width + (part + 1) * share)
        staged[part, :, :, :high, :] = jnp.concatenate([found[:, columns], found[:, rest]], axis=1).reshape(shape)
        near = jnp.bitwise_xor(me_ref[1], part)
        send_out(me_ref, near % 2, near // 2, staged, part, own_ref, other_ref, sems)

    for third in range(3):

        @pl.when(step == third)
        def _():
            found[:, third * width : (third + 1) * width] = dot_nn(normed_t[...], gproj_ref[...]).astype(BF)
            for part in ((0,), (1,), (2, 3))[third]:
                finish(part)
            if third == 2:
                for part in range(4):
                    wait_out(staged, part, own_ref, sems)


def attention_weight_split(me, normed, mixed, gproj, gmiddle, depth, extra=None):
    rows, width = normed.shape
    high = width // (2 * depth)
    whole = lambda array: pl.BlockSpec(array.shape, lambda i: (0,) * array.ndim)
    extras = [] if extra is None else list(extra)
    shape = (2, 2, depth, high + (0 if extra is None else 16), width)
    operands = [normed, mixed, gproj, gmiddle] + extras
    return pl.pallas_call(
        attention_weight_split_kernel,
        grid=(3,),
        in_specs=[pl.BlockSpec(memory_space=pltpu.SMEM), whole(normed), whole(mixed)]
        + [pl.BlockSpec((rows, width), lambda i: (0, i))]
        + [whole(operand) for operand in operands[3:]],
        out_specs=[pl.BlockSpec(memory_space=pl.ANY)] * 2,
        out_shape=[jax.ShapeDtypeStruct(shape, BF)] * 2,
        scratch_shapes=[pltpu.VMEM((width, rows), BF)] * 3
        + [
            pltpu.VMEM((width, 4 * width), BF),
            pltpu.VMEM((4,) + shape[1:], BF),
            pltpu.VMEM((4, 16, width), F32),
            pltpu.SemaphoreType.DMA((4, 2)),
        ],
        compiler_params=pltpu.CompilerParams(vmem_limit_bytes=VMEM_LIMIT),
        cost_estimate=pl.CostEstimate(flops=10 * 10**9, bytes_accessed=20 * 10**6, transcendentals=0),
        name="attention_weight",
    )(me, *operands)


def pair_bias(slot_kind, slot_valid, across):
    same_kind = slot_kind[:, :, None] == slot_kind[:, None, :]
    partner = jnp.logical_not(same_kind) if across else same_kind
    allowed = jnp.logical_and(partner, slot_valid[:, None, :] > 0)
    return jnp.where(allowed, 0.0, -1e30).astype(F32)


def ordered_vectors(small_one, small_two):
    picked = (small_one, 0), (small_two, 0), (small_one, 1), (small_one, 2)
    picked += (small_one, 3), (small_two, 3), (small_two, 1), (small_two, 2)
    return jnp.stack([sums[row] for sums, row in picked])


def adam_step(master, grad, moment_one, moment_two, factor, decayed):
    clipped = grad * factor
    first_new = beta_one * moment_one + (1.0 - beta_one) * clipped
    second_new = beta_two * moment_two + (1.0 - beta_two) * clipped * clipped
    change = first_new / bias_one / (jnp.sqrt(second_new / bias_two) + epsilon)
    if decayed:
        change = change + weight_decay * master
    return (-learn_rate * change, first_new, second_new)


def gather_rows(pieces, sizes):
    kinds, high, width = pieces.shape
    rows = lax.all_gather(pieces.reshape(-1, width), ("dp", "tensor"), axis=0, tiled=False)
    if high % 16 == 0:
        return [(("rows", kind * high), [rows]) for kind in range(kinds)]
    split = rows.reshape(sizes["dp"], sizes["tensor"], kinds, high, width)
    return [(("whole",), [jnp.swapaxes(split[:, :, kind], 0, 1).reshape(-1, width, width)]) for kind in range(kinds)]


def scatter_rows(grad, sizes):
    stripes, parts, kinds, high, width = grad.shape
    inner = sizes["dp"] // stripes
    if inner > 1:
        grad = jnp.moveaxis(grad.reshape(stripes, parts, kinds, inner, high // inner, width), 3, 1)
    mine = lax.psum_scatter(grad.reshape(-1, width), ("dp", "tensor"), scatter_dimension=0, tiled=True)
    return mine.reshape(kinds, -1, width).astype(F32)


class Exchange:
    def __init__(self, sizes):
        self.sizes = sizes
        self.depth = sizes["dp"] // 2

    def swap(self, value, partner):
        dp, tensor = self.sizes["dp"], self.sizes["tensor"]
        pairs = []
        for i in range(dp):
            for j in range(tensor):
                far_i, far_j = partner(i, j)
                pairs.append((i * tensor + j, far_i * tensor + far_j))
        return lax.ppermute(value, ("dp", "tensor"), pairs)

    def part(self, bits, value):
        return self.swap(value, lambda i, j: (i, j ^ bits))

    def core(self, value):
        return self.part(1, value)

    def x(self, value):
        return self.swap(value, lambda i, j: (i ^ 1, j))

    def y(self, value):
        return self.part(2, value)

    def diagonal(self, value):
        return self.swap(value, lambda i, j: (i ^ 1, j ^ 2))

    def first(self, value):
        return self.swap(value, lambda i, j: (i, j ^ 2) if j & 1 else (i ^ 1, j))

    def second(self, value):
        return self.swap(value, lambda i, j: (i ^ 1, j) if j & 1 else (i, j ^ 2))

    def z(self, distance, value):
        return self.swap(value, lambda i, j: (i ^ (2 * distance), j))

    def z_sends(self, values):
        return [(functools.partial(self.z, distance), values[distance]) for distance in range(1, self.depth)]

    def gather_z(self, piece):
        groups = [[2 * z + x for z in range(self.depth)] for x in range(2)]
        return lax.all_gather(piece, "dp", axis=0, tiled=False, axis_index_groups=groups)

    def total(self, value):
        value = value + self.core(value)
        value = value + self.y(value)
        value = value + self.x(value)
        bit = 1
        while bit < self.depth:
            value = value + self.z(bit, value)
            bit *= 2
        return value


def tie(values, after):
    return lax.optimization_barrier((values, after))[0]


class Spread:
    def __init__(self, exchange, quad, fixed):
        self.exchange, self.quad, self.fixed = exchange, quad, fixed

    def go_first(self):
        return [(self.exchange.first, self.quad)]

    def go_second(self, came):
        self.pair = jnp.stack([self.quad, came[0]])
        return [(self.exchange.second, self.pair), (self.exchange.core, self.pair)]

    def go_core(self, came):
        self.two, self.far_pair = came
        return [(self.exchange.core, self.two)]

    def weight(self, came, offset=0):
        positions = [[(0, second, core), (1, second, core)] for core in range(2) for second in range(2)]
        arrays = [self.pair, self.two, self.far_pair, came[0]]
        return (("near", offset, positions, self.fixed), arrays)


class Reduce:
    def __init__(self, exchange, other, own):
        self.exchange, self.other, self.own = exchange, other, own

    def wide(self, value):
        return value.astype(F32)

    def go_core(self):
        return [(self.exchange.core, self.other)]

    def go_second(self, came):
        self.came = came[0]
        value = (self.wide(self.own[1]) + self.wide(self.came[1])).astype(BF)
        return [(self.exchange.second, value)]

    def go_first(self, came):
        self.beside = came[0]
        value = self.wide(self.own[0, 1]) + self.wide(self.came[0, 1]) + self.wide(self.beside[1])
        return [(self.exchange.first, value.astype(BF))]

    def depths(self, came):
        ahead = came[0]
        return (
            self.wide(self.own[0, 0]) + self.wide(self.came[0, 0]) + self.wide(self.beside[0]) + self.wide(ahead)
        )


def mid_first(sends):
    at = (len(sends) + 1) // 2 - 1
    return sends[at : at + 1] + sends[:at] + sends[at + 1 :]


class Lane:
    def __init__(self):
        self.last = None

    def after_last(self, values):
        return values if self.last is None else tie(values, self.last)

    def step(self, sends, kernel=None, arrays=()):
        values = [value for _, value in sends]
        values, arrays = self.after_last((values, list(arrays)))
        came = [move(value) for (move, _), value in zip(sends, values)]
        results = [] if kernel is None else list(kernel(*arrays))
        came, results = lax.optimization_barrier((came, results))
        self.last = results[-1] if results else came[-1]
        return came, results


def shards(
    sizes,
    tokens, out_grad, slot_kind, slot_valid,
    qkv_weight, qkv_first, qkv_second,
    out_weight, out_first, out_second,
    up_weight, up_first, up_second,
    down_weight, down_first, down_second,
    gain_weight, gain_first, gain_second,
    bias_weight, bias_first, bias_second,
    hidden_weight, hidden_first, hidden_second,
):
    parts = sizes["tensor"]
    width = tokens.shape[1]
    cut = qkv_weight.shape[2]
    high = qkv_weight.shape[1]
    split = parts == 4 and high % 32 == 0 and sizes["dp"] in (4, 8, 16)
    exchange = Exchange(sizes)
    stripes = sizes["dp"] if high % 16 == 0 else 2
    me = jnp.stack([lax.axis_index("dp"), lax.axis_index("tensor")]).astype(jnp.int32)
    attn_pieces = jnp.concatenate([qkv_weight.astype(BF), out_weight.astype(BF)], axis=2)
    up_pieces = up_weight.astype(BF)
    down_pieces = jnp.swapaxes(down_weight.astype(BF), 1, 2)
    pages = slot_kind.shape[0]
    block_pages = 2 if pages % 2 == 0 else 1
    block = block_pages * slot_kind.shape[1]
    masks = [pair_bias(slot_kind, slot_valid, index == 0) for index in range(2)]
    lane = Lane()
    gathered = lambda index: gather_rows(
        jnp.stack([attn_pieces[index], up_pieces[index], down_pieces[index]]), sizes
    )
    small = hidden = None
    saved = [None, None]

    def attention_forward_of(index, weight):
        return lambda stream: attention_forward(
            me, stream, masks[index], small[index], weight, block_pages, parts
        )

    def ffn_forward_of(index, up_w, down_w):
        return lambda nffn, middle: ffn_forward(
            me, nffn, middle, small[index], hidden[index : index + 1], up_w, down_w, block, parts
        )

    def ffn_backward_of(index):
        kept = saved[index]
        return lambda grad: ffn_backward(
            me, grad, kept["slope"], kept["middle"], small[index], kept["up_w"], kept["down_w"], block, parts
        )

    def ffn_weight_of(index, grad, turned=None):
        kept = saved[index]
        if not split:
            return lambda gupper: (ffn_weight(kept["nffn"], grad, gupper, kept["active"], stripes, parts),)
        core = 1 if turned is None else 0
        left, right = (kept["nffn"], grad) if turned is None else turned
        return lambda gupper: ffn_weight_split(me, left, right, gupper, kept["active"], exchange.depth, core)

    def attention_backward_of(index, begin, end, before=None):
        kept = saved[index]
        return lambda gmiddle: attention_backward(
            gmiddle, kept["stream"], kept["proj"], kept["probs"], small[index], kept["weight"],
            block_pages, begin, end, before,
        )

    def attention_weight_of(index, gmiddle, extra=None):
        kept = saved[index]
        if split:
            return lambda gproj: attention_weight_split(
                me, kept["normed"], kept["mixed"], gproj, gmiddle, exchange.depth, extra
            )
        return lambda gproj: (attention_weight(kept["normed"], kept["mixed"], gproj, gmiddle, stripes, parts),)

    def keep(index, stream, attention, ffn):
        middle, nffn, normed, proj, probs, mixed, qkv_w, out_w = attention
        saved[index] = dict(
            stream=stream, middle=middle, nffn=nffn, normed=normed, proj=proj, probs=probs, mixed=mixed,
            weight=(qkv_w, out_w), active=ffn[1],
        )
        if len(ffn) > 2:
            saved[index].update(slope=ffn[2], up_w=(("whole",), [ffn[3]]), down_w=(("whole",), [ffn[4]]))

    if split:
        depth = exchange.depth
        late = jnp.concatenate([attn_pieces[1], up_pieces[1], down_pieces[1]], axis=0)
        own_small = jnp.concatenate(
            [gain_weight, bias_weight, hidden_weight.reshape(2, -1, gain_weight.shape[2])], axis=1
        )
        own_small = lax.reduce_precision(own_small, 8, 7)
        small_sends = [(functools.partial(exchange.part, bits), own_small) for bits in range(1, 4)]
        late = exchange.gather_z(late)
        came, _ = lane.step(exchange.z_sends([attn_pieces[0]] * depth))
        attn_zero = Spread(exchange, jnp.stack([attn_pieces[0]] + came), False)
        ffn_piece = jnp.concatenate([up_pieces[0], down_pieces[0]], axis=0)
        ffn_sends = exchange.z_sends([ffn_piece] * depth)
        middle_at = depth // 2 - 1
        came, _ = lane.step(attn_zero.go_first() + ffn_sends[middle_at : middle_at + 1] + small_sends)
        ffn_came = came[1:2]
        mine = lax.axis_index("tensor")

        def order_small(*values):
            every = jnp.zeros((4,) + own_small.shape, F32)
            for bits, value in enumerate(values):
                every = lax.dynamic_update_slice_in_dim(every, value[None], jnp.bitwise_xor(mine, bits), 0)
            small = jnp.moveaxis(every[:, :, :8], 0, 2).reshape(2, 8, width)
            return small[0], small[1], jnp.moveaxis(every[:, :, 8:], 0, 1).reshape(2, -1)

        ffn_sends = ffn_sends[:middle_at] + ffn_sends[middle_at + 1 :]
        came, results = lane.step(attn_zero.go_second(came[:1]) + ffn_sends, order_small, [own_small] + came[2:])
        small, hidden = results[:2], results[2]
        others = came[2:]
        others.insert(middle_at, ffn_came[0])
        ffn_zero = Spread(exchange, jnp.stack([ffn_piece] + others), False)
        came, _ = lane.step(attn_zero.go_core(came[:2]) + ffn_zero.go_first())
        attn_w = attn_zero.weight(came[:1])
        came, attention = lane.step(ffn_zero.go_second(came[1:]), attention_forward_of(0, attn_w), [tokens])
        late = lane.after_last(late)
        attn_one = Spread(exchange, late[:, :high], True)
        ffn_one = Spread(exchange, late[:, high:], True)
        came, _ = lane.step(ffn_zero.go_core(came) + attn_one.go_first())
        up_w, down_w = ffn_zero.weight(came[:1]), ffn_zero.weight(came[:1], high)
        came, ffn = lane.step(
            attn_one.go_second(came[1:]) + ffn_one.go_first(), ffn_forward_of(0, up_w, down_w), attention[1::-1]
        )
        keep(0, tokens, attention, ffn)
        stream = ffn[0]
        ffn_came = came[2:]
        came, _ = lane.step(attn_one.go_core(came[:2]))
        attn_w = attn_one.weight(came)
        came, attention = lane.step(ffn_one.go_second(ffn_came), attention_forward_of(1, attn_w), [stream])
        came, _ = lane.step(ffn_one.go_core(came))
        up_w, down_w = ffn_one.weight(came), ffn_one.weight(came, high)
        both = lambda nffn, middle: ffn_both(
            me, nffn, middle, out_grad, small[1], hidden[1:], up_w, down_w, block, parts
        )
        _, results = lane.step([], both, attention[1::-1])
        block_output, active, gupper, gmiddle, small_two, hidden_one = results
        keep(1, stream, attention, (None, active))
        _, (other, *turned) = lane.step([], ffn_weight_of(1, out_grad), [gupper])
        came, (own,) = lane.step([(exchange.core, other)], ffn_weight_of(1, out_grad, turned), [gupper])
        ffn_one = Reduce(exchange, other, own)
        came, (grad, gproj, small_one) = lane.step(
            ffn_one.go_second(came), attention_backward_of(1, 0, pages), [gmiddle]
        )
        sums_one = (small_one, small_two, hidden_one)
        came, grads = lane.step(ffn_one.go_first(came), attention_weight_of(1, gmiddle), [gproj])
        ffn_layers = ffn_one.depths(came)
        ffn_sends = mid_first(exchange.z_sends([ffn_layers[z].astype(BF) for z in range(depth)]))
        attn_one = Reduce(exchange, *grads)
        came, results = lane.step(attn_one.go_core() + ffn_sends[:1], ffn_backward_of(0), [grad])
        ffn_came = came[1:]
        gupper, gmiddle, small_two, hidden_zero = results
        came, (other, *turned) = lane.step(
            attn_one.go_second(came[:1]) + ffn_sends[1:], ffn_weight_of(0, grad), [gupper]
        )
        ffn_came = ffn_came + came[1:]
        total = ffn_layers[0] + sum(value.astype(F32) for value in ffn_came)
        grad_up, grad_down = [None, total[:high]], [None, total[high:]]
        came, (own,) = lane.step(
            [(exchange.core, other)] + attn_one.go_first(came[:1]), ffn_weight_of(0, grad, turned), [gupper]
        )
        ffn_zero = Reduce(exchange, other, own)
        attn_layers = attn_one.depths(came[1:])
        attn_sends = mid_first(exchange.z_sends([attn_layers[z].astype(BF) for z in range(depth)]))
        came, (input_grad, gproj, small_one) = lane.step(
            ffn_zero.go_second(came[:1]) + attn_sends[:1], attention_backward_of(0, 0, pages), [gmiddle]
        )
        attn_came = came[1:]
        came, grads = lane.step(
            ffn_zero.go_first(came[:1]) + attn_sends[1:],
            attention_weight_of(0, gmiddle, (small_one, small_two, hidden_zero) + sums_one),
            [gproj],
        )
        grad_attn = [None, attn_layers[0] + sum(value.astype(F32) for value in attn_came + came[1:])]
        layers = ffn_zero.depths(came[:1])
        ffn_sends = exchange.z_sends([layers[z].astype(BF) for z in range(depth)])
        ffn_sends = mid_first(ffn_sends)
        attn_zero = Reduce(exchange, *grads)
        ((move, value),) = ffn_sends[:1]
        ffn_came = [move(lane.after_last(value))]
        came, _ = lane.step(attn_zero.go_core())
        came, _ = lane.step(attn_zero.go_second(came) + ffn_sends[1:])
        ffn_came = ffn_came + came[1:]
        came, _ = lane.step(attn_zero.go_first(came[:1]))
        total = layers[0] + sum(value.astype(F32) for value in ffn_came)
        grad_up[0], grad_down[0] = total[:high], total[high:]
        layers = attn_zero.depths(came[:1])
        came, _ = lane.step(exchange.z_sends([layers[z].astype(BF) for z in range(depth)]))
        total = layers[0] + sum(value.astype(F32) for value in came)
        grad_attn[0] = total[:high]
        shared_squares = jnp.sum(total[high:] * total[high:])
        share = width // parts
        vectors = []
        for at in (0, width // 3):
            sums = total[high : high + 8, at : at + share]
            vectors.append(ordered_vectors(sums[:4], sums[4:]))
        vectors = jnp.stack(vectors)
        grad_hidden = total[high + 8 : high + 10]
    else:
        small = jnp.concatenate([gain_weight, bias_weight], axis=1).astype(BF)
        small = lax.all_gather(small, "tensor", axis=2, tiled=True).astype(F32)
        hidden = lax.all_gather(hidden_weight.astype(BF), "tensor", axis=1, tiled=True).astype(F32)
        stream = tokens
        for index in range(2):
            attn_w, up_w, down_w = gathered(index)
            attention = attention_forward_of(index, attn_w)(stream)
            ffn = ffn_forward_of(index, up_w, down_w)(*attention[1::-1])
            keep(index, stream, attention, ffn)
            stream = ffn[0]
        block_output = stream
        grad = out_grad
        grad_attn, grad_up, grad_down, vectors, grad_hidden = ([None, None] for _ in range(5))
        for index in (1, 0):
            gupper, gmiddle, small_two, grad_hidden[index] = ffn_backward_of(index)(grad)
            (gffn,) = ffn_weight_of(index, grad)(gupper)
            grad_up[index], grad_down[index] = scatter_rows(gffn, sizes)
            grad, gproj, small_one = attention_backward_of(index, 0, pages)(gmiddle)
            (grad_attn[index],) = scatter_rows(attention_weight_of(index, gmiddle)(gproj)[0], sizes)
            vectors[index] = ordered_vectors(small_one, small_two)
        input_grad = grad
        vectors, grad_hidden = lax.psum((jnp.stack(vectors), jnp.concatenate(grad_hidden, axis=0)), ("dp", "tensor"))
        at = lax.axis_index("tensor")
        slice_of = lambda whole: lax.dynamic_slice_in_dim(
            whole, at * (whole.shape[-1] // parts), whole.shape[-1] // parts, whole.ndim - 1
        )
        vectors, grad_hidden = slice_of(vectors), slice_of(grad_hidden)
        shared_squares = jnp.sum(vectors * vectors) + jnp.sum(grad_hidden * grad_hidden)
    grad_gain, grad_bias = vectors[:, :2], vectors[:, 2:]
    local_squares = sum(jnp.sum(grad * grad) for pair in (grad_up, grad_down, grad_attn) for grad in pair[::-1])
    grad_attn, grad_up, grad_down = jnp.stack(grad_attn), jnp.stack(grad_up), jnp.stack(grad_down)
    local_squares = local_squares + jnp.where(lax.axis_index("dp") == 0, shared_squares, 0.0)
    grad_down = jnp.swapaxes(grad_down, 1, 2)
    if split:
        total_squares = exchange.total(local_squares.reshape(1, 1))[0, 0]
    else:
        total_squares = lax.psum(local_squares, ("dp", "tensor"))
    grad_norm = jnp.sqrt(total_squares)
    factor = clip_norm / jnp.maximum(grad_norm, clip_norm)
    masters = (qkv_weight, out_weight, up_weight, down_weight, gain_weight, bias_weight, hidden_weight)
    firsts = (qkv_first, out_first, up_first, down_first, gain_first, bias_first, hidden_first)
    seconds = (qkv_second, out_second, up_second, down_second, gain_second, bias_second, hidden_second)
    gradients = (
        grad_attn[:, :, :cut], grad_attn[:, :, cut:], grad_up, grad_down, grad_gain, grad_bias, grad_hidden,
    )
    results = [block_output, input_grad, grad_norm]
    for member in range(7):
        update, first_new, second_new = adam_step(
            masters[member], gradients[member], firsts[member], seconds[member], factor, member < 4
        )
        results = results + [gradients[member], update, first_new, second_new]
    return tuple(results)


def solution(mesh):
    rows = P(("dp", "tensor"), None)
    matrix = P(None, "dp", "tensor")
    turned = P(None, "tensor", "dp")
    vectors = P(None, None, "tensor")
    hidden = P(None, "tensor")
    return jax.shard_map(
        functools.partial(shards, dict(mesh.shape)),
        mesh=mesh,
        in_specs=(rows,) * 4 + (matrix,) * 9 + (turned,) * 3 + (vectors,) * 6 + (hidden,) * 3,
        out_specs=(rows, rows, P()) + (matrix,) * 12 + (turned,) * 4 + (vectors,) * 8 + (hidden,) * 4,
        check_vma=False,
    )
```

```python
import functools

import jax
import jax.numpy as jnp
from jax import lax
from jax.experimental import pallas as pl
from jax.experimental.pallas import tpu as pltpu
from jax.sharding import PartitionSpec as P

HEADS = 12
PAIRS = HEADS // 2

beta_one = 0.9
beta_two = 0.99
learn_rate = 0.01
weight_decay = 0.01
epsilon = 1e-08
clip_norm = 1.0
bias_one = 1.0 - beta_one**10
bias_two = 1.0 - beta_two**10

BF = jnp.bfloat16
F32 = jnp.float32
VMEM_LIMIT = 56 * 1024 * 1024


def dot_nn(a, b):
    return lax.dot_general(a, b, (((1,), (0,)), ((), ())), preferred_element_type=F32)


def dot_nt(a, b):
    return lax.dot_general(a, b, (((1,), (1,)), ((), ())), preferred_element_type=F32)


def dot_tn(a, b):
    return lax.dot_general(a, b, (((0,), (0,)), ((), ())), preferred_element_type=F32)


def normalize(stream):
    average = jnp.mean(stream, axis=-1, keepdims=True)
    centered = stream - average
    spread = jnp.mean(centered * centered, axis=-1, keepdims=True)
    root = lax.rsqrt(spread + 1e-05)
    return centered * root, root


def norm_backward(grad, unit, root, gain):
    scaled = grad * gain
    first = jnp.mean(scaled, axis=-1, keepdims=True)
    second = jnp.mean(scaled * unit, axis=-1, keepdims=True)
    return root * (scaled - first - unit * second)


def column_sum(value):
    return jnp.sum(value, axis=0, keepdims=True)


def split_heads(pair):
    lane = lax.broadcasted_iota(jnp.int32, pair.shape, 1)
    zero = jnp.zeros_like(pair)
    half = pair.shape[1] // 2
    return jnp.concatenate([jnp.where(lane < half, pair, zero), jnp.where(lane >= half, pair, zero)], axis=0)


def plane(me_ref, first, second, core):
    turned = jnp.bitwise_xor(jnp.bitwise_and(me_ref[1], 1), core) == 1
    return jnp.where(turned, second, first), jnp.where(turned, first, second)


def weight_copies(plan, refs, me_ref, full, sems):
    copies = []

    def add(source, part, rows):
        copies.append(pltpu.make_async_copy(source, full.at[part, rows, :], sems.at[part]))

    parts, width, _ = full.shape
    if plan[0] == "whole":
        for part in range(parts):
            add(refs[0].at[part], part, pl.ds(0, width))
    elif plan[0] == "rows":
        high = width * parts // refs[0].shape[0]
        for index in range(refs[0].shape[0]):
            stripe, part = divmod(index, parts)
            add(refs[0].at[index, pl.ds(plan[1], high), :], part, pl.ds(stripe * high, high))
    else:
        for ref, positions in zip(refs, plan[2]):
            depth = ref.shape[1]
            high = width // (2 * depth)
            for place, (first, second, core) in enumerate(positions):
                x, y = plane(me_ref, first, second, core)
                part = jnp.bitwise_xor(me_ref[1], 2 * y + core)
                if plan[3]:
                    side = jnp.bitwise_xor(jnp.bitwise_and(me_ref[0], 1), x)
                    stripes = full.reshape(parts, depth, 2, high, width).at[part, :, side]
                    source = ref.at[place, :, pl.ds(plan[1], high), :]
                    copies.append(pltpu.make_async_copy(source, stripes, sems.at[part]))
                    continue
                for z in range(depth):
                    start = pl.multiple_of(jnp.bitwise_xor(me_ref[0], 2 * z + x) * high, 16)
                    add(ref.at[place, z, pl.ds(plan[1], high), :], part, pl.ds(start, high))
    return copies


def start_weights(groups):
    for together in zip(*[weight_copies(*group) for group in groups]):
        for copy in together:
            copy.start()


def wait_weight(full, sems, part):
    pltpu.make_async_copy(full.at[part], full.at[part], sems.at[part]).wait()


def part_order(me_ref, plan, parts):
    if plan[0] != "near":
        return list(range(parts))
    return [jnp.bitwise_xor(me_ref[1], near) for near in (0, 2, 1, 3)]


def split_attention(raw, qkv_s, out_s):
    parts = raw.shape[0]
    cut = qkv_s.shape[1] // parts
    step = 96

    def relay(index, _):
        rows = pl.ds(pl.multiple_of(index * step, step), step)
        pieces = [raw[part, rows, :] for part in range(parts)]
        qkv_s[rows, :] = jnp.concatenate([piece[:, :cut] for piece in pieces], axis=1)
        out_s[rows, :] = jnp.concatenate([piece[:, cut:] for piece in pieces], axis=1)
        return 0

    lax.fori_loop(0, raw.shape[1] // step, relay, 0)


def attention_forward_kernel(plan, me_ref, stream_ref, mask_ref, vec_ref, *refs):
    weight_refs = refs[:-10]
    middle_ref, nffn_ref, normed_ref, proj_ref, probs_ref, mixed_ref, qkv_s, out_s, raw, sems = refs[-10:]

    @pl.when(pl.program_id(0) == 0)
    def _():
        start_weights([(plan, weight_refs, me_ref, raw, sems)])
        for part in range(raw.shape[0]):
            wait_weight(raw, sems, part)
        split_attention(raw, qkv_s, out_s)

    width = stream_ref.shape[1]
    slots = mask_ref.shape[1]
    scale = (width // HEADS) ** (-0.5)
    stream = stream_ref[...].astype(F32)
    unit, _ = normalize(stream)
    normed = (unit * vec_ref[0:1, :] + vec_ref[2:3, :]).astype(BF)
    normed_ref[...] = normed
    projected = dot_nn(normed, qkv_s[...])
    proj_ref[:, :width] = (projected[:, :width] + vec_ref[3:4, :]).astype(BF)
    proj_ref[:, width : 2 * width] = projected[:, width : 2 * width].astype(BF)
    proj_ref[:, 2 * width :] = (projected[:, 2 * width :] + vec_ref[4:5, :]).astype(BF)
    lanes = 2 * (width // HEADS)
    for page in range(mask_ref.shape[0]):
        rows = slice(page * slots, (page + 1) * slots)
        bias = mask_ref[page]
        for pair in range(PAIRS):
            at = pair * lanes
            queries = proj_ref[rows, at : at + lanes] * jnp.asarray(scale, BF)
            keys_in = split_heads(proj_ref[rows, width + at : width + at + lanes])
            values = split_heads(proj_ref[rows, 2 * width + at : 2 * width + at + lanes])
            scores = dot_nt(queries, keys_in)
            soft = []
            for head in range(2):
                masked = scores[:, head * slots : (head + 1) * slots] + bias
                peak = jnp.max(masked, axis=-1, keepdims=True)
                exponent = jnp.exp(masked - peak)
                total = jnp.sum(exponent, axis=-1, keepdims=True)
                soft.append((exponent * (1.0 / total)).astype(BF))
            probs = jnp.concatenate(soft, axis=1)
            probs_ref[page, pair] = probs
            mixed_ref[rows, at : at + lanes] = dot_nn(probs, values).astype(BF)
    middle = stream + dot_nn(mixed_ref[...], out_s[...]) + vec_ref[5:6, :]
    middle_ref[...] = middle
    unit, _ = normalize(middle)
    nffn_ref[...] = (unit * vec_ref[1:2, :] + vec_ref[6:7, :]).astype(BF)


def attention_forward(me, stream, mask, vec, weight, block_pages, parts):
    plan, arrays = weight
    rows, width = stream.shape
    pages, slots, _ = mask.shape
    block = block_pages * slots
    row_spec = lambda cols: pl.BlockSpec((block, cols), lambda i: (i, 0))
    return pl.pallas_call(
        functools.partial(attention_forward_kernel, plan),
        grid=(pages // block_pages,),
        in_specs=[
            pl.BlockSpec(memory_space=pltpu.SMEM),
            row_spec(width),
            pl.BlockSpec((block_pages, slots, slots), lambda i: (i, 0, 0)),
            pl.BlockSpec(vec.shape, lambda i: (0, 0)),
        ]
        + [pl.BlockSpec(memory_space=pl.ANY)] * len(arrays),
        out_specs=[
            row_spec(width),
            row_spec(width),
            row_spec(width),
            row_spec(3 * width),
            pl.BlockSpec((block_pages, PAIRS, slots, 2 * slots), lambda i: (i, 0, 0, 0)),
            row_spec(width),
            pl.BlockSpec((width, 3 * width), lambda i: (0, 0)),
            pl.BlockSpec((width, width), lambda i: (0, 0)),
        ],
        out_shape=[
            jax.ShapeDtypeStruct((rows, width), F32),
            jax.ShapeDtypeStruct((rows, width), BF),
            jax.ShapeDtypeStruct((rows, width), BF),
            jax.ShapeDtypeStruct((rows, 3 * width), BF),
            jax.ShapeDtypeStruct((pages, PAIRS, slots, 2 * slots), BF),
            jax.ShapeDtypeStruct((rows, width), BF),
            jax.ShapeDtypeStruct((width, 3 * width), BF),
            jax.ShapeDtypeStruct((width, width), BF),
        ],
        scratch_shapes=[
            pltpu.VMEM((parts, width, width), BF),
            pltpu.SemaphoreType.DMA((parts,)),
        ],
        compiler_params=pltpu.CompilerParams(vmem_limit_bytes=VMEM_LIMIT),
        cost_estimate=pl.CostEstimate(flops=20 * 10**9, bytes_accessed=30 * 10**6, transcendentals=0),
        name="attention_forward",
    )(me, stream, mask, vec, *arrays)


def ffn_forward_kernel(plans, me_ref, nffn_ref, middle_ref, vec_ref, hidden_ref, *refs):
    result_ref, active_ref, slope_ref, up_ref, down_ref, up_s, down_s, up_sems, down_sems = refs[-9:]
    up_refs = refs[: (len(refs) - 9) // 2]
    down_refs = refs[len(up_refs) : -9]
    kept = [pltpu.make_async_copy(up_s, up_ref, up_sems.at[0]), pltpu.make_async_copy(down_s, down_ref, down_sems.at[0])]

    first = pl.program_id(0) == 0
    parts, _, chunk = up_s.shape
    curve = 0.7978845608028654

    @pl.when(first)
    def _():
        start_weights([(plans[0], up_refs, me_ref, up_s, up_sems), (plans[1], down_refs, me_ref, down_s, down_sems)])

    def body(wait):
        nffn = nffn_ref[...]
        total = middle_ref[...] + vec_ref[7:8, :]
        for part in part_order(me_ref, plans[0], parts):
            cols = pl.ds(pl.multiple_of(part * chunk, chunk), chunk)
            if wait:
                wait_weight(up_s, up_sems, part)
            upper = dot_nn(nffn, up_s[part]) + hidden_ref[:, cols]
            square = upper * upper
            angle = jnp.tanh(upper * (curve + (curve * 0.044715) * square))
            half = 0.5 * upper
            lift = 1.0 + angle
            active = (half * lift).astype(BF)
            slope = 0.5 * lift + half * (1.0 - angle * angle) * (curve + (3.0 * curve * 0.044715) * square)
            active_ref[:, cols] = active
            slope_ref[:, cols] = slope.astype(BF)
            if wait:
                wait_weight(down_s, down_sems, part)
            total = total + dot_nt(active, down_s[part])
        result_ref[...] = total
        if wait:
            for copy in kept:
                copy.start()

    pl.when(first)(functools.partial(body, True))
    pl.when(jnp.logical_not(first))(functools.partial(body, False))

    @pl.when(pl.program_id(0) == pl.num_programs(0) - 1)
    def _():
        for copy in kept:
            copy.wait()


def ffn_forward(me, nffn, middle, vec, hidden, up_w, down_w, block, parts):
    rows, width = nffn.shape
    ffn = hidden.shape[1]
    arrays = up_w[1] + down_w[1]
    row_spec = lambda cols: pl.BlockSpec((block, cols), lambda i: (i, 0))
    return pl.pallas_call(
        functools.partial(ffn_forward_kernel, (up_w[0], down_w[0])),
        grid=(rows // block,),
        in_specs=[
            pl.BlockSpec(memory_space=pltpu.SMEM),
            row_spec(width),
            row_spec(width),
            pl.BlockSpec(vec.shape, lambda i: (0, 0)),
            pl.BlockSpec(hidden.shape, lambda i: (0, 0)),
        ]
        + [pl.BlockSpec(memory_space=pl.ANY)] * len(arrays),
        out_specs=[row_spec(width), row_spec(ffn), row_spec(ffn)] + [pl.BlockSpec(memory_space=pl.ANY)] * 2,
        out_shape=[
            jax.ShapeDtypeStruct((rows, width), F32),
            jax.ShapeDtypeStruct((rows, ffn), BF),
            jax.ShapeDtypeStruct((rows, ffn), BF),
        ]
        + [jax.ShapeDtypeStruct((parts, width, ffn // parts), BF)] * 2,
        scratch_shapes=[
            pltpu.VMEM((parts, width, ffn // parts), BF),
            pltpu.VMEM((parts, width, ffn // parts), BF),
            pltpu.SemaphoreType.DMA((parts,)),
            pltpu.SemaphoreType.DMA((parts,)),
        ],
        compiler_params=pltpu.CompilerParams(vmem_limit_bytes=VMEM_LIMIT),
        cost_estimate=pl.CostEstimate(flops=15 * 10**9, bytes_accessed=30 * 10**6, transcendentals=0),
        name="ffn_forward",
    )(me, nffn, middle, vec, hidden, *arrays)


def ffn_backward_kernel(plans, me_ref, grad_ref, slope_ref, middle_ref, vec_ref, *refs):
    gupper_ref, gmiddle_ref, small_ref, ghidden_ref, up_s, down_s, up_sems, down_sems = refs[-8:]
    up_refs = refs[: (len(refs) - 8) // 2]
    down_refs = refs[len(up_refs) : -8]

    first = pl.program_id(0) == 0
    parts, _, chunk = up_s.shape

    @pl.when(first)
    def _():
        start_weights([(plans[1], down_refs, me_ref, down_s, down_sems), (plans[0], up_refs, me_ref, up_s, up_sems)])
        small_ref[...] = jnp.zeros_like(small_ref)
        ghidden_ref[...] = jnp.zeros_like(ghidden_ref)

    def body(wait):
        grad = grad_ref[...].astype(F32)
        lower = grad.astype(BF)
        gnormed = jnp.zeros(grad.shape, F32)
        for part in part_order(me_ref, plans[0], parts):
            cols = pl.ds(pl.multiple_of(part * chunk, chunk), chunk)
            if wait:
                wait_weight(down_s, down_sems, part)
            gupper = (dot_nn(lower, down_s[part]) * slope_ref[:, cols].astype(F32)).astype(BF)
            gupper_ref[:, cols] = gupper
            ghidden_ref[:, cols] += column_sum(gupper.astype(F32))
            if wait:
                wait_weight(up_s, up_sems, part)
            gnormed = gnormed + dot_nt(gupper, up_s[part])
        unit, root = normalize(middle_ref[...])
        gmiddle = grad + norm_backward(gnormed, unit, root, vec_ref[1:2, :])
        gmiddle_ref[...] = gmiddle
        small_ref[0:1, :] += column_sum(gnormed * unit)
        small_ref[1:2, :] += column_sum(gnormed)
        small_ref[2:3, :] += column_sum(lower.astype(F32))
        small_ref[3:4, :] += column_sum(gmiddle.astype(BF).astype(F32))

    pl.when(first)(functools.partial(body, True))
    pl.when(jnp.logical_not(first))(functools.partial(body, False))


def ffn_backward(me, grad, slope, middle, vec, up_w, down_w, block, parts):
    rows, width = grad.shape
    ffn = slope.shape[1]
    arrays = up_w[1] + down_w[1]
    row_spec = lambda cols: pl.BlockSpec((block, cols), lambda i: (i, 0))
    return pl.pallas_call(
        functools.partial(ffn_backward_kernel, (up_w[0], down_w[0])),
        grid=(rows // block,),
        in_specs=[
            pl.BlockSpec(memory_space=pltpu.SMEM),
            row_spec(width),
            row_spec(ffn),
            row_spec(width),
            pl.BlockSpec(vec.shape, lambda i: (0, 0)),
        ]
        + [pl.BlockSpec(memory_space=pl.ANY)] * len(arrays),
        out_specs=[
            row_spec(ffn),
            row_spec(width),
            pl.BlockSpec((8, width), lambda i: (0, 0)),
            pl.BlockSpec((1, ffn), lambda i: (0, 0)),
        ],
        out_shape=[
            jax.ShapeDtypeStruct((rows, ffn), BF),
            jax.ShapeDtypeStruct((rows, width), F32),
            jax.ShapeDtypeStruct((8, width), F32),
            jax.ShapeDtypeStruct((1, ffn), F32),
        ],
        scratch_shapes=[
            pltpu.VMEM((parts, width, ffn // parts), BF),
            pltpu.VMEM((parts, width, ffn // parts), BF),
            pltpu.SemaphoreType.DMA((parts,)),
            pltpu.SemaphoreType.DMA((parts,)),
        ],
        compiler_params=pltpu.CompilerParams(vmem_limit_bytes=VMEM_LIMIT),
        cost_estimate=pl.CostEstimate(flops=15 * 10**9, bytes_accessed=30 * 10**6, transcendentals=0),
        name="ffn_backward",
    )(me, grad, slope, middle, vec, *arrays)


def ffn_both_kernel(plans, me_ref, nffn_ref, middle_ref, grad_ref, vec_ref, hidden_ref, *refs):
    result_ref, active_ref, gupper_ref, gmiddle_ref, small_ref, ghidden_ref, up_s, down_s, up_sems, down_sems = refs[-10:]
    up_refs = refs[: (len(refs) - 10) // 2]
    down_refs = refs[len(up_refs) : -10]
    first = pl.program_id(0) == 0
    parts, _, chunk = up_s.shape
    curve = 0.7978845608028654

    @pl.when(first)
    def _():
        start_weights([(plans[0], up_refs, me_ref, up_s, up_sems), (plans[1], down_refs, me_ref, down_s, down_sems)])
        small_ref[...] = jnp.zeros_like(small_ref)
        ghidden_ref[...] = jnp.zeros_like(ghidden_ref)

    def body(wait):
        nffn = nffn_ref[...]
        middle = middle_ref[...]
        grad = grad_ref[...].astype(F32)
        lower = grad.astype(BF)
        total = middle + vec_ref[7:8, :]
        gnormed = jnp.zeros(grad.shape, F32)
        for part in part_order(me_ref, plans[0], parts):
            cols = pl.ds(pl.multiple_of(part * chunk, chunk), chunk)
            if wait:
                wait_weight(up_s, up_sems, part)
                wait_weight(down_s, down_sems, part)
            gactive = dot_nn(lower, down_s[part])
            upper = dot_nn(nffn, up_s[part]) + hidden_ref[:, cols]
            square = upper * upper
            angle = jnp.tanh(upper * (curve + (curve * 0.044715) * square))
            half = 0.5 * upper
            lift = 1.0 + angle
            active = (half * lift).astype(BF)
            slope = 0.5 * lift + half * (1.0 - angle * angle) * (curve + (3.0 * curve * 0.044715) * square)
            gupper = (gactive * slope).astype(BF)
            active_ref[:, cols] = active
            gupper_ref[:, cols] = gupper
            ghidden_ref[:, cols] += column_sum(gupper.astype(F32))
            total = total + dot_nt(active, down_s[part])
            gnormed = gnormed + dot_nt(gupper, up_s[part])
        result_ref[...] = total
        unit, root = normalize(middle)
        gmiddle = grad + norm_backward(gnormed, unit, root, vec_ref[1:2, :])
        gmiddle_ref[...] = gmiddle
        small_ref[0:1, :] += column_sum(gnormed * unit)
        small_ref[1:2, :] += column_sum(gnormed)
        small_ref[2:3, :] += column_sum(lower.astype(F32))
        small_ref[3:4, :] += column_sum(gmiddle.astype(BF).astype(F32))

    pl.when(first)(functools.partial(body, True))
    pl.when(jnp.logical_not(first))(functools.partial(body, False))


def ffn_both(me, nffn, middle, grad, vec, hidden, up_w, down_w, block, parts):
    rows, width = nffn.shape
    ffn = hidden.shape[1]
    arrays = up_w[1] + down_w[1]
    row_spec = lambda cols: pl.BlockSpec((block, cols), lambda i: (i, 0))
    return pl.pallas_call(
        functools.partial(ffn_both_kernel, (up_w[0], down_w[0])),
        grid=(rows // block,),
        in_specs=[
            pl.BlockSpec(memory_space=pltpu.SMEM),
            row_spec(width),
            row_spec(width),
            row_spec(width),
            pl.BlockSpec(vec.shape, lambda i: (0, 0)),
            pl.BlockSpec(hidden.shape, lambda i: (0, 0)),
        ]
        + [pl.BlockSpec(memory_space=pl.ANY)] * len(arrays),
        out_specs=[
            row_spec(width),
            row_spec(ffn),
            row_spec(ffn),
            row_spec(width),
            pl.BlockSpec((8, width), lambda i: (0, 0)),
            pl.BlockSpec((1, ffn), lambda i: (0, 0)),
        ],
        out_shape=[
            jax.ShapeDtypeStruct((rows, width), F32),
            jax.ShapeDtypeStruct((rows, ffn), BF),
            jax.ShapeDtypeStruct((rows, ffn), BF),
            jax.ShapeDtypeStruct((rows, width), F32),
            jax.ShapeDtypeStruct((8, width), F32),
            jax.ShapeDtypeStruct((1, ffn), F32),
        ],
        scratch_shapes=[
            pltpu.VMEM((parts, width, ffn // parts), BF),
            pltpu.VMEM((parts, width, ffn // parts), BF),
            pltpu.SemaphoreType.DMA((parts,)),
            pltpu.SemaphoreType.DMA((parts,)),
        ],
        compiler_params=pltpu.CompilerParams(vmem_limit_bytes=VMEM_LIMIT),
        cost_estimate=pl.CostEstimate(flops=25 * 10**9, bytes_accessed=40 * 10**6, transcendentals=0),
        name="ffn_both",
    )(me, nffn, middle, grad, vec, hidden, *arrays)


def ffn_weight_kernel(nffn_ref, grad_ref, gupper_ref, active_ref, out_ref, nffn_t, grad_t):
    @pl.when(pl.program_id(0) == 0)
    def _():
        nffn_t[...] = nffn_ref[...].T
        grad_t[...] = grad_ref[...].astype(BF).T

    shape = (out_ref.shape[0],) + out_ref.shape[3:]
    out_ref[:, 0, 0] = dot_nn(nffn_t[...], gupper_ref[...]).astype(BF).reshape(shape)
    out_ref[:, 0, 1] = dot_nn(grad_t[...], active_ref[...]).astype(BF).reshape(shape)


def ffn_weight(nffn, grad, gupper, active, stripes, parts):
    rows, width = nffn.shape
    piece = gupper.shape[1] // parts
    high = width // stripes
    whole = pl.BlockSpec((rows, width), lambda i: (0, 0))
    return pl.pallas_call(
        ffn_weight_kernel,
        grid=(parts,),
        in_specs=[
            whole,
            whole,
            pl.BlockSpec((rows, piece), lambda i: (0, i)),
            pl.BlockSpec((rows, piece), lambda i: (0, i)),
        ],
        out_specs=pl.BlockSpec((stripes, 1, 2, high, piece), lambda i: (0, i, 0, 0, 0)),
        out_shape=jax.ShapeDtypeStruct((stripes, parts, 2, high, piece), BF),
        scratch_shapes=[pltpu.VMEM((width, rows), BF), pltpu.VMEM((width, rows), BF)],
        compiler_params=pltpu.CompilerParams(vmem_limit_bytes=VMEM_LIMIT),
        cost_estimate=pl.CostEstimate(flops=15 * 10**9, bytes_accessed=30 * 10**6, transcendentals=0),
        name="ffn_weight",
    )(nffn, grad, gupper, active)


def attention_backward_kernel(gmiddle_ref, stream_ref, proj_ref, probs_ref, vec_ref, qkv_s, out_s, *refs):
    gstream_ref, gproj_ref, small_ref, gmixed_s = refs[-4:]

    @pl.when(pl.program_id(0) == 0)
    def _():
        small_ref[...] = jnp.zeros_like(small_ref)

    width = stream_ref.shape[1]
    block_pages, _, slots, _ = probs_ref.shape
    scale = (width // HEADS) ** (-0.5)
    gmiddle = gmiddle_ref[...]
    gmixed_s[...] = dot_nt(gmiddle.astype(BF), out_s[...]).astype(BF)
    lanes = 2 * (width // HEADS)
    for page in range(block_pages):
        rows = slice(page * slots, (page + 1) * slots)
        for pair in range(PAIRS):
            at = pair * lanes
            gmixed = gmixed_s[rows, at : at + lanes]
            queries = split_heads(proj_ref[rows, at : at + lanes])
            keys_in = split_heads(proj_ref[rows, width + at : width + at + lanes])
            values = split_heads(proj_ref[rows, 2 * width + at : 2 * width + at + lanes])
            probs = probs_ref[page, pair]
            gsoft = dot_nt(gmixed, values)
            gscore = []
            for head in range(2):
                cols = slice(head * slots, (head + 1) * slots)
                soft = probs[:, cols].astype(F32)
                grad = gsoft[:, cols]
                inner = jnp.sum(soft * grad, axis=-1, keepdims=True)
                gscore.append((soft * (grad - inner)).astype(BF))
            stacked = jnp.concatenate([probs[:, :slots], probs[:, slots:]], axis=0)
            gvalues = dot_tn(stacked, split_heads(gmixed))
            gqueries = dot_nn(jnp.concatenate(gscore, axis=1), keys_in) * scale
            gkeys = dot_tn(jnp.concatenate(gscore, axis=0), queries) * scale
            gproj_ref[rows, at : at + lanes] = gqueries.astype(BF)
            gproj_ref[rows, width + at : width + at + lanes] = gkeys.astype(BF)
            gproj_ref[rows, 2 * width + at : 2 * width + at + lanes] = gvalues.astype(BF)
    gnormed = dot_nt(gproj_ref[...], qkv_s[...])
    unit, root = normalize(stream_ref[...].astype(F32))
    gstream_ref[...] = gmiddle + norm_backward(gnormed, unit, root, vec_ref[0:1, :])
    small_ref[0:1, :] += column_sum(gnormed * unit)
    small_ref[1:2, :] += column_sum(gnormed)
    small_ref[2:3, :] += column_sum(gproj_ref[:, :width].astype(F32))
    small_ref[3:4, :] += column_sum(gproj_ref[:, 2 * width :].astype(F32))


def attention_backward(gmiddle, stream, proj, probs, vec, weight, block_pages, begin, end, before):
    rows, width = stream.shape
    _, _, slots, _ = probs.shape
    block = block_pages * slots
    first = begin // block_pages
    row_spec = lambda cols: pl.BlockSpec((block, cols), lambda i: (i + first, 0))
    whole = lambda array: pl.BlockSpec(array.shape, lambda i: (0, 0))
    before = [] if before is None else list(before)
    operands = [gmiddle, stream, proj, probs, vec, weight[0], weight[1]]
    return pl.pallas_call(
        attention_backward_kernel,
        grid=((end - begin) // block_pages,),
        in_specs=[
            row_spec(width),
            row_spec(width),
            row_spec(3 * width),
            pl.BlockSpec((block_pages, PAIRS, slots, 2 * slots), lambda i: (i + first, 0, 0, 0)),
            whole(vec),
            whole(weight[0]),
            whole(weight[1]),
        ]
        + [pl.BlockSpec(memory_space=pl.ANY)] * len(before),
        out_specs=[row_spec(width), row_spec(3 * width), pl.BlockSpec((8, width), lambda i: (0, 0))],
        out_shape=[
            jax.ShapeDtypeStruct((rows, width), F32),
            jax.ShapeDtypeStruct((rows, 3 * width), BF),
            jax.ShapeDtypeStruct((8, width), F32),
        ],
        scratch_shapes=[pltpu.VMEM((block, width), BF)],
        input_output_aliases={len(operands) + index: index for index in range(len(before))},
        compiler_params=pltpu.CompilerParams(vmem_limit_bytes=VMEM_LIMIT),
        cost_estimate=pl.CostEstimate(flops=15 * 10**9, bytes_accessed=20 * 10**6, transcendentals=0),
        name="attention_backward",
    )(*operands, *before)


def attention_weight_kernel(normed_ref, mixed_ref, gproj_ref, gmiddle_ref, grad_ref):
    gqkv = dot_tn(normed_ref[...], gproj_ref[...])
    gout = dot_tn(mixed_ref[...], gmiddle_ref[...].astype(BF))
    parts = grad_ref.shape[1]
    cut = gqkv.shape[1] // parts
    rest = gout.shape[1] // parts
    shape = (grad_ref.shape[0],) + grad_ref.shape[3:]
    for part in range(parts):
        qkv_part = gqkv[:, part * cut : (part + 1) * cut].astype(BF)
        out_part = gout[:, part * rest : (part + 1) * rest].astype(BF)
        grad_ref[:, part, 0] = jnp.concatenate([qkv_part, out_part], axis=1).reshape(shape)


def attention_weight(normed, mixed, gproj, gmiddle, stripes, parts):
    rows, width = normed.shape
    block = width // 2
    high = width // stripes
    return pl.pallas_call(
        attention_weight_kernel,
        grid=(2,),
        in_specs=[
            pl.BlockSpec((rows, block), lambda i: (0, i)),
            pl.BlockSpec((rows, block), lambda i: (0, i)),
            pl.BlockSpec((rows, 3 * width), lambda i: (0, 0)),
            pl.BlockSpec((rows, width), lambda i: (0, 0)),
        ],
        out_specs=pl.BlockSpec((stripes // 2, parts, 1, high, width), lambda i: (i, 0, 0, 0, 0)),
        out_shape=jax.ShapeDtypeStruct((stripes, parts, 1, high, width), BF),
        compiler_params=pltpu.CompilerParams(vmem_limit_bytes=VMEM_LIMIT),
        cost_estimate=pl.CostEstimate(flops=10 * 10**9, bytes_accessed=20 * 10**6, transcendentals=0),
        name="attention_weight",
    )(normed, mixed, gproj, gmiddle)


def relative_rows(source, target, me, depth):
    high = source.shape[0] // (2 * depth)
    for x in range(2):
        for z in range(depth):
            start = pl.multiple_of(jnp.bitwise_xor(me, 2 * z + x) * high, 16)
            at = (x * depth + z) * high
            target[at : at + high, :] = source[pl.ds(start, high), :]


def send_out(me_ref, core, y, staged, slot, own_ref, other_ref, sems):
    for x in range(2):
        first, second = plane(me_ref, x, y, core)

        @pl.when(core == 0)
        def _():
            pltpu.make_async_copy(staged.at[slot, x], own_ref.at[second, first], sems.at[slot, x]).start()

        @pl.when(core == 1)
        def _():
            pltpu.make_async_copy(staged.at[slot, x], other_ref.at[second, first], sems.at[slot, x]).start()


def wait_out(staged, slot, own_ref, sems):
    for x in range(2):
        pltpu.make_async_copy(staged.at[slot, x], own_ref.at[0, 0], sems.at[slot, x]).wait()


def ffn_weight_split_kernel(core, me_ref, nffn_ref, grad_ref, gupper_ref, active_ref, out_ref, *refs):
    step = pl.program_id(0)
    staged, sems = refs[-2:]
    _, _, depth, high, width = staged.shape
    high = high // 2
    if core == 1:
        nffn_out, grad_out, turned, nffn_t, grad_t = refs[:-2]
        kept = [
            pltpu.make_async_copy(nffn_t, nffn_out, sems.at[2, 0]),
            pltpu.make_async_copy(grad_t, grad_out, sems.at[2, 1]),
        ]

        @pl.when(step == 0)
        def _():
            turned[...] = nffn_ref[...].T
            relative_rows(turned, nffn_t, me_ref[0], depth)
            turned[...] = grad_ref[...].astype(BF).T
            relative_rows(turned, grad_t, me_ref[0], depth)
            for copy in kept:
                copy.start()
    else:
        nffn_t, grad_t, kept = nffn_ref, grad_ref, []

    shape = (2, depth, high, width)
    staged[step, :, :, :high, :] = dot_nn(nffn_t[...], gupper_ref[...]).astype(BF).reshape(shape)
    staged[step, :, :, high:, :] = dot_nn(grad_t[...], active_ref[...]).astype(BF).reshape(shape)
    for x in range(2):
        first, second = plane(me_ref, x, step, core)
        pltpu.make_async_copy(staged.at[step, x], out_ref.at[second, first], sems.at[step, x]).start()

    @pl.when(step == 1)
    def _():
        wait_out(staged, 0, out_ref, sems)
        wait_out(staged, 1, out_ref, sems)
        for copy in kept:
            copy.wait()


def ffn_weight_split(me, nffn, grad, gupper, active, depth, core):
    rows, piece = gupper.shape[0], gupper.shape[1] // 4
    width = piece
    high = width // (2 * depth)
    whole = lambda array: pl.BlockSpec(array.shape, lambda i, me: (0, 0))
    column = pl.BlockSpec((rows, piece), lambda i, me: (0, jnp.bitwise_xor(me[1], 2 * i + core)))
    shape = (2, 2, depth, 2 * high, piece)
    return pl.pallas_call(
        functools.partial(ffn_weight_split_kernel, core),
        grid_spec=pltpu.PrefetchScalarGridSpec(
            num_scalar_prefetch=1,
            grid=(2,),
            in_specs=[whole(nffn), whole(grad), column, column],
            out_specs=[pl.BlockSpec(memory_space=pl.ANY)] * (1 + 2 * core),
            scratch_shapes=[pltpu.VMEM((width, rows), BF)] * (3 * core)
            + [pltpu.VMEM(shape, BF), pltpu.SemaphoreType.DMA((3, 2))],
        ),
        out_shape=[jax.ShapeDtypeStruct(shape, BF)] + [jax.ShapeDtypeStruct((width, rows), BF)] * (2 * core),
        compiler_params=pltpu.CompilerParams(vmem_limit_bytes=VMEM_LIMIT),
        cost_estimate=pl.CostEstimate(flops=8 * 10**9, bytes_accessed=15 * 10**6, transcendentals=0),
        name="ffn_weight",
    )(me, nffn, grad, gupper, active)


def attention_weight_split_kernel(me_ref, normed_ref, mixed_ref, gproj_ref, gmiddle_ref, *refs):
    other_ref, own_ref, turned, normed_t, mixed_t, found, staged, extra_s, sems = refs[-9:]
    extra_refs = refs[:-9]
    step = pl.program_id(0)
    _, _, depth, rows, width = staged.shape
    high = width // (2 * depth)
    share = width // 4
    shape = (2, depth, high, width)

    @pl.when(step == 0)
    def _():
        turned[...] = mixed_ref[...].T
        relative_rows(turned, mixed_t, me_ref[0], depth)
        found[:, 3 * width :] = dot_nn(mixed_t[...], gmiddle_ref[...].astype(BF)).astype(BF)
        turned[...] = normed_ref[...].T
        relative_rows(turned, normed_t, me_ref[0], depth)
        if extra_refs:
            extra_s[...] = jnp.zeros_like(extra_s)
            for index in range(2):
                one_ref, two_ref, hidden_ref = extra_refs[3 * index : 3 * index + 3]
                sums = jnp.concatenate([one_ref[:4, :], two_ref[:4, :]], axis=0)
                for part in range(4):
                    at = index * (width // 3)
                    extra_s[part, :8, at : at + share] = sums[:, part * share : (part + 1) * share]
                    extra_s[part, 8 + index : 9 + index, :] = hidden_ref[:, part * width : (part + 1) * width]
            for part in range(4):
                extra = extra_s[part].astype(BF)
                staged[part, :, :, high:, :] = jnp.broadcast_to(extra[None, None], (2, depth) + extra.shape)

    def finish(part):
        columns = slice(part * 3 * share, (part + 1) * 3 * share)
        rest = slice(3 * width + part * share, 3 * width + (part + 1) * share)
        staged[part, :, :, :high, :] = jnp.concatenate([found[:, columns], found[:, rest]], axis=1).reshape(shape)
        near = jnp.bitwise_xor(me_ref[1], part)
        send_out(me_ref, near % 2, near // 2, staged, part, own_ref, other_ref, sems)

    for third in range(3):

        @pl.when(step == third)
        def _():
            found[:, third * width : (third + 1) * width] = dot_nn(normed_t[...], gproj_ref[...]).astype(BF)
            for part in ((0,), (1,), (2, 3))[third]:
                finish(part)
            if third == 2:
                for part in range(4):
                    wait_out(staged, part, own_ref, sems)


def attention_weight_split(me, normed, mixed, gproj, gmiddle, depth, extra=None):
    rows, width = normed.shape
    high = width // (2 * depth)
    whole = lambda array: pl.BlockSpec(array.shape, lambda i: (0,) * array.ndim)
    extras = [] if extra is None else list(extra)
    shape = (2, 2, depth, high + (0 if extra is None else 16), width)
    operands = [normed, mixed, gproj, gmiddle] + extras
    return pl.pallas_call(
        attention_weight_split_kernel,
        grid=(3,),
        in_specs=[pl.BlockSpec(memory_space=pltpu.SMEM), whole(normed), whole(mixed)]
        + [pl.BlockSpec((rows, width), lambda i: (0, i))]
        + [whole(operand) for operand in operands[3:]],
        out_specs=[pl.BlockSpec(memory_space=pl.ANY)] * 2,
        out_shape=[jax.ShapeDtypeStruct(shape, BF)] * 2,
        scratch_shapes=[pltpu.VMEM((width, rows), BF)] * 3
        + [
            pltpu.VMEM((width, 4 * width), BF),
            pltpu.VMEM((4,) + shape[1:], BF),
            pltpu.VMEM((4, 16, width), F32),
            pltpu.SemaphoreType.DMA((4, 2)),
        ],
        compiler_params=pltpu.CompilerParams(vmem_limit_bytes=VMEM_LIMIT),
        cost_estimate=pl.CostEstimate(flops=10 * 10**9, bytes_accessed=20 * 10**6, transcendentals=0),
        name="attention_weight",
    )(me, *operands)


def pair_bias(slot_kind, slot_valid, across):
    same_kind = slot_kind[:, :, None] == slot_kind[:, None, :]
    partner = jnp.logical_not(same_kind) if across else same_kind
    allowed = jnp.logical_and(partner, slot_valid[:, None, :] > 0)
    return jnp.where(allowed, 0.0, -1e30).astype(F32)


def ordered_vectors(small_one, small_two):
    picked = (small_one, 0), (small_two, 0), (small_one, 1), (small_one, 2)
    picked += (small_one, 3), (small_two, 3), (small_two, 1), (small_two, 2)
    return jnp.stack([sums[row] for sums, row in picked])


def adam_step(master, grad, moment_one, moment_two, factor, decayed):
    clipped = grad * factor
    first_new = beta_one * moment_one + (1.0 - beta_one) * clipped
    second_new = beta_two * moment_two + (1.0 - beta_two) * clipped * clipped
    change = first_new / bias_one / (jnp.sqrt(second_new / bias_two) + epsilon)
    if decayed:
        change = change + weight_decay * master
    return (-learn_rate * change, first_new, second_new)


def gather_rows(pieces, sizes):
    kinds, high, width = pieces.shape
    rows = lax.all_gather(pieces.reshape(-1, width), ("dp", "tensor"), axis=0, tiled=False)
    if high % 16 == 0:
        return [(("rows", kind * high), [rows]) for kind in range(kinds)]
    split = rows.reshape(sizes["dp"], sizes["tensor"], kinds, high, width)
    return [(("whole",), [jnp.swapaxes(split[:, :, kind], 0, 1).reshape(-1, width, width)]) for kind in range(kinds)]


def scatter_rows(grad, sizes):
    stripes, parts, kinds, high, width = grad.shape
    inner = sizes["dp"] // stripes
    if inner > 1:
        grad = jnp.moveaxis(grad.reshape(stripes, parts, kinds, inner, high // inner, width), 3, 1)
    mine = lax.psum_scatter(grad.reshape(-1, width), ("dp", "tensor"), scatter_dimension=0, tiled=True)
    return mine.reshape(kinds, -1, width).astype(F32)


class Exchange:
    def __init__(self, sizes):
        self.sizes = sizes
        self.depth = sizes["dp"] // 2

    def swap(self, value, partner):
        dp, tensor = self.sizes["dp"], self.sizes["tensor"]
        pairs = []
        for i in range(dp):
            for j in range(tensor):
                far_i, far_j = partner(i, j)
                pairs.append((i * tensor + j, far_i * tensor + far_j))
        return lax.ppermute(value, ("dp", "tensor"), pairs)

    def part(self, bits, value):
        return self.swap(value, lambda i, j: (i, j ^ bits))

    def core(self, value):
        return self.part(1, value)

    def x(self, value):
        return self.swap(value, lambda i, j: (i ^ 1, j))

    def y(self, value):
        return self.part(2, value)

    def diagonal(self, value):
        return self.swap(value, lambda i, j: (i ^ 1, j ^ 2))

    def first(self, value):
        return self.swap(value, lambda i, j: (i, j ^ 2) if j & 1 else (i ^ 1, j))

    def second(self, value):
        return self.swap(value, lambda i, j: (i ^ 1, j) if j & 1 else (i, j ^ 2))

    def z(self, distance, value):
        return self.swap(value, lambda i, j: (i ^ (2 * distance), j))

    def z_sends(self, values):
        return [(functools.partial(self.z, distance), values[distance]) for distance in range(1, self.depth)]

    def gather_z(self, piece):
        groups = [[2 * z + x for z in range(self.depth)] for x in range(2)]
        return lax.all_gather(piece, "dp", axis=0, tiled=False, axis_index_groups=groups)

    def total(self, value):
        value = value + self.core(value)
        value = value + self.y(value)
        value = value + self.x(value)
        bit = 1
        while bit < self.depth:
            value = value + self.z(bit, value)
            bit *= 2
        return value


def tie(values, after):
    return lax.optimization_barrier((values, after))[0]


class Spread:
    def __init__(self, exchange, quad, fixed):
        self.exchange, self.quad, self.fixed = exchange, quad, fixed

    def go_first(self):
        return [(self.exchange.first, self.quad)]

    def go_second(self, came):
        self.pair = jnp.stack([self.quad, came[0]])
        return [(self.exchange.second, self.pair), (self.exchange.core, self.pair)]

    def go_core(self, came):
        self.two, self.far_pair = came
        return [(self.exchange.core, self.two)]

    def weight(self, came, offset=0):
        positions = [[(0, second, core), (1, second, core)] for core in range(2) for second in range(2)]
        arrays = [self.pair, self.two, self.far_pair, came[0]]
        return (("near", offset, positions, self.fixed), arrays)


class Reduce:
    def __init__(self, exchange, other, own):
        self.exchange, self.other, self.own = exchange, other, own

    def wide(self, value):
        return value.astype(F32)

    def go_core(self):
        return [(self.exchange.core, self.other)]

    def go_second(self, came):
        self.came = came[0]
        value = (self.wide(self.own[1]) + self.wide(self.came[1])).astype(BF)
        return [(self.exchange.second, value)]

    def go_first(self, came):
        self.beside = came[0]
        value = self.wide(self.own[0, 1]) + self.wide(self.came[0, 1]) + self.wide(self.beside[1])
        return [(self.exchange.first, value.astype(BF))]

    def depths(self, came):
        ahead = came[0]
        return (
            self.wide(self.own[0, 0]) + self.wide(self.came[0, 0]) + self.wide(self.beside[0]) + self.wide(ahead)
        )


def mid_first(sends):
    at = (len(sends) + 1) // 2 - 1
    return sends[at : at + 1] + sends[:at] + sends[at + 1 :]


class Lane:
    def __init__(self):
        self.last = None

    def after_last(self, values):
        return values if self.last is None else tie(values, self.last)

    def step(self, sends, kernel=None, arrays=()):
        values = [value for _, value in sends]
        values, arrays = self.after_last((values, list(arrays)))
        came = [move(value) for (move, _), value in zip(sends, values)]
        results = [] if kernel is None else list(kernel(*arrays))
        came, results = lax.optimization_barrier((came, results))
        self.last = results[-1] if results else came[-1]
        return came, results


def shards(
    sizes,
    tokens, out_grad, slot_kind, slot_valid,
    qkv_weight, qkv_first, qkv_second,
    out_weight, out_first, out_second,
    up_weight, up_first, up_second,
    down_weight, down_first, down_second,
    gain_weight, gain_first, gain_second,
    bias_weight, bias_first, bias_second,
    hidden_weight, hidden_first, hidden_second,
):
    parts = sizes["tensor"]
    width = tokens.shape[1]
    cut = qkv_weight.shape[2]
    high = qkv_weight.shape[1]
    split = parts == 4 and high % 32 == 0 and sizes["dp"] in (4, 8, 16)
    exchange = Exchange(sizes)
    stripes = sizes["dp"] if high % 16 == 0 else 2
    me = jnp.stack([lax.axis_index("dp"), lax.axis_index("tensor")]).astype(jnp.int32)
    attn_pieces = jnp.concatenate([qkv_weight.astype(BF), out_weight.astype(BF)], axis=2)
    up_pieces = up_weight.astype(BF)
    down_pieces = jnp.swapaxes(down_weight.astype(BF), 1, 2)
    pages = slot_kind.shape[0]
    block_pages = 2 if pages % 2 == 0 else 1
    block = block_pages * slot_kind.shape[1]
    masks = [pair_bias(slot_kind, slot_valid, index == 0) for index in range(2)]
    lane = Lane()
    gathered = lambda index: gather_rows(
        jnp.stack([attn_pieces[index], up_pieces[index], down_pieces[index]]), sizes
    )
    small = hidden = None
    saved = [None, None]

    def attention_forward_of(index, weight):
        return lambda stream: attention_forward(
            me, stream, masks[index], small[index], weight, block_pages, parts
        )

    def ffn_forward_of(index, up_w, down_w):
        return lambda nffn, middle: ffn_forward(
            me, nffn, middle, small[index], hidden[index : index + 1], up_w, down_w, block, parts
        )

    def ffn_backward_of(index):
        kept = saved[index]
        return lambda grad: ffn_backward(
            me, grad, kept["slope"], kept["middle"], small[index], kept["up_w"], kept["down_w"], block, parts
        )

    def ffn_weight_of(index, grad, turned=None):
        kept = saved[index]
        if not split:
            return lambda gupper: (ffn_weight(kept["nffn"], grad, gupper, kept["active"], stripes, parts),)
        core = 1 if turned is None else 0
        left, right = (kept["nffn"], grad) if turned is None else turned
        return lambda gupper: ffn_weight_split(me, left, right, gupper, kept["active"], exchange.depth, core)

    def attention_backward_of(index, begin, end, before=None):
        kept = saved[index]
        return lambda gmiddle: attention_backward(
            gmiddle, kept["stream"], kept["proj"], kept["probs"], small[index], kept["weight"],
            4 if pages % 4 == 0 else block_pages, begin, end, before,
        )

    def attention_weight_of(index, gmiddle, extra=None):
        kept = saved[index]
        if split:
            return lambda gproj: attention_weight_split(
                me, kept["normed"], kept["mixed"], gproj, gmiddle, exchange.depth, extra
            )
        return lambda gproj: (attention_weight(kept["normed"], kept["mixed"], gproj, gmiddle, stripes, parts),)

    def keep(index, stream, attention, ffn):
        middle, nffn, normed, proj, probs, mixed, qkv_w, out_w = attention
        saved[index] = dict(
            stream=stream, middle=middle, nffn=nffn, normed=normed, proj=proj, probs=probs, mixed=mixed,
            weight=(qkv_w, out_w), active=ffn[1],
        )
        if len(ffn) > 2:
            saved[index].update(slope=ffn[2], up_w=(("whole",), [ffn[3]]), down_w=(("whole",), [ffn[4]]))

    if split:
        depth = exchange.depth
        late = jnp.concatenate([attn_pieces[1], up_pieces[1], down_pieces[1]], axis=0)
        own_small = jnp.concatenate(
            [gain_weight, bias_weight, hidden_weight.reshape(2, -1, gain_weight.shape[2])], axis=1
        )
        own_small = lax.reduce_precision(own_small, 8, 7)
        small_sends = [(functools.partial(exchange.part, bits), own_small) for bits in range(1, 4)]
        late = exchange.gather_z(late)
        came, _ = lane.step(exchange.z_sends([attn_pieces[0]] * depth))
        attn_zero = Spread(exchange, jnp.stack([attn_pieces[0]] + came), False)
        ffn_piece = jnp.concatenate([up_pieces[0], down_pieces[0]], axis=0)
        ffn_sends = exchange.z_sends([ffn_piece] * depth)
        middle_at = depth // 2 - 1
        came, _ = lane.step(attn_zero.go_first() + ffn_sends[middle_at : middle_at + 1] + small_sends)
        ffn_came = came[1:2]
        mine = lax.axis_index("tensor")

        def order_small(*values):
            every = jnp.zeros((4,) + own_small.shape, F32)
            for bits, value in enumerate(values):
                every = lax.dynamic_update_slice_in_dim(every, value[None], jnp.bitwise_xor(mine, bits), 0)
            small = jnp.moveaxis(every[:, :, :8], 0, 2).reshape(2, 8, width)
            return small[0], small[1], jnp.moveaxis(every[:, :, 8:], 0, 1).reshape(2, -1)

        ffn_sends = ffn_sends[:middle_at] + ffn_sends[middle_at + 1 :]
        came, results = lane.step(attn_zero.go_second(came[:1]) + ffn_sends, order_small, [own_small] + came[2:])
        small, hidden = results[:2], results[2]
        others = came[2:]
        others.insert(middle_at, ffn_came[0])
        ffn_zero = Spread(exchange, jnp.stack([ffn_piece] + others), False)
        came, _ = lane.step(attn_zero.go_core(came[:2]) + ffn_zero.go_first())
        attn_w = attn_zero.weight(came[:1])
        came, attention = lane.step(ffn_zero.go_second(came[1:]), attention_forward_of(0, attn_w), [tokens])
        late = lane.after_last(late)
        attn_one = Spread(exchange, late[:, :high], True)
        ffn_one = Spread(exchange, late[:, high:], True)
        came, _ = lane.step(ffn_zero.go_core(came) + attn_one.go_first())
        up_w, down_w = ffn_zero.weight(came[:1]), ffn_zero.weight(came[:1], high)
        came, ffn = lane.step(
            attn_one.go_second(came[1:]) + ffn_one.go_first(), ffn_forward_of(0, up_w, down_w), attention[1::-1]
        )
        keep(0, tokens, attention, ffn)
        stream = ffn[0]
        ffn_came = came[2:]
        came, _ = lane.step(attn_one.go_core(came[:2]))
        attn_w = attn_one.weight(came)
        came, attention = lane.step(ffn_one.go_second(ffn_came), attention_forward_of(1, attn_w), [stream])
        came, _ = lane.step(ffn_one.go_core(came))
        up_w, down_w = ffn_one.weight(came), ffn_one.weight(came, high)
        both = lambda nffn, middle: ffn_both(
            me, nffn, middle, out_grad, small[1], hidden[1:], up_w, down_w, block, parts
        )
        _, results = lane.step([], both, attention[1::-1])
        block_output, active, gupper, gmiddle, small_two, hidden_one = results
        keep(1, stream, attention, (None, active))
        _, (other, *turned) = lane.step([], ffn_weight_of(1, out_grad), [gupper])
        came, (own,) = lane.step([(exchange.core, other)], ffn_weight_of(1, out_grad, turned), [gupper])
        ffn_one = Reduce(exchange, other, own)
        came, (grad, gproj, small_one) = lane.step(
            ffn_one.go_second(came), attention_backward_of(1, 0, pages), [gmiddle]
        )
        sums_one = (small_one, small_two, hidden_one)
        came, grads = lane.step(ffn_one.go_first(came), attention_weight_of(1, gmiddle), [gproj])
        ffn_layers = ffn_one.depths(came)
        ffn_sends = mid_first(exchange.z_sends([ffn_layers[z].astype(BF) for z in range(depth)]))
        attn_one = Reduce(exchange, *grads)
        came, results = lane.step(attn_one.go_core() + ffn_sends[:1], ffn_backward_of(0), [grad])
        ffn_came = came[1:]
        gupper, gmiddle, small_two, hidden_zero = results
        came, (other, *turned) = lane.step(
            attn_one.go_second(came[:1]) + ffn_sends[1:], ffn_weight_of(0, grad), [gupper]
        )
        ffn_came = ffn_came + came[1:]
        total = ffn_layers[0] + sum(value.astype(F32) for value in ffn_came)
        grad_up, grad_down = [None, total[:high]], [None, total[high:]]
        came, (own,) = lane.step(
            [(exchange.core, other)] + attn_one.go_first(came[:1]), ffn_weight_of(0, grad, turned), [gupper]
        )
        ffn_zero = Reduce(exchange, other, own)
        attn_layers = attn_one.depths(came[1:])
        attn_sends = mid_first(exchange.z_sends([attn_layers[z].astype(BF) for z in range(depth)]))
        came, (input_grad, gproj, small_one) = lane.step(
            ffn_zero.go_second(came[:1]) + attn_sends[:1], attention_backward_of(0, 0, pages), [gmiddle]
        )
        attn_came = came[1:]
        came, grads = lane.step(
            ffn_zero.go_first(came[:1]) + attn_sends[1:],
            attention_weight_of(0, gmiddle, (small_one, small_two, hidden_zero) + sums_one),
            [gproj],
        )
        grad_attn = [None, attn_layers[0] + sum(value.astype(F32) for value in attn_came + came[1:])]
        layers = ffn_zero.depths(came[:1])
        ffn_sends = exchange.z_sends([layers[z].astype(BF) for z in range(depth)])
        ffn_sends = mid_first(ffn_sends)
        attn_zero = Reduce(exchange, *grads)
        ((move, value),) = ffn_sends[:1]
        ffn_came = [move(lane.after_last(value))]
        came, _ = lane.step(attn_zero.go_core())
        came, _ = lane.step(attn_zero.go_second(came) + ffn_sends[1:])
        ffn_came = ffn_came + came[1:]
        came, _ = lane.step(attn_zero.go_first(came[:1]))
        total = layers[0] + sum(value.astype(F32) for value in ffn_came)
        grad_up[0], grad_down[0] = total[:high], total[high:]
        layers = attn_zero.depths(came[:1])
        came, _ = lane.step(exchange.z_sends([layers[z].astype(BF) for z in range(depth)]))
        total = layers[0] + sum(value.astype(F32) for value in came)
        grad_attn[0] = total[:high]
        shared_squares = jnp.sum(total[high:] * total[high:])
        share = width // parts
        vectors = []
        for at in (0, width // 3):
            sums = total[high : high + 8, at : at + share]
            vectors.append(ordered_vectors(sums[:4], sums[4:]))
        vectors = jnp.stack(vectors)
        grad_hidden = total[high + 8 : high + 10]
    else:
        small = jnp.concatenate([gain_weight, bias_weight], axis=1).astype(BF)
        small = lax.all_gather(small, "tensor", axis=2, tiled=True).astype(F32)
        hidden = lax.all_gather(hidden_weight.astype(BF), "tensor", axis=1, tiled=True).astype(F32)
        stream = tokens
        for index in range(2):
            attn_w, up_w, down_w = gathered(index)
            attention = attention_forward_of(index, attn_w)(stream)
            ffn = ffn_forward_of(index, up_w, down_w)(*attention[1::-1])
            keep(index, stream, attention, ffn)
            stream = ffn[0]
        block_output = stream
        grad = out_grad
        grad_attn, grad_up, grad_down, vectors, grad_hidden = ([None, None] for _ in range(5))
        for index in (1, 0):
            gupper, gmiddle, small_two, grad_hidden[index] = ffn_backward_of(index)(grad)
            (gffn,) = ffn_weight_of(index, grad)(gupper)
            grad_up[index], grad_down[index] = scatter_rows(gffn, sizes)
            grad, gproj, small_one = attention_backward_of(index, 0, pages)(gmiddle)
            (grad_attn[index],) = scatter_rows(attention_weight_of(index, gmiddle)(gproj)[0], sizes)
            vectors[index] = ordered_vectors(small_one, small_two)
        input_grad = grad
        vectors, grad_hidden = lax.psum((jnp.stack(vectors), jnp.concatenate(grad_hidden, axis=0)), ("dp", "tensor"))
        at = lax.axis_index("tensor")
        slice_of = lambda whole: lax.dynamic_slice_in_dim(
            whole, at * (whole.shape[-1] // parts), whole.shape[-1] // parts, whole.ndim - 1
        )
        vectors, grad_hidden = slice_of(vectors), slice_of(grad_hidden)
        shared_squares = jnp.sum(vectors * vectors) + jnp.sum(grad_hidden * grad_hidden)
    grad_gain, grad_bias = vectors[:, :2], vectors[:, 2:]
    local_squares = sum(jnp.sum(grad * grad) for pair in (grad_up, grad_down, grad_attn) for grad in pair[::-1])
    grad_attn, grad_up, grad_down = jnp.stack(grad_attn), jnp.stack(grad_up), jnp.stack(grad_down)
    local_squares = local_squares + jnp.where(lax.axis_index("dp") == 0, shared_squares, 0.0)
    grad_down = jnp.swapaxes(grad_down, 1, 2)
    if split:
        total_squares = exchange.total(local_squares.reshape(1, 1))[0, 0]
    else:
        total_squares = lax.psum(local_squares, ("dp", "tensor"))
    grad_norm = jnp.sqrt(total_squares)
    factor = clip_norm / jnp.maximum(grad_norm, clip_norm)
    masters = (qkv_weight, out_weight, up_weight, down_weight, gain_weight, bias_weight, hidden_weight)
    firsts = (qkv_first, out_first, up_first, down_first, gain_first, bias_first, hidden_first)
    seconds = (qkv_second, out_second, up_second, down_second, gain_second, bias_second, hidden_second)
    gradients = (
        grad_attn[:, :, :cut], grad_attn[:, :, cut:], grad_up, grad_down, grad_gain, grad_bias, grad_hidden,
    )
    results = [block_output, input_grad, grad_norm]
    for member in range(7):
        update, first_new, second_new = adam_step(
            masters[member], gradients[member], firsts[member], seconds[member], factor, member < 4
        )
        results = results + [gradients[member], update, first_new, second_new]
    return tuple(results)


def solution(mesh):
    rows = P(("dp", "tensor"), None)
    matrix = P(None, "dp", "tensor")
    turned = P(None, "tensor", "dp")
    vectors = P(None, None, "tensor")
    hidden = P(None, "tensor")
    return jax.shard_map(
        functools.partial(shards, dict(mesh.shape)),
        mesh=mesh,
        in_specs=(rows,) * 4 + (matrix,) * 9 + (turned,) * 3 + (vectors,) * 6 + (hidden,) * 3,
        out_specs=(rows, rows, P()) + (matrix,) * 12 + (turned,) * 4 + (vectors,) * 8 + (hidden,) * 4,
        check_vma=False,
    )
```

```python
import functools

import jax
import jax.numpy as jnp
from jax import lax
from jax.experimental import pallas as pl
from jax.experimental.pallas import tpu as pltpu
from jax.sharding import PartitionSpec as P

HEADS = 12
PAIRS = HEADS // 2

beta_one = 0.9
beta_two = 0.99
learn_rate = 0.01
weight_decay = 0.01
epsilon = 1e-08
clip_norm = 1.0
bias_one = 1.0 - beta_one**10
bias_two = 1.0 - beta_two**10

BF = jnp.bfloat16
F32 = jnp.float32
VMEM_LIMIT = 56 * 1024 * 1024


def dot_nn(a, b):
    return lax.dot_general(a, b, (((1,), (0,)), ((), ())), preferred_element_type=F32)


def dot_nt(a, b):
    return lax.dot_general(a, b, (((1,), (1,)), ((), ())), preferred_element_type=F32)


def dot_tn(a, b):
    return lax.dot_general(a, b, (((0,), (0,)), ((), ())), preferred_element_type=F32)


def normalize(stream):
    average = jnp.mean(stream, axis=-1, keepdims=True)
    centered = stream - average
    spread = jnp.mean(centered * centered, axis=-1, keepdims=True)
    root = lax.rsqrt(spread + 1e-05)
    return centered * root, root


def norm_backward(grad, unit, root, gain):
    scaled = grad * gain
    first = jnp.mean(scaled, axis=-1, keepdims=True)
    second = jnp.mean(scaled * unit, axis=-1, keepdims=True)
    return root * (scaled - first - unit * second)


def column_sum(value):
    return jnp.sum(value, axis=0, keepdims=True)


def split_heads(pair):
    lane = lax.broadcasted_iota(jnp.int32, pair.shape, 1)
    zero = jnp.zeros_like(pair)
    half = pair.shape[1] // 2
    return jnp.concatenate([jnp.where(lane < half, pair, zero), jnp.where(lane >= half, pair, zero)], axis=0)


def plane(me_ref, first, second, core):
    turned = jnp.bitwise_xor(jnp.bitwise_and(me_ref[1], 1), core) == 1
    return jnp.where(turned, second, first), jnp.where(turned, first, second)


def weight_copies(plan, refs, me_ref, full, sems):
    copies = []

    def add(source, part, rows):
        copies.append(pltpu.make_async_copy(source, full.at[part, rows, :], sems.at[part]))

    parts, width, _ = full.shape
    if plan[0] == "whole":
        for part in range(parts):
            add(refs[0].at[part], part, pl.ds(0, width))
    elif plan[0] == "rows":
        high = width * parts // refs[0].shape[0]
        for index in range(refs[0].shape[0]):
            stripe, part = divmod(index, parts)
            add(refs[0].at[index, pl.ds(plan[1], high), :], part, pl.ds(stripe * high, high))
    else:
        for ref, positions in zip(refs, plan[2]):
            depth = ref.shape[1]
            high = width // (2 * depth)
            for place, (first, second, core) in enumerate(positions):
                x, y = plane(me_ref, first, second, core)
                part = jnp.bitwise_xor(me_ref[1], 2 * y + core)
                if plan[3]:
                    side = jnp.bitwise_xor(jnp.bitwise_and(me_ref[0], 1), x)
                    stripes = full.reshape(parts, depth, 2, high, width).at[part, :, side]
                    source = ref.at[place, :, pl.ds(plan[1], high), :]
                    copies.append(pltpu.make_async_copy(source, stripes, sems.at[part]))
                    continue
                for z in range(depth):
                    start = pl.multiple_of(jnp.bitwise_xor(me_ref[0], 2 * z + x) * high, 16)
                    add(ref.at[place, z, pl.ds(plan[1], high), :], part, pl.ds(start, high))
    return copies


def start_weights(groups):
    for together in zip(*[weight_copies(*group) for group in groups]):
        for copy in together:
            copy.start()


def wait_weight(full, sems, part):
    pltpu.make_async_copy(full.at[part], full.at[part], sems.at[part]).wait()


def part_order(me_ref, plan, parts):
    if plan[0] != "near":
        return list(range(parts))
    return [jnp.bitwise_xor(me_ref[1], near) for near in (0, 2, 1, 3)]


def split_attention(raw, qkv_s, out_s):
    parts = raw.shape[0]
    cut = qkv_s.shape[1] // parts
    step = 96

    def relay(index, _):
        rows = pl.ds(pl.multiple_of(index * step, step), step)
        pieces = [raw[part, rows, :] for part in range(parts)]
        qkv_s[rows, :] = jnp.concatenate([piece[:, :cut] for piece in pieces], axis=1)
        out_s[rows, :] = jnp.concatenate([piece[:, cut:] for piece in pieces], axis=1)
        return 0

    lax.fori_loop(0, raw.shape[1] // step, relay, 0)


def attention_forward_kernel(plan, me_ref, stream_ref, mask_ref, vec_ref, *refs):
    weight_refs = refs[:-10]
    middle_ref, nffn_ref, normed_ref, proj_ref, probs_ref, mixed_ref, qkv_s, out_s, raw, sems = refs[-10:]

    @pl.when(pl.program_id(0) == 0)
    def _():
        start_weights([(plan, weight_refs, me_ref, raw, sems)])
        for part in range(raw.shape[0]):
            wait_weight(raw, sems, part)
        split_attention(raw, qkv_s, out_s)

    width = stream_ref.shape[1]
    slots = mask_ref.shape[1]
    scale = (width // HEADS) ** (-0.5)
    stream = stream_ref[...].astype(F32)
    unit, _ = normalize(stream)
    normed = (unit * vec_ref[0:1, :] + vec_ref[2:3, :]).astype(BF)
    normed_ref[...] = normed
    projected = dot_nn(normed, qkv_s[...])
    proj_ref[:, :width] = (projected[:, :width] + vec_ref[3:4, :]).astype(BF)
    proj_ref[:, width : 2 * width] = projected[:, width : 2 * width].astype(BF)
    proj_ref[:, 2 * width :] = (projected[:, 2 * width :] + vec_ref[4:5, :]).astype(BF)
    lanes = 2 * (width // HEADS)
    for page in range(mask_ref.shape[0]):
        rows = slice(page * slots, (page + 1) * slots)
        bias = mask_ref[page]
        for pair in range(PAIRS):
            at = pair * lanes
            queries = proj_ref[rows, at : at + lanes] * jnp.asarray(scale, BF)
            keys_in = split_heads(proj_ref[rows, width + at : width + at + lanes])
            values = split_heads(proj_ref[rows, 2 * width + at : 2 * width + at + lanes])
            scores = dot_nt(queries, keys_in)
            soft = []
            for head in range(2):
                masked = scores[:, head * slots : (head + 1) * slots] + bias
                peak = jnp.max(masked, axis=-1, keepdims=True)
                exponent = jnp.exp(masked - peak)
                total = jnp.sum(exponent, axis=-1, keepdims=True)
                soft.append((exponent * (1.0 / total)).astype(BF))
            probs = jnp.concatenate(soft, axis=1)
            probs_ref[page, pair] = probs
            mixed_ref[rows, at : at + lanes] = dot_nn(probs, values).astype(BF)
    middle = stream + dot_nn(mixed_ref[...], out_s[...]) + vec_ref[5:6, :]
    middle_ref[...] = middle
    unit, _ = normalize(middle)
    nffn_ref[...] = (unit * vec_ref[1:2, :] + vec_ref[6:7, :]).astype(BF)


def attention_forward(me, stream, mask, vec, weight, block_pages, parts):
    plan, arrays = weight
    rows, width = stream.shape
    pages, slots, _ = mask.shape
    block = block_pages * slots
    row_spec = lambda cols: pl.BlockSpec((block, cols), lambda i: (i, 0))
    return pl.pallas_call(
        functools.partial(attention_forward_kernel, plan),
        grid=(pages // block_pages,),
        in_specs=[
            pl.BlockSpec(memory_space=pltpu.SMEM),
            row_spec(width),
            pl.BlockSpec((block_pages, slots, slots), lambda i: (i, 0, 0)),
            pl.BlockSpec(vec.shape, lambda i: (0, 0)),
        ]
        + [pl.BlockSpec(memory_space=pl.ANY)] * len(arrays),
        out_specs=[
            row_spec(width),
            row_spec(width),
            row_spec(width),
            row_spec(3 * width),
            pl.BlockSpec((block_pages, PAIRS, slots, 2 * slots), lambda i: (i, 0, 0, 0)),
            row_spec(width),
            pl.BlockSpec((width, 3 * width), lambda i: (0, 0)),
            pl.BlockSpec((width, width), lambda i: (0, 0)),
        ],
        out_shape=[
            jax.ShapeDtypeStruct((rows, width), F32),
            jax.ShapeDtypeStruct((rows, width), BF),
            jax.ShapeDtypeStruct((rows, width), BF),
            jax.ShapeDtypeStruct((rows, 3 * width), BF),
            jax.ShapeDtypeStruct((pages, PAIRS, slots, 2 * slots), BF),
            jax.ShapeDtypeStruct((rows, width), BF),
            jax.ShapeDtypeStruct((width, 3 * width), BF),
            jax.ShapeDtypeStruct((width, width), BF),
        ],
        scratch_shapes=[
            pltpu.VMEM((parts, width, width), BF),
            pltpu.SemaphoreType.DMA((parts,)),
        ],
        compiler_params=pltpu.CompilerParams(vmem_limit_bytes=VMEM_LIMIT),
        cost_estimate=pl.CostEstimate(flops=20 * 10**9, bytes_accessed=30 * 10**6, transcendentals=0),
        name="attention_forward",
    )(me, stream, mask, vec, *arrays)


def ffn_forward_kernel(plans, me_ref, nffn_ref, middle_ref, vec_ref, hidden_ref, *refs):
    result_ref, active_ref, slope_ref, up_ref, down_ref, up_s, down_s, up_sems, down_sems = refs[-9:]
    up_refs = refs[: (len(refs) - 9) // 2]
    down_refs = refs[len(up_refs) : -9]
    kept = [pltpu.make_async_copy(up_s, up_ref, up_sems.at[0]), pltpu.make_async_copy(down_s, down_ref, down_sems.at[0])]

    first = pl.program_id(0) == 0
    parts, _, chunk = up_s.shape
    curve = 0.7978845608028654

    @pl.when(first)
    def _():
        start_weights([(plans[0], up_refs, me_ref, up_s, up_sems), (plans[1], down_refs, me_ref, down_s, down_sems)])

    def body(wait):
        nffn = nffn_ref[...]
        total = middle_ref[...] + vec_ref[7:8, :]
        for part in part_order(me_ref, plans[0], parts):
            cols = pl.ds(pl.multiple_of(part * chunk, chunk), chunk)
            if wait:
                wait_weight(up_s, up_sems, part)
            upper = dot_nn(nffn, up_s[part]) + hidden_ref[:, cols]
            square = upper * upper
            angle = jnp.tanh(upper * (curve + (curve * 0.044715) * square))
            half = 0.5 * upper
            lift = 1.0 + angle
            active = (half * lift).astype(BF)
            slope = 0.5 * lift + half * (1.0 - angle * angle) * (curve + (3.0 * curve * 0.044715) * square)
            active_ref[:, cols] = active
            slope_ref[:, cols] = slope.astype(BF)
            if wait:
                wait_weight(down_s, down_sems, part)
            total = total + dot_nt(active, down_s[part])
        result_ref[...] = total
        if wait:
            for copy in kept:
                copy.start()

    pl.when(first)(functools.partial(body, True))
    pl.when(jnp.logical_not(first))(functools.partial(body, False))

    @pl.when(pl.program_id(0) == pl.num_programs(0) - 1)
    def _():
        for copy in kept:
            copy.wait()


def ffn_forward(me, nffn, middle, vec, hidden, up_w, down_w, block, parts):
    rows, width = nffn.shape
    ffn = hidden.shape[1]
    arrays = up_w[1] + down_w[1]
    row_spec = lambda cols: pl.BlockSpec((block, cols), lambda i: (i, 0))
    return pl.pallas_call(
        functools.partial(ffn_forward_kernel, (up_w[0], down_w[0])),
        grid=(rows // block,),
        in_specs=[
            pl.BlockSpec(memory_space=pltpu.SMEM),
            row_spec(width),
            row_spec(width),
            pl.BlockSpec(vec.shape, lambda i: (0, 0)),
            pl.BlockSpec(hidden.shape, lambda i: (0, 0)),
        ]
        + [pl.BlockSpec(memory_space=pl.ANY)] * len(arrays),
        out_specs=[row_spec(width), row_spec(ffn), row_spec(ffn)] + [pl.BlockSpec(memory_space=pl.ANY)] * 2,
        out_shape=[
            jax.ShapeDtypeStruct((rows, width), F32),
            jax.ShapeDtypeStruct((rows, ffn), BF),
            jax.ShapeDtypeStruct((rows, ffn), BF),
        ]
        + [jax.ShapeDtypeStruct((parts, width, ffn // parts), BF)] * 2,
        scratch_shapes=[
            pltpu.VMEM((parts, width, ffn // parts), BF),
            pltpu.VMEM((parts, width, ffn // parts), BF),
            pltpu.SemaphoreType.DMA((parts,)),
            pltpu.SemaphoreType.DMA((parts,)),
        ],
        compiler_params=pltpu.CompilerParams(vmem_limit_bytes=VMEM_LIMIT),
        cost_estimate=pl.CostEstimate(flops=15 * 10**9, bytes_accessed=30 * 10**6, transcendentals=0),
        name="ffn_forward",
    )(me, nffn, middle, vec, hidden, *arrays)


def ffn_backward_kernel(plans, me_ref, grad_ref, slope_ref, middle_ref, vec_ref, *refs):
    gupper_ref, gmiddle_ref, small_ref, ghidden_ref, up_s, down_s, up_sems, down_sems = refs[-8:]
    up_refs = refs[: (len(refs) - 8) // 2]
    down_refs = refs[len(up_refs) : -8]

    first = pl.program_id(0) == 0
    parts, _, chunk = up_s.shape

    @pl.when(first)
    def _():
        start_weights([(plans[1], down_refs, me_ref, down_s, down_sems), (plans[0], up_refs, me_ref, up_s, up_sems)])
        small_ref[...] = jnp.zeros_like(small_ref)
        ghidden_ref[...] = jnp.zeros_like(ghidden_ref)

    def body(wait):
        grad = grad_ref[...].astype(F32)
        lower = grad.astype(BF)
        gnormed = jnp.zeros(grad.shape, F32)
        for part in part_order(me_ref, plans[0], parts):
            cols = pl.ds(pl.multiple_of(part * chunk, chunk), chunk)
            if wait:
                wait_weight(down_s, down_sems, part)
            gupper = (dot_nn(lower, down_s[part]) * slope_ref[:, cols].astype(F32)).astype(BF)
            gupper_ref[:, cols] = gupper
            ghidden_ref[:, cols] += column_sum(gupper.astype(F32))
            if wait:
                wait_weight(up_s, up_sems, part)
            gnormed = gnormed + dot_nt(gupper, up_s[part])
        unit, root = normalize(middle_ref[...])
        gmiddle = grad + norm_backward(gnormed, unit, root, vec_ref[1:2, :])
        gmiddle_ref[...] = gmiddle
        small_ref[0:1, :] += column_sum(gnormed * unit)
        small_ref[1:2, :] += column_sum(gnormed)
        small_ref[2:3, :] += column_sum(lower.astype(F32))
        small_ref[3:4, :] += column_sum(gmiddle.astype(BF).astype(F32))

    pl.when(first)(functools.partial(body, True))
    pl.when(jnp.logical_not(first))(functools.partial(body, False))


def ffn_backward(me, grad, slope, middle, vec, up_w, down_w, block, parts):
    rows, width = grad.shape
    ffn = slope.shape[1]
    arrays = up_w[1] + down_w[1]
    row_spec = lambda cols: pl.BlockSpec((block, cols), lambda i: (i, 0))
    return pl.pallas_call(
        functools.partial(ffn_backward_kernel, (up_w[0], down_w[0])),
        grid=(rows // block,),
        in_specs=[
            pl.BlockSpec(memory_space=pltpu.SMEM),
            row_spec(width),
            row_spec(ffn),
            row_spec(width),
            pl.BlockSpec(vec.shape, lambda i: (0, 0)),
        ]
        + [pl.BlockSpec(memory_space=pl.ANY)] * len(arrays),
        out_specs=[
            row_spec(ffn),
            row_spec(width),
            pl.BlockSpec((8, width), lambda i: (0, 0)),
            pl.BlockSpec((1, ffn), lambda i: (0, 0)),
        ],
        out_shape=[
            jax.ShapeDtypeStruct((rows, ffn), BF),
            jax.ShapeDtypeStruct((rows, width), F32),
            jax.ShapeDtypeStruct((8, width), F32),
            jax.ShapeDtypeStruct((1, ffn), F32),
        ],
        scratch_shapes=[
            pltpu.VMEM((parts, width, ffn // parts), BF),
            pltpu.VMEM((parts, width, ffn // parts), BF),
            pltpu.SemaphoreType.DMA((parts,)),
            pltpu.SemaphoreType.DMA((parts,)),
        ],
        compiler_params=pltpu.CompilerParams(vmem_limit_bytes=VMEM_LIMIT),
        cost_estimate=pl.CostEstimate(flops=15 * 10**9, bytes_accessed=30 * 10**6, transcendentals=0),
        name="ffn_backward",
    )(me, grad, slope, middle, vec, *arrays)


def ffn_both_kernel(plans, me_ref, nffn_ref, middle_ref, grad_ref, vec_ref, hidden_ref, *refs):
    result_ref, active_ref, gupper_ref, gmiddle_ref, small_ref, ghidden_ref, up_s, down_s, up_sems, down_sems = refs[-10:]
    up_refs = refs[: (len(refs) - 10) // 2]
    down_refs = refs[len(up_refs) : -10]
    first = pl.program_id(0) == 0
    parts, _, chunk = up_s.shape
    curve = 0.7978845608028654

    @pl.when(first)
    def _():
        start_weights([(plans[0], up_refs, me_ref, up_s, up_sems), (plans[1], down_refs, me_ref, down_s, down_sems)])
        small_ref[...] = jnp.zeros_like(small_ref)
        ghidden_ref[...] = jnp.zeros_like(ghidden_ref)

    def body(wait):
        nffn = nffn_ref[...]
        middle = middle_ref[...]
        grad = grad_ref[...].astype(F32)
        lower = grad.astype(BF)
        total = middle + vec_ref[7:8, :]
        gnormed = jnp.zeros(grad.shape, F32)
        for part in part_order(me_ref, plans[0], parts):
            cols = pl.ds(pl.multiple_of(part * chunk, chunk), chunk)
            if wait:
                wait_weight(up_s, up_sems, part)
                wait_weight(down_s, down_sems, part)
            gactive = dot_nn(lower, down_s[part])
            upper = dot_nn(nffn, up_s[part]) + hidden_ref[:, cols]
            square = upper * upper
            angle = jnp.tanh(upper * (curve + (curve * 0.044715) * square))
            half = 0.5 * upper
            lift = 1.0 + angle
            active = (half * lift).astype(BF)
            slope = 0.5 * lift + half * (1.0 - angle * angle) * (curve + (3.0 * curve * 0.044715) * square)
            gupper = (gactive * slope).astype(BF)
            active_ref[:, cols] = active
            gupper_ref[:, cols] = gupper
            ghidden_ref[:, cols] += column_sum(gupper.astype(F32))
            total = total + dot_nt(active, down_s[part])
            gnormed = gnormed + dot_nt(gupper, up_s[part])
        result_ref[...] = total
        unit, root = normalize(middle)
        gmiddle = grad + norm_backward(gnormed, unit, root, vec_ref[1:2, :])
        gmiddle_ref[...] = gmiddle
        small_ref[0:1, :] += column_sum(gnormed * unit)
        small_ref[1:2, :] += column_sum(gnormed)
        small_ref[2:3, :] += column_sum(lower.astype(F32))
        small_ref[3:4, :] += column_sum(gmiddle.astype(BF).astype(F32))

    pl.when(first)(functools.partial(body, True))
    pl.when(jnp.logical_not(first))(functools.partial(body, False))


def ffn_both(me, nffn, middle, grad, vec, hidden, up_w, down_w, block, parts):
    rows, width = nffn.shape
    ffn = hidden.shape[1]
    arrays = up_w[1] + down_w[1]
    row_spec = lambda cols: pl.BlockSpec((block, cols), lambda i: (i, 0))
    return pl.pallas_call(
        functools.partial(ffn_both_kernel, (up_w[0], down_w[0])),
        grid=(rows // block,),
        in_specs=[
            pl.BlockSpec(memory_space=pltpu.SMEM),
            row_spec(width),
            row_spec(width),
            row_spec(width),
            pl.BlockSpec(vec.shape, lambda i: (0, 0)),
            pl.BlockSpec(hidden.shape, lambda i: (0, 0)),
        ]
        + [pl.BlockSpec(memory_space=pl.ANY)] * len(arrays),
        out_specs=[
            row_spec(width),
            row_spec(ffn),
            row_spec(ffn),
            row_spec(width),
            pl.BlockSpec((8, width), lambda i: (0, 0)),
            pl.BlockSpec((1, ffn), lambda i: (0, 0)),
        ],
        out_shape=[
            jax.ShapeDtypeStruct((rows, width), F32),
            jax.ShapeDtypeStruct((rows, ffn), BF),
            jax.ShapeDtypeStruct((rows, ffn), BF),
            jax.ShapeDtypeStruct((rows, width), F32),
            jax.ShapeDtypeStruct((8, width), F32),
            jax.ShapeDtypeStruct((1, ffn), F32),
        ],
        scratch_shapes=[
            pltpu.VMEM((parts, width, ffn // parts), BF),
            pltpu.VMEM((parts, width, ffn // parts), BF),
            pltpu.SemaphoreType.DMA((parts,)),
            pltpu.SemaphoreType.DMA((parts,)),
        ],
        compiler_params=pltpu.CompilerParams(vmem_limit_bytes=VMEM_LIMIT),
        cost_estimate=pl.CostEstimate(flops=25 * 10**9, bytes_accessed=40 * 10**6, transcendentals=0),
        name="ffn_both",
    )(me, nffn, middle, grad, vec, hidden, *arrays)


def ffn_weight_kernel(nffn_ref, grad_ref, gupper_ref, active_ref, out_ref, nffn_t, grad_t):
    @pl.when(pl.program_id(0) == 0)
    def _():
        nffn_t[...] = nffn_ref[...].T
        grad_t[...] = grad_ref[...].astype(BF).T

    shape = (out_ref.shape[0],) + out_ref.shape[3:]
    out_ref[:, 0, 0] = dot_nn(nffn_t[...], gupper_ref[...]).astype(BF).reshape(shape)
    out_ref[:, 0, 1] = dot_nn(grad_t[...], active_ref[...]).astype(BF).reshape(shape)


def ffn_weight(nffn, grad, gupper, active, stripes, parts):
    rows, width = nffn.shape
    piece = gupper.shape[1] // parts
    high = width // stripes
    whole = pl.BlockSpec((rows, width), lambda i: (0, 0))
    return pl.pallas_call(
        ffn_weight_kernel,
        grid=(parts,),
        in_specs=[
            whole,
            whole,
            pl.BlockSpec((rows, piece), lambda i: (0, i)),
            pl.BlockSpec((rows, piece), lambda i: (0, i)),
        ],
        out_specs=pl.BlockSpec((stripes, 1, 2, high, piece), lambda i: (0, i, 0, 0, 0)),
        out_shape=jax.ShapeDtypeStruct((stripes, parts, 2, high, piece), BF),
        scratch_shapes=[pltpu.VMEM((width, rows), BF), pltpu.VMEM((width, rows), BF)],
        compiler_params=pltpu.CompilerParams(vmem_limit_bytes=VMEM_LIMIT),
        cost_estimate=pl.CostEstimate(flops=15 * 10**9, bytes_accessed=30 * 10**6, transcendentals=0),
        name="ffn_weight",
    )(nffn, grad, gupper, active)


def attention_backward_kernel(gmiddle_ref, stream_ref, proj_ref, probs_ref, vec_ref, qkv_s, out_s, *refs):
    gstream_ref, gproj_ref, small_ref, gmixed_s = refs[-4:]

    @pl.when(pl.program_id(0) == 0)
    def _():
        small_ref[...] = jnp.zeros_like(small_ref)

    width = stream_ref.shape[1]
    block_pages, _, slots, _ = probs_ref.shape
    scale = (width // HEADS) ** (-0.5)
    gmiddle = gmiddle_ref[...]
    gmixed_s[...] = dot_nt(gmiddle.astype(BF), out_s[...]).astype(BF)
    lanes = 2 * (width // HEADS)
    for page in range(block_pages):
        rows = slice(page * slots, (page + 1) * slots)
        for pair in range(PAIRS):
            at = pair * lanes
            gmixed = gmixed_s[rows, at : at + lanes]
            queries = split_heads(proj_ref[rows, at : at + lanes])
            keys_in = split_heads(proj_ref[rows, width + at : width + at + lanes])
            values = split_heads(proj_ref[rows, 2 * width + at : 2 * width + at + lanes])
            probs = probs_ref[page, pair]
            gsoft = dot_nt(gmixed, values)
            gscore = []
            for head in range(2):
                cols = slice(head * slots, (head + 1) * slots)
                soft = probs[:, cols].astype(F32)
                grad = gsoft[:, cols]
                inner = jnp.sum(soft * grad, axis=-1, keepdims=True)
                gscore.append((soft * (grad - inner)).astype(BF))
            stacked = jnp.concatenate([probs[:, :slots], probs[:, slots:]], axis=0)
            gvalues = dot_tn(stacked, split_heads(gmixed))
            gqueries = dot_nn(jnp.concatenate(gscore, axis=1), keys_in) * scale
            gkeys = dot_tn(jnp.concatenate(gscore, axis=0), queries) * scale
            gproj_ref[rows, at : at + lanes] = gqueries.astype(BF)
            gproj_ref[rows, width + at : width + at + lanes] = gkeys.astype(BF)
            gproj_ref[rows, 2 * width + at : 2 * width + at + lanes] = gvalues.astype(BF)
    gnormed = dot_nt(gproj_ref[...], qkv_s[...])
    unit, root = normalize(stream_ref[...].astype(F32))
    gstream_ref[...] = gmiddle + norm_backward(gnormed, unit, root, vec_ref[0:1, :])
    small_ref[0:1, :] += column_sum(gnormed * unit)
    small_ref[1:2, :] += column_sum(gnormed)
    small_ref[2:3, :] += column_sum(gproj_ref[:, :width].astype(F32))
    small_ref[3:4, :] += column_sum(gproj_ref[:, 2 * width :].astype(F32))


def attention_backward(gmiddle, stream, proj, probs, vec, weight, block_pages, begin, end, before):
    rows, width = stream.shape
    _, _, slots, _ = probs.shape
    block = block_pages * slots
    first = begin // block_pages
    row_spec = lambda cols: pl.BlockSpec((block, cols), lambda i: (i + first, 0))
    whole = lambda array: pl.BlockSpec(array.shape, lambda i: (0, 0))
    before = [] if before is None else list(before)
    operands = [gmiddle, stream, proj, probs, vec, weight[0], weight[1]]
    return pl.pallas_call(
        attention_backward_kernel,
        grid=((end - begin) // block_pages,),
        in_specs=[
            row_spec(width),
            row_spec(width),
            row_spec(3 * width),
            pl.BlockSpec((block_pages, PAIRS, slots, 2 * slots), lambda i: (i + first, 0, 0, 0)),
            whole(vec),
            whole(weight[0]),
            whole(weight[1]),
        ]
        + [pl.BlockSpec(memory_space=pl.ANY)] * len(before),
        out_specs=[row_spec(width), row_spec(3 * width), pl.BlockSpec((8, width), lambda i: (0, 0))],
        out_shape=[
            jax.ShapeDtypeStruct((rows, width), F32),
            jax.ShapeDtypeStruct((rows, 3 * width), BF),
            jax.ShapeDtypeStruct((8, width), F32),
        ],
        scratch_shapes=[pltpu.VMEM((block, width), BF)],
        input_output_aliases={len(operands) + index: index for index in range(len(before))},
        compiler_params=pltpu.CompilerParams(vmem_limit_bytes=VMEM_LIMIT),
        cost_estimate=pl.CostEstimate(flops=15 * 10**9, bytes_accessed=20 * 10**6, transcendentals=0),
        name="attention_backward",
    )(*operands, *before)


def attention_weight_kernel(normed_ref, mixed_ref, gproj_ref, gmiddle_ref, grad_ref):
    gqkv = dot_tn(normed_ref[...], gproj_ref[...])
    gout = dot_tn(mixed_ref[...], gmiddle_ref[...].astype(BF))
    parts = grad_ref.shape[1]
    cut = gqkv.shape[1] // parts
    rest = gout.shape[1] // parts
    shape = (grad_ref.shape[0],) + grad_ref.shape[3:]
    for part in range(parts):
        qkv_part = gqkv[:, part * cut : (part + 1) * cut].astype(BF)
        out_part = gout[:, part * rest : (part + 1) * rest].astype(BF)
        grad_ref[:, part, 0] = jnp.concatenate([qkv_part, out_part], axis=1).reshape(shape)


def attention_weight(normed, mixed, gproj, gmiddle, stripes, parts):
    rows, width = normed.shape
    block = width // 2
    high = width // stripes
    return pl.pallas_call(
        attention_weight_kernel,
        grid=(2,),
        in_specs=[
            pl.BlockSpec((rows, block), lambda i: (0, i)),
            pl.BlockSpec((rows, block), lambda i: (0, i)),
            pl.BlockSpec((rows, 3 * width), lambda i: (0, 0)),
            pl.BlockSpec((rows, width), lambda i: (0, 0)),
        ],
        out_specs=pl.BlockSpec((stripes // 2, parts, 1, high, width), lambda i: (i, 0, 0, 0, 0)),
        out_shape=jax.ShapeDtypeStruct((stripes, parts, 1, high, width), BF),
        compiler_params=pltpu.CompilerParams(vmem_limit_bytes=VMEM_LIMIT),
        cost_estimate=pl.CostEstimate(flops=10 * 10**9, bytes_accessed=20 * 10**6, transcendentals=0),
        name="attention_weight",
    )(normed, mixed, gproj, gmiddle)


def relative_rows(source, target, me, depth):
    high = source.shape[0] // (2 * depth)
    for x in range(2):
        for z in range(depth):
            start = pl.multiple_of(jnp.bitwise_xor(me, 2 * z + x) * high, 16)
            at = (x * depth + z) * high
            target[at : at + high, :] = source[pl.ds(start, high), :]


def send_out(me_ref, core, y, staged, slot, own_ref, other_ref, sems):
    for x in range(2):
        first, second = plane(me_ref, x, y, core)

        @pl.when(core == 0)
        def _():
            pltpu.make_async_copy(staged.at[slot, x], own_ref.at[second, first], sems.at[slot, x]).start()

        @pl.when(core == 1)
        def _():
            pltpu.make_async_copy(staged.at[slot, x], other_ref.at[second, first], sems.at[slot, x]).start()


def wait_out(staged, slot, own_ref, sems):
    for x in range(2):
        pltpu.make_async_copy(staged.at[slot, x], own_ref.at[0, 0], sems.at[slot, x]).wait()


def ffn_weight_split_kernel(core, me_ref, nffn_ref, grad_ref, gupper_ref, active_ref, out_ref, *refs):
    step = pl.program_id(0)
    staged, sems = refs[-2:]
    _, _, depth, high, width = staged.shape
    high = high // 2
    if core == 1:
        nffn_out, grad_out, turned, nffn_t, grad_t = refs[:-2]
        kept = [
            pltpu.make_async_copy(nffn_t, nffn_out, sems.at[2, 0]),
            pltpu.make_async_copy(grad_t, grad_out, sems.at[2, 1]),
        ]

        @pl.when(step == 0)
        def _():
            turned[...] = nffn_ref[...].T
            relative_rows(turned, nffn_t, me_ref[0], depth)
            turned[...] = grad_ref[...].astype(BF).T
            relative_rows(turned, grad_t, me_ref[0], depth)
            for copy in kept:
                copy.start()
    else:
        nffn_t, grad_t, kept = nffn_ref, grad_ref, []

    shape = (2, depth, high, width)
    staged[step, :, :, :high, :] = dot_nn(nffn_t[...], gupper_ref[...]).astype(BF).reshape(shape)
    staged[step, :, :, high:, :] = dot_nn(grad_t[...], active_ref[...]).astype(BF).reshape(shape)
    for x in range(2):
        first, second = plane(me_ref, x, step, core)
        pltpu.make_async_copy(staged.at[step, x], out_ref.at[second, first], sems.at[step, x]).start()

    @pl.when(step == 1)
    def _():
        wait_out(staged, 0, out_ref, sems)
        wait_out(staged, 1, out_ref, sems)
        for copy in kept:
            copy.wait()


def ffn_weight_split(me, nffn, grad, gupper, active, depth, core):
    rows, piece = gupper.shape[0], gupper.shape[1] // 4
    width = piece
    high = width // (2 * depth)
    whole = lambda array: pl.BlockSpec(array.shape, lambda i, me: (0, 0))
    column = pl.BlockSpec((rows, piece), lambda i, me: (0, jnp.bitwise_xor(me[1], 2 * i + core)))
    shape = (2, 2, depth, 2 * high, piece)
    return pl.pallas_call(
        functools.partial(ffn_weight_split_kernel, core),
        grid_spec=pltpu.PrefetchScalarGridSpec(
            num_scalar_prefetch=1,
            grid=(2,),
            in_specs=[whole(nffn), whole(grad), column, column],
            out_specs=[pl.BlockSpec(memory_space=pl.ANY)] * (1 + 2 * core),
            scratch_shapes=[pltpu.VMEM((width, rows), BF)] * (3 * core)
            + [pltpu.VMEM(shape, BF), pltpu.SemaphoreType.DMA((3, 2))],
        ),
        out_shape=[jax.ShapeDtypeStruct(shape, BF)] + [jax.ShapeDtypeStruct((width, rows), BF)] * (2 * core),
        compiler_params=pltpu.CompilerParams(vmem_limit_bytes=VMEM_LIMIT),
        cost_estimate=pl.CostEstimate(flops=8 * 10**9, bytes_accessed=15 * 10**6, transcendentals=0),
        name="ffn_weight",
    )(me, nffn, grad, gupper, active)


def attention_weight_split_kernel(me_ref, normed_ref, mixed_ref, gproj_ref, gmiddle_ref, *refs):
    other_ref, own_ref, turned, normed_t, mixed_t, found, staged, extra_s, sems = refs[-9:]
    extra_refs = refs[:-9]
    step = pl.program_id(0)
    _, _, depth, rows, width = staged.shape
    high = width // (2 * depth)
    share = width // 4
    shape = (2, depth, high, width)

    @pl.when(step == 0)
    def _():
        turned[...] = mixed_ref[...].T
        relative_rows(turned, mixed_t, me_ref[0], depth)
        found[:, 3 * width :] = dot_nn(mixed_t[...], gmiddle_ref[...].astype(BF)).astype(BF)
        turned[...] = normed_ref[...].T
        relative_rows(turned, normed_t, me_ref[0], depth)
        if extra_refs:
            extra_s[...] = jnp.zeros_like(extra_s)
            for index in range(2):
                one_ref, two_ref, hidden_ref = extra_refs[3 * index : 3 * index + 3]
                sums = jnp.concatenate([one_ref[:4, :], two_ref[:4, :]], axis=0)
                for part in range(4):
                    at = index * (width // 3)
                    extra_s[part, :8, at : at + share] = sums[:, part * share : (part + 1) * share]
                    extra_s[part, 8 + index : 9 + index, :] = hidden_ref[:, part * width : (part + 1) * width]
            for part in range(4):
                extra = extra_s[part].astype(BF)
                staged[part, :, :, high:, :] = jnp.broadcast_to(extra[None, None], (2, depth) + extra.shape)

    def finish(part):
        columns = slice(part * 3 * share, (part + 1) * 3 * share)
        rest = slice(3 * width + part * share, 3 * width + (part + 1) * share)
        staged[part, :, :, :high, :] = jnp.concatenate([found[:, columns], found[:, rest]], axis=1).reshape(shape)
        near = jnp.bitwise_xor(me_ref[1], part)
        send_out(me_ref, near % 2, near // 2, staged, part, own_ref, other_ref, sems)

    for third in range(3):

        @pl.when(step == third)
        def _():
            found[:, third * width : (third + 1) * width] = dot_nn(normed_t[...], gproj_ref[...]).astype(BF)
            for part in ((0,), (1,), (2, 3))[third]:
                finish(part)
            if third == 2:
                for part in range(4):
                    wait_out(staged, part, own_ref, sems)


def attention_weight_split(me, normed, mixed, gproj, gmiddle, depth, extra=None):
    rows, width = normed.shape
    high = width // (2 * depth)
    whole = lambda array: pl.BlockSpec(array.shape, lambda i: (0,) * array.ndim)
    extras = [] if extra is None else list(extra)
    shape = (2, 2, depth, high + (0 if extra is None else 16), width)
    operands = [normed, mixed, gproj, gmiddle] + extras
    return pl.pallas_call(
        attention_weight_split_kernel,
        grid=(3,),
        in_specs=[pl.BlockSpec(memory_space=pltpu.SMEM), whole(normed), whole(mixed)]
        + [pl.BlockSpec((rows, width), lambda i: (0, i))]
        + [whole(operand) for operand in operands[3:]],
        out_specs=[pl.BlockSpec(memory_space=pl.ANY)] * 2,
        out_shape=[jax.ShapeDtypeStruct(shape, BF)] * 2,
        scratch_shapes=[pltpu.VMEM((width, rows), BF)] * 3
        + [
            pltpu.VMEM((width, 4 * width), BF),
            pltpu.VMEM((4,) + shape[1:], BF),
            pltpu.VMEM((4, 16, width), F32),
            pltpu.SemaphoreType.DMA((4, 2)),
        ],
        compiler_params=pltpu.CompilerParams(vmem_limit_bytes=VMEM_LIMIT),
        cost_estimate=pl.CostEstimate(flops=10 * 10**9, bytes_accessed=20 * 10**6, transcendentals=0),
        name="attention_weight",
    )(me, *operands)


def pair_bias(slot_kind, slot_valid, across):
    same_kind = slot_kind[:, :, None] == slot_kind[:, None, :]
    partner = jnp.logical_not(same_kind) if across else same_kind
    allowed = jnp.logical_and(partner, slot_valid[:, None, :] > 0)
    return jnp.where(allowed, 0.0, -1e30).astype(F32)


def ordered_vectors(small_one, small_two):
    picked = (small_one, 0), (small_two, 0), (small_one, 1), (small_one, 2)
    picked += (small_one, 3), (small_two, 3), (small_two, 1), (small_two, 2)
    return jnp.stack([sums[row] for sums, row in picked])


def adam_step(master, grad, moment_one, moment_two, factor, decayed):
    clipped = grad * factor
    first_new = beta_one * moment_one + (1.0 - beta_one) * clipped
    second_new = beta_two * moment_two + (1.0 - beta_two) * clipped * clipped
    change = first_new / bias_one / (jnp.sqrt(second_new / bias_two) + epsilon)
    if decayed:
        change = change + weight_decay * master
    return (-learn_rate * change, first_new, second_new)


def gather_rows(pieces, sizes):
    kinds, high, width = pieces.shape
    rows = lax.all_gather(pieces.reshape(-1, width), ("dp", "tensor"), axis=0, tiled=False)
    if high % 16 == 0:
        return [(("rows", kind * high), [rows]) for kind in range(kinds)]
    split = rows.reshape(sizes["dp"], sizes["tensor"], kinds, high, width)
    return [(("whole",), [jnp.swapaxes(split[:, :, kind], 0, 1).reshape(-1, width, width)]) for kind in range(kinds)]


def scatter_rows(grad, sizes):
    stripes, parts, kinds, high, width = grad.shape
    inner = sizes["dp"] // stripes
    if inner > 1:
        grad = jnp.moveaxis(grad.reshape(stripes, parts, kinds, inner, high // inner, width), 3, 1)
    mine = lax.psum_scatter(grad.reshape(-1, width), ("dp", "tensor"), scatter_dimension=0, tiled=True)
    return mine.reshape(kinds, -1, width).astype(F32)


class Exchange:
    def __init__(self, sizes):
        self.sizes = sizes
        self.depth = sizes["dp"] // 2

    def swap(self, value, partner):
        dp, tensor = self.sizes["dp"], self.sizes["tensor"]
        pairs = []
        for i in range(dp):
            for j in range(tensor):
                far_i, far_j = partner(i, j)
                pairs.append((i * tensor + j, far_i * tensor + far_j))
        return lax.ppermute(value, ("dp", "tensor"), pairs)

    def part(self, bits, value):
        return self.swap(value, lambda i, j: (i, j ^ bits))

    def core(self, value):
        return self.part(1, value)

    def x(self, value):
        return self.swap(value, lambda i, j: (i ^ 1, j))

    def y(self, value):
        return self.part(2, value)

    def diagonal(self, value):
        return self.swap(value, lambda i, j: (i ^ 1, j ^ 2))

    def first(self, value):
        return self.swap(value, lambda i, j: (i, j ^ 2) if j & 1 else (i ^ 1, j))

    def second(self, value):
        return self.swap(value, lambda i, j: (i ^ 1, j) if j & 1 else (i, j ^ 2))

    def z(self, distance, value):
        return self.swap(value, lambda i, j: (i ^ (2 * distance), j))

    def z_sends(self, values):
        return [(functools.partial(self.z, distance), values[distance]) for distance in range(1, self.depth)]

    def gather_z(self, piece):
        groups = [[2 * z + x for z in range(self.depth)] for x in range(2)]
        return lax.all_gather(piece, "dp", axis=0, tiled=False, axis_index_groups=groups)

    def total(self, value):
        value = value + self.core(value)
        value = value + self.y(value)
        value = value + self.x(value)
        bit = 1
        while bit < self.depth:
            value = value + self.z(bit, value)
            bit *= 2
        return value


def tie(values, after):
    return lax.optimization_barrier((values, after))[0]


class Spread:
    def __init__(self, exchange, quad, fixed):
        self.exchange, self.quad, self.fixed = exchange, quad, fixed

    def go_first(self):
        return [(self.exchange.first, self.quad)]

    def go_second(self, came):
        self.pair = jnp.stack([self.quad, came[0]])
        return [(self.exchange.second, self.pair), (self.exchange.core, self.pair)]

    def go_core(self, came):
        self.two, self.far_pair = came
        return [(self.exchange.core, self.two)]

    def weight(self, came, offset=0):
        positions = [[(0, second, core), (1, second, core)] for core in range(2) for second in range(2)]
        arrays = [self.pair, self.two, self.far_pair, came[0]]
        return (("near", offset, positions, self.fixed), arrays)


class Reduce:
    def __init__(self, exchange, other, own):
        self.exchange, self.other, self.own = exchange, other, own

    def wide(self, value):
        return value.astype(F32)

    def go_core(self):
        return [(self.exchange.core, self.other)]

    def go_second(self, came):
        self.came = came[0]
        value = (self.wide(self.own[1]) + self.wide(self.came[1])).astype(BF)
        return [(self.exchange.second, value)]

    def go_first(self, came):
        self.beside = came[0]
        value = self.wide(self.own[0, 1]) + self.wide(self.came[0, 1]) + self.wide(self.beside[1])
        return [(self.exchange.first, value.astype(BF))]

    def depths(self, came):
        ahead = came[0]
        return (
            self.wide(self.own[0, 0]) + self.wide(self.came[0, 0]) + self.wide(self.beside[0]) + self.wide(ahead)
        )


def mid_first(sends):
    at = (len(sends) + 1) // 2 - 1
    return sends[at : at + 1] + sends[:at] + sends[at + 1 :]


class Lane:
    def __init__(self):
        self.last = None

    def after_last(self, values):
        return values if self.last is None else tie(values, self.last)

    def step(self, sends, kernel=None, arrays=()):
        values = [value for _, value in sends]
        values, arrays = self.after_last((values, list(arrays)))
        came = [move(value) for (move, _), value in zip(sends, values)]
        results = [] if kernel is None else list(kernel(*arrays))
        came, results = lax.optimization_barrier((came, results))
        self.last = results[-1] if results else came[-1]
        return came, results


def shards(
    sizes,
    tokens, out_grad, slot_kind, slot_valid,
    qkv_weight, qkv_first, qkv_second,
    out_weight, out_first, out_second,
    up_weight, up_first, up_second,
    down_weight, down_first, down_second,
    gain_weight, gain_first, gain_second,
    bias_weight, bias_first, bias_second,
    hidden_weight, hidden_first, hidden_second,
):
    parts = sizes["tensor"]
    width = tokens.shape[1]
    cut = qkv_weight.shape[2]
    high = qkv_weight.shape[1]
    split = parts == 4 and high % 32 == 0 and sizes["dp"] in (4, 8, 16)
    exchange = Exchange(sizes)
    stripes = sizes["dp"] if high % 16 == 0 else 2
    me = jnp.stack([lax.axis_index("dp"), lax.axis_index("tensor")]).astype(jnp.int32)
    attn_pieces = jnp.concatenate([qkv_weight.astype(BF), out_weight.astype(BF)], axis=2)
    up_pieces = up_weight.astype(BF)
    down_pieces = jnp.swapaxes(down_weight.astype(BF), 1, 2)
    pages = slot_kind.shape[0]
    block_pages = 2 if pages % 2 == 0 else 1
    block = block_pages * slot_kind.shape[1]
    masks = [pair_bias(slot_kind, slot_valid, index == 0) for index in range(2)]
    lane = Lane()
    gathered = lambda index: gather_rows(
        jnp.stack([attn_pieces[index], up_pieces[index], down_pieces[index]]), sizes
    )
    small = hidden = None
    saved = [None, None]

    def attention_forward_of(index, weight):
        return lambda stream: attention_forward(
            me, stream, masks[index], small[index], weight, block_pages, parts
        )

    def ffn_forward_of(index, up_w, down_w):
        return lambda nffn, middle: ffn_forward(
            me, nffn, middle, small[index], hidden[index : index + 1], up_w, down_w, block, parts
        )

    def ffn_backward_of(index):
        kept = saved[index]
        return lambda grad: ffn_backward(
            me, grad, kept["slope"], kept["middle"], small[index], kept["up_w"], kept["down_w"], block, parts
        )

    def ffn_weight_of(index, grad, turned=None):
        kept = saved[index]
        if not split:
            return lambda gupper: (ffn_weight(kept["nffn"], grad, gupper, kept["active"], stripes, parts),)
        core = 1 if turned is None else 0
        left, right = (kept["nffn"], grad) if turned is None else turned
        return lambda gupper: ffn_weight_split(me, left, right, gupper, kept["active"], exchange.depth, core)

    def attention_backward_of(index, begin, end, before=None):
        kept = saved[index]
        return lambda gmiddle: attention_backward(
            gmiddle, kept["stream"], kept["proj"], kept["probs"], small[index], kept["weight"],
            4 if pages % 4 == 0 else block_pages, begin, end, before,
        )

    def attention_weight_of(index, gmiddle, extra=None):
        kept = saved[index]
        if split:
            return lambda gproj: attention_weight_split(
                me, kept["normed"], kept["mixed"], gproj, gmiddle, exchange.depth, extra
            )
        return lambda gproj: (attention_weight(kept["normed"], kept["mixed"], gproj, gmiddle, stripes, parts),)

    def keep(index, stream, attention, ffn):
        middle, nffn, normed, proj, probs, mixed, qkv_w, out_w = attention
        saved[index] = dict(
            stream=stream, middle=middle, nffn=nffn, normed=normed, proj=proj, probs=probs, mixed=mixed,
            weight=(qkv_w, out_w), active=ffn[1],
        )
        if len(ffn) > 2:
            saved[index].update(slope=ffn[2], up_w=(("whole",), [ffn[3]]), down_w=(("whole",), [ffn[4]]))

    if split:
        depth = exchange.depth
        late = jnp.concatenate([attn_pieces[1], up_pieces[1], down_pieces[1]], axis=0)
        own_small = jnp.concatenate(
            [gain_weight, bias_weight, hidden_weight.reshape(2, -1, gain_weight.shape[2])], axis=1
        )
        own_small = lax.reduce_precision(own_small, 8, 7)
        small_sends = [(functools.partial(exchange.part, bits), own_small) for bits in range(1, 4)]
        came, _ = lane.step(exchange.z_sends([attn_pieces[0]] * depth))
        late = exchange.gather_z(lane.after_last(late))
        attn_zero = Spread(exchange, jnp.stack([attn_pieces[0]] + came), False)
        ffn_piece = jnp.concatenate([up_pieces[0], down_pieces[0]], axis=0)
        ffn_sends = exchange.z_sends([ffn_piece] * depth)
        middle_at = depth // 2 - 1
        came, _ = lane.step(attn_zero.go_first() + ffn_sends[middle_at : middle_at + 1] + small_sends)
        ffn_came = came[1:2]
        mine = lax.axis_index("tensor")

        def order_small(*values):
            every = jnp.zeros((4,) + own_small.shape, F32)
            for bits, value in enumerate(values):
                every = lax.dynamic_update_slice_in_dim(every, value[None], jnp.bitwise_xor(mine, bits), 0)
            small = jnp.moveaxis(every[:, :, :8], 0, 2).reshape(2, 8, width)
            return small[0], small[1], jnp.moveaxis(every[:, :, 8:], 0, 1).reshape(2, -1)

        ffn_sends = ffn_sends[:middle_at] + ffn_sends[middle_at + 1 :]
        came, results = lane.step(attn_zero.go_second(came[:1]) + ffn_sends, order_small, [own_small] + came[2:])
        small, hidden = results[:2], results[2]
        others = came[2:]
        others.insert(middle_at, ffn_came[0])
        ffn_zero = Spread(exchange, jnp.stack([ffn_piece] + others), False)
        came, _ = lane.step(attn_zero.go_core(came[:2]) + ffn_zero.go_first())
        attn_w = attn_zero.weight(came[:1])
        came, attention = lane.step(ffn_zero.go_second(came[1:]), attention_forward_of(0, attn_w), [tokens])
        late = lane.after_last(late)
        attn_one = Spread(exchange, late[:, :high], True)
        ffn_one = Spread(exchange, late[:, high:], True)
        came, _ = lane.step(ffn_zero.go_core(came) + attn_one.go_first())
        up_w, down_w = ffn_zero.weight(came[:1]), ffn_zero.weight(came[:1], high)
        came, ffn = lane.step(
            attn_one.go_second(came[1:]) + ffn_one.go_first(), ffn_forward_of(0, up_w, down_w), attention[1::-1]
        )
        keep(0, tokens, attention, ffn)
        stream = ffn[0]
        ffn_came = came[2:]
        came, _ = lane.step(attn_one.go_core(came[:2]))
        attn_w = attn_one.weight(came)
        came, attention = lane.step(ffn_one.go_second(ffn_came), attention_forward_of(1, attn_w), [stream])
        came, _ = lane.step(ffn_one.go_core(came))
        up_w, down_w = ffn_one.weight(came), ffn_one.weight(came, high)
        both = lambda nffn, middle: ffn_both(
            me, nffn, middle, out_grad, small[1], hidden[1:], up_w, down_w, block, parts
        )
        _, results = lane.step([], both, attention[1::-1])
        block_output, active, gupper, gmiddle, small_two, hidden_one = results
        keep(1, stream, attention, (None, active))
        _, (other, *turned) = lane.step([], ffn_weight_of(1, out_grad), [gupper])
        came, (own,) = lane.step([(exchange.core, other)], ffn_weight_of(1, out_grad, turned), [gupper])
        ffn_one = Reduce(exchange, other, own)
        came, (grad, gproj, small_one) = lane.step(
            ffn_one.go_second(came), attention_backward_of(1, 0, pages), [gmiddle]
        )
        sums_one = (small_one, small_two, hidden_one)
        came, grads = lane.step(ffn_one.go_first(came), attention_weight_of(1, gmiddle), [gproj])
        ffn_layers = ffn_one.depths(came)
        ffn_sends = mid_first(exchange.z_sends([ffn_layers[z].astype(BF) for z in range(depth)]))
        attn_one = Reduce(exchange, *grads)
        came, results = lane.step(attn_one.go_core() + ffn_sends[:1], ffn_backward_of(0), [grad])
        ffn_came = came[1:]
        gupper, gmiddle, small_two, hidden_zero = results
        came, (other, *turned) = lane.step(
            attn_one.go_second(came[:1]) + ffn_sends[1:], ffn_weight_of(0, grad), [gupper]
        )
        ffn_came = ffn_came + came[1:]
        total = ffn_layers[0] + sum(value.astype(F32) for value in ffn_came)
        grad_up, grad_down = [None, total[:high]], [None, total[high:]]
        came, (own,) = lane.step(
            [(exchange.core, other)] + attn_one.go_first(came[:1]), ffn_weight_of(0, grad, turned), [gupper]
        )
        ffn_zero = Reduce(exchange, other, own)
        attn_layers = attn_one.depths(came[1:])
        attn_sends = mid_first(exchange.z_sends([attn_layers[z].astype(BF) for z in range(depth)]))
        came, (input_grad, gproj, small_one) = lane.step(
            ffn_zero.go_second(came[:1]) + attn_sends[:1], attention_backward_of(0, 0, pages), [gmiddle]
        )
        attn_came = came[1:]
        came, grads = lane.step(
            ffn_zero.go_first(came[:1]) + attn_sends[1:],
            attention_weight_of(0, gmiddle, (small_one, small_two, hidden_zero) + sums_one),
            [gproj],
        )
        grad_attn = [None, attn_layers[0] + sum(value.astype(F32) for value in attn_came + came[1:])]
        layers = ffn_zero.depths(came[:1])
        ffn_sends = exchange.z_sends([layers[z].astype(BF) for z in range(depth)])
        ffn_sends = mid_first(ffn_sends)
        attn_zero = Reduce(exchange, *grads)
        ((move, value),) = ffn_sends[:1]
        ffn_came = [move(lane.after_last(value))]
        came, _ = lane.step(attn_zero.go_core())
        came, _ = lane.step(attn_zero.go_second(came) + ffn_sends[1:])
        ffn_came = ffn_came + came[1:]
        came, _ = lane.step(attn_zero.go_first(came[:1]))
        total = layers[0] + sum(value.astype(F32) for value in ffn_came)
        grad_up[0], grad_down[0] = total[:high], total[high:]
        layers = attn_zero.depths(came[:1])
        came, _ = lane.step(exchange.z_sends([layers[z].astype(BF) for z in range(depth)]))
        total = layers[0] + sum(value.astype(F32) for value in came)
        grad_attn[0] = total[:high]
        shared_squares = jnp.sum(total[high:] * total[high:])
        share = width // parts
        vectors = []
        for at in (0, width // 3):
            sums = total[high : high + 8, at : at + share]
            vectors.append(ordered_vectors(sums[:4], sums[4:]))
        vectors = jnp.stack(vectors)
        grad_hidden = total[high + 8 : high + 10]
    else:
        small = jnp.concatenate([gain_weight, bias_weight], axis=1).astype(BF)
        small = lax.all_gather(small, "tensor", axis=2, tiled=True).astype(F32)
        hidden = lax.all_gather(hidden_weight.astype(BF), "tensor", axis=1, tiled=True).astype(F32)
        stream = tokens
        for index in range(2):
            attn_w, up_w, down_w = gathered(index)
            attention = attention_forward_of(index, attn_w)(stream)
            ffn = ffn_forward_of(index, up_w, down_w)(*attention[1::-1])
            keep(index, stream, attention, ffn)
            stream = ffn[0]
        block_output = stream
        grad = out_grad
        grad_attn, grad_up, grad_down, vectors, grad_hidden = ([None, None] for _ in range(5))
        for index in (1, 0):
            gupper, gmiddle, small_two, grad_hidden[index] = ffn_backward_of(index)(grad)
            (gffn,) = ffn_weight_of(index, grad)(gupper)
            grad_up[index], grad_down[index] = scatter_rows(gffn, sizes)
            grad, gproj, small_one = attention_backward_of(index, 0, pages)(gmiddle)
            (grad_attn[index],) = scatter_rows(attention_weight_of(index, gmiddle)(gproj)[0], sizes)
            vectors[index] = ordered_vectors(small_one, small_two)
        input_grad = grad
        vectors, grad_hidden = lax.psum((jnp.stack(vectors), jnp.concatenate(grad_hidden, axis=0)), ("dp", "tensor"))
        at = lax.axis_index("tensor")
        slice_of = lambda whole: lax.dynamic_slice_in_dim(
            whole, at * (whole.shape[-1] // parts), whole.shape[-1] // parts, whole.ndim - 1
        )
        vectors, grad_hidden = slice_of(vectors), slice_of(grad_hidden)
        shared_squares = jnp.sum(vectors * vectors) + jnp.sum(grad_hidden * grad_hidden)
    grad_gain, grad_bias = vectors[:, :2], vectors[:, 2:]
    local_squares = sum(jnp.sum(grad * grad) for pair in (grad_up, grad_down, grad_attn) for grad in pair[::-1])
    grad_attn, grad_up, grad_down = jnp.stack(grad_attn), jnp.stack(grad_up), jnp.stack(grad_down)
    local_squares = local_squares + jnp.where(lax.axis_index("dp") == 0, shared_squares, 0.0)
    grad_down = jnp.swapaxes(grad_down, 1, 2)
    if split:
        total_squares = exchange.total(local_squares.reshape(1, 1))[0, 0]
    else:
        total_squares = lax.psum(local_squares, ("dp", "tensor"))
    grad_norm = jnp.sqrt(total_squares)
    factor = clip_norm / jnp.maximum(grad_norm, clip_norm)
    masters = (qkv_weight, out_weight, up_weight, down_weight, gain_weight, bias_weight, hidden_weight)
    firsts = (qkv_first, out_first, up_first, down_first, gain_first, bias_first, hidden_first)
    seconds = (qkv_second, out_second, up_second, down_second, gain_second, bias_second, hidden_second)
    gradients = (
        grad_attn[:, :, :cut], grad_attn[:, :, cut:], grad_up, grad_down, grad_gain, grad_bias, grad_hidden,
    )
    results = [block_output, input_grad, grad_norm]
    for member in range(7):
        update, first_new, second_new = adam_step(
            masters[member], gradients[member], firsts[member], seconds[member], factor, member < 4
        )
        results = results + [gradients[member], update, first_new, second_new]
    return tuple(results)


def solution(mesh):
    rows = P(("dp", "tensor"), None)
    matrix = P(None, "dp", "tensor")
    turned = P(None, "tensor", "dp")
    vectors = P(None, None, "tensor")
    hidden = P(None, "tensor")
    return jax.shard_map(
        functools.partial(shards, dict(mesh.shape)),
        mesh=mesh,
        in_specs=(rows,) * 4 + (matrix,) * 9 + (turned,) * 3 + (vectors,) * 6 + (hidden,) * 3,
        out_specs=(rows, rows, P()) + (matrix,) * 12 + (turned,) * 4 + (vectors,) * 8 + (hidden,) * 4,
        check_vma=False,
    )
```
